128 devices in a mesh: cache: 32 (over y, x, core), psg: 4 (over z).
Axes of the slice: x: 4, y: 4, z: 4, core: 2. Of those that a mesh axis runs over, the one named last changes fastest.
Arguments:
- question_ids: int32 [32, 16], P('cache'), may hold values from 0 to 32127
- answer_ids: int32 [32, 32], P('cache'), may hold values from 0 to 32127
- owner: int32 [32, 32, 1], P('cache', 'psg'), may hold values from 0 to 31; in each aligned block of 32 rows (0 to 31, 32 to 63, ..., all dimensions but the last counted through in order) at most 2 rows name the same one
- slot: int32 [32, 32], P('cache', 'psg'), may hold values from 0 to 31
- passage_score: float32 [32, 32], P('cache', 'psg'), may hold values from -4 to 304
- memory: bfloat16 [1024, 16, 4096], P('cache', None, 'psg'), may hold values from -64 to 64
- embedding: bfloat16 [32128, 4096], P('cache', 'psg'), may hold values from -6 to 6
- live_gain: float32 [4096], replicated, may hold values from 0.1 to 1.9
- live_qkv: bfloat16 [4096, 3, 2048], P(None, None, 'psg'), may hold values from -0.09375 to 0.09375
- rel_bias: float32 [32, 32], P('psg'), may hold values from -6 to 306
- live_out: bfloat16 [2048, 4096], P('psg'), may hold values from -0.375 to 0.375
- enc_gain: float32 [4096], replicated, may hold values from 0.1 to 1.9
- cross_kv: bfloat16 [4096, 2, 2048], P(None, None, 'psg'), may hold values from -0.09375 to 0.09375
- dec_gain: float32 [4096], replicated, may hold values from 0.1 to 1.9
- cross_query: bfloat16 [4096, 2048], P(None, 'psg'), may hold values from -0.09375 to 0.09375
- cross_out: bfloat16 [2048, 4096], P('psg'), may hold values from -0.375 to 0.375
Outputs:
- encoded: bfloat16 [32, 32, 32, 4096], P('cache', 'psg')
- decoded: bfloat16 [32, 32, 4096], P('cache', None, 'psg')
The draws below stay inside these ranges and needn't reach their ends.
Inputs may be any that keep to these rules, and one draw needn't show every extreme that they name: Among the 32 passages of one question at most 2 have the same owner, and in some question an owner has exactly 2.
All inputs are finite; a program needn't handle non-finite values.
Results may differ from the reference program's by a relative error of at most 0.025.
Values may be sent and summed in bfloat16 or wider, within the bound.
A program may use at most 192 MiB of HBM per device.

```python
import math
import jax
import jax.numpy as jnp
import numpy as np
from jax import lax

D = 4096
HEAD = 64
HEADS_L = 32
HEADS_C = 32
VOCAB = 32128
BUCKETS = 32
LEN = 16
QLEN = 16
ALEN = 32
ENTRIES_DEV = 32
ENTRIES = 1024
QUESTIONS = 32
PSG_Q = 32
CAP = 2
N_CACHE = 32
N_PSG = 4


def draw_memory(key, part):
    key = jax.random.fold_in(key, 11)
    key_base, key_rows, key_cols = jax.random.split(key, 3)
    full_shape = (ENTRIES, LEN, D)
    base_values = jnp.clip(jax.random.normal(key_base, full_shape, jnp.float32), -6.0, 6.0)
    row_scale = jnp.exp(jax.random.uniform(key_rows, (ENTRIES, LEN, 1), jnp.float32, -1.15, 1.15))
    col_scale = jnp.exp(jax.random.uniform(key_cols, (1, 1, D), jnp.float32, -1.15, 1.15))
    values = base_values * row_scale * col_scale
    return values.astype(jnp.bfloat16)


def draw_rel_bias(key, part):
    key = jax.random.fold_in(key, 23)
    key_base = jax.random.fold_in(key, 0)
    base_values = jnp.clip(1.5 * jax.random.normal(key_base, (HEADS_L, BUCKETS), jnp.float32), -6.0, 6.0)
    return base_values.astype(jnp.float32)


def draw_passage_score(key, part):
    key = jax.random.fold_in(key, 37)
    key_base = jax.random.fold_in(key, 0)
    base_values = jnp.clip(jax.random.normal(key_base, (QUESTIONS, PSG_Q), jnp.float32), -4.0, 4.0)
    return base_values.astype(jnp.float32)


def place_ends(values, rng, low, largest):
    index_at = [jax.random.randint(jax.random.fold_in(rng, axis), (), 0, length) for axis, length in enumerate(values.shape)]
    longest = values.shape.index(max(values.shape))
    neighbour = index_at[:longest] + [(index_at[longest] + 1) % values.shape[longest]] + index_at[longest + 1:]
    return values.at[tuple(index_at)].set(low).at[tuple(neighbour)].set(largest)


def shard_levels(stream_key, dims, cuts, smallest, top_value):
    gain, own = 1.0, jax.random.fold_in(stream_key, 6)
    for axis_at, shards_of in cuts:
        heights = jnp.exp(jax.random.uniform(jax.random.fold_in(own, axis_at), (shards_of,), jnp.float32, smallest / len(cuts), top_value / len(cuts)))
        gain = gain * jnp.repeat(heights, dims[axis_at] // shards_of).reshape([-1 if axis == axis_at else 1 for axis in range(len(dims))])
    return gain


def rank_bounds(count, skew):
    loads = [(1 << 20) // math.isqrt(standing ** skew) + 1 for standing in range(1, count + 1)]
    deviation = 1 + sum(loads) // (1 << 30)
    return np.cumsum(np.array([max(1, weight // deviation) for weight in loads]))


def ranked(key, dims, amount, skew):
    grid = rank_bounds(amount, skew)
    lot = jax.random.randint(jax.random.fold_in(key, 1), dims, 0, int(grid[amount - 1]))
    grade = jnp.searchsorted(jnp.asarray(grid, jnp.int32), lot, side="right")
    return jax.random.permutation(jax.random.fold_in(key, 2), amount)[grade].astype(jnp.int32)


def shared_out(rng, own, number, rows, amount, top, reach, skew):
    ranking = jax.random.permutation(rng, amount)
    packed, ordinary = load_shares(amount, rows * top, reach, skew, True), load_shares(amount, rows * top, reach, skew, False)
    places = jnp.arange(amount)

    def named(sizes, rotation):
        used = int((sizes > 0).sum())
        fixed = max(1, used // 4)
        shifted = fixed + (places - fixed + rotation * (used - fixed)) % max(1, amount - fixed)
        return jnp.zeros((amount,), jnp.int32).at[ranking[jnp.where(places < fixed, places, shifted)]].set(jnp.asarray(sizes, jnp.int32))

    sizes = jnp.where(number % 4 == 0, named(packed, number // 4), named(ordinary, number - number // 4 - 1))
    mixed = jax.random.permutation(jax.random.fold_in(own, 3), amount)
    donor, sink = mixed[0:amount // 2 * 2:2], mixed[1:amount // 2 * 2:2]
    slack = jnp.minimum(sizes[donor] - 1, reach - sizes[sink]) // 2
    slack = jnp.where((donor == ranking[0]) | (sink == ranking[0]) | (sizes[sink] == 0), 0, jnp.maximum(slack, 0))
    shifted = jax.random.randint(jax.random.fold_in(own, 4), (amount // 2,), 0, 1 << 20) % (slack + 1)
    sizes = sizes.at[donor].add(-shifted).at[sink].add(shifted)
    members = jnp.searchsorted(jnp.cumsum(sizes), jnp.arange(rows * top), side="right").astype(jnp.int32)
    table = members.reshape(top, rows).T
    table = table[jax.random.permutation(jax.random.fold_in(own, 1), rows)]
    rotation = jax.random.randint(jax.random.fold_in(own, 2), (rows, 1), 0, top)
    return jnp.take_along_axis(table, (jnp.arange(top)[None, :] + rotation) % top, axis=1)


def load_shares(number_of, total, bound, slope, full):
    portions = [(1 << 20) // math.isqrt(grade ** slope) + 1 for grade in range(1, number_of + 1)]
    largest = bound if full else min(bound, max(-(-total // number_of), total * portions[0] // sum(portions)))
    least = 1 if total - largest >= number_of - 1 else 0
    given, spare = [largest] + [least] * (number_of - 1), total - largest - least * (number_of - 1)
    while spare > 0:
        movable = [i for i in range(1, number_of) if given[i] < largest] or [i for i in range(1, number_of) if given[i] < bound]
        pool, left = sum([portions[i] for i in movable]), spare
        for i in movable:
            extra = min(bound - given[i], max(1, left * portions[i] // pool), spare)
            given[i] = given[i] + extra
            spare = spare - extra
    return np.array(given)


def normal_values(rng, shape, scale, limit, cuts=(), kind=jnp.bfloat16):
    factor_of = shard_levels(rng, shape, cuts, -0.22, 0.18) if cuts else 1.0
    values = jax.random.normal(rng, shape, jnp.float32) * scale * factor_of
    return jnp.minimum(jnp.maximum(values, -limit), limit).astype(kind)


def setup_inputs(seed: int = 0) -> dict:
    arg_keys = jax.random.split(jax.random.key(seed), 17)
    question_ids = place_ends(ranked(arg_keys[0], (QUESTIONS, QLEN), VOCAB, 2), jax.random.fold_in(arg_keys[0], 3), 0, VOCAB - 1).astype(jnp.int32)
    answer_ids = place_ends(ranked(arg_keys[1], (QUESTIONS, ALEN), VOCAB, 2), jax.random.fold_in(arg_keys[1], 3), 0, VOCAB - 1).astype(jnp.int32)
    owner_keys = jax.random.split(jax.random.fold_in(arg_keys[2], 1), QUESTIONS * PSG_Q // PSG_Q)
    owner_turns = jax.random.permutation(jax.random.fold_in(arg_keys[2], 3), QUESTIONS * PSG_Q // PSG_Q)
    owner = jax.vmap(lambda own, number: shared_out(jax.random.fold_in(arg_keys[2], 2), own, number, PSG_Q, N_CACHE, 1, CAP, 2))(owner_keys, owner_turns).reshape((QUESTIONS, PSG_Q, 1))
    slot = place_ends(jax.random.randint(arg_keys[3], (QUESTIONS, PSG_Q), 0, ENTRIES_DEV), jax.random.fold_in(arg_keys[3], 1), 0, ENTRIES_DEV - 1).astype(jnp.int32)
    passage_score = draw_passage_score(jax.random.fold_in(arg_keys[16], 71), 0)
    memory = draw_memory(jax.random.fold_in(arg_keys[16], 71), 0)
    embedding = normal_values(arg_keys[6], (VOCAB, D), 1.0, 6.0, ((0, 32), (1, 4)))
    live_gain = jnp.clip(1.0 + 0.18 * jax.random.normal(arg_keys[7], (D,), jnp.float32), 0.1, 1.9)
    live_qkv = normal_values(arg_keys[8], (D, 3, HEADS_L * HEAD), D ** -0.5, 0.09375, ((2, 4),))
    rel_bias = draw_rel_bias(jax.random.fold_in(arg_keys[16], 71), 0)
    live_out = normal_values(arg_keys[10], (HEADS_L * HEAD, D), (HEADS_L * 8) ** -0.5, 0.375, ((0, 4),))
    enc_gain = jnp.clip(1.0 + 0.18 * jax.random.normal(arg_keys[11], (D,), jnp.float32), 0.1, 1.9)
    cross_kv = normal_values(arg_keys[12], (D, 2, HEADS_C * HEAD), D ** -0.5, 0.09375, ((2, 4),))
    dec_gain = jnp.clip(1.0 + 0.18 * jax.random.normal(arg_keys[13], (D,), jnp.float32), 0.1, 1.9)
    cross_query = normal_values(arg_keys[14], (D, HEADS_C * HEAD), D ** -0.5, 0.09375, ((1, 4),))
    cross_out = normal_values(arg_keys[15], (HEADS_C * HEAD, D), (HEADS_C * 8) ** -0.5, 0.375, ((0, 4),))
    return dict(question_ids=question_ids, answer_ids=answer_ids, owner=owner, slot=slot, passage_score=passage_score, memory=memory, embedding=embedding, live_gain=live_gain, live_qkv=live_qkv, rel_bias=rel_bias, live_out=live_out, enc_gain=enc_gain, cross_kv=cross_kv, dec_gain=dec_gain, cross_query=cross_query, cross_out=cross_out)


EPSILON = 1e-06

def bucket_table(length, bucket_count):
    positions = np.arange(length)
    relative = positions[None, :] - positions[:, None]
    halfway = bucket_count // 2
    exact_span = halfway // 2
    upper_side = (relative > 0).astype(np.int64) * halfway
    distance = np.abs(relative)
    log_bucket = exact_span + (np.log(np.maximum(distance, 1) / exact_span) / np.log(128.0 / exact_span) * (halfway - exact_span)).astype(np.int64)
    log_bucket = np.minimum(log_bucket, halfway - 1)
    return upper_side + np.where(distance < exact_span, distance, log_bucket)

def position_bias(bias_table, length):
    bucket_count = bias_table.shape[1]
    buckets = bucket_table(length, bucket_count).reshape(-1)
    onehot = (buckets[None, :] == np.arange(bucket_count)[:, None]).astype(np.float32)
    spread = jnp.dot(bias_table, jnp.asarray(onehot, dtype=bias_table.dtype), precision=lax.Precision.HIGHEST)
    return spread.reshape(bias_table.shape[0], length, length)

def norm_project(rows_in, gain_vector, weights):
    wide = rows_in.astype(jnp.float32)
    inverse = lax.rsqrt(lax.optimization_barrier(jnp.mean(wide * wide, axis=-1, keepdims=True)) + EPSILON)
    scaled = (wide * gain_vector).astype(jnp.bfloat16)
    projected = jnp.dot(scaled, weights, preferred_element_type=jnp.float32)
    return (projected * inverse).astype(jnp.bfloat16)

def softmax_rows(scores):
    maximum = lax.optimization_barrier(jnp.max(scores, axis=-1, keepdims=True))
    exponents = jnp.exp(scores - maximum)
    return (exponents / lax.optimization_barrier(jnp.sum(exponents, axis=-1, keepdims=True))).astype(jnp.bfloat16)

def reference(question_ids, answer_ids, owner, slot, passage_score, memory, embedding, live_gain, live_qkv, rel_bias, live_out, enc_gain, cross_kv, dec_gain, cross_query, cross_out):
    seq_len = LEN + QLEN
    score_scale = HEAD ** (-0.5)
    position = position_bias(rel_bias, seq_len)
    qkv_weights = live_qkv.reshape(D, 3 * HEADS_L * HEAD)
    kv_weights = cross_kv.reshape(D, 2 * HEADS_C * HEAD)
    group_cols = HEADS_L * HEAD // N_PSG

    def one_question(inputs):
        asked_ids, answered_ids, owner_row, slot_row, score_row = inputs
        entry_index = (owner_row[:, 0] * ENTRIES_DEV + slot_row).astype(jnp.int32)
        passages = jnp.take(memory, entry_index, axis=0)
        question = jnp.take(embedding, asked_ids, axis=0)
        answer = jnp.take(embedding, answered_ids, axis=0)
        stacked = jnp.concatenate([passages, jnp.broadcast_to(question[None], (PSG_Q, QLEN, D))], axis=1)
        flattened = stacked.reshape(PSG_Q * seq_len, D)
        projections = norm_project(flattened, live_gain, qkv_weights).reshape(PSG_Q, seq_len, 3, HEADS_L, HEAD).astype(jnp.float32)
        scores = jnp.einsum('pqhd,pkhd->phqk', projections[:, :, 0], projections[:, :, 1]) * score_scale + position[None]
        weights = softmax_rows(scores).astype(jnp.float32)
        context = jnp.einsum('phqk,pkhd->pqhd', weights, projections[:, :, 2]).astype(jnp.bfloat16).reshape(PSG_Q * seq_len, HEADS_L * HEAD)
        attended = jnp.zeros((PSG_Q * seq_len, D), jnp.float32)
        for group_index in range(N_PSG):
            first_col = group_index * group_cols
            partial_value = jnp.dot(context[:, first_col:first_col + group_cols], live_out[first_col:first_col + group_cols], preferred_element_type=jnp.float32).astype(jnp.bfloat16)
            attended = attended + lax.optimization_barrier(partial_value).astype(jnp.float32)
        encoded = (flattened.astype(jnp.float32) + attended).astype(jnp.bfloat16)
        keys_values = norm_project(encoded, enc_gain, kv_weights).reshape(PSG_Q * seq_len, 2, HEADS_C, HEAD).astype(jnp.float32)
        dec_queries = norm_project(answer, dec_gain, cross_query).reshape(ALEN, HEADS_C, HEAD).astype(jnp.float32)
        key_bias = jnp.repeat(score_row, seq_len)
        cross_scores = jnp.einsum('qhd,khd->qhk', dec_queries, keys_values[:, 0]) * score_scale + key_bias
        cross_weights = softmax_rows(cross_scores).astype(jnp.float32)
        cross_context = jnp.einsum('qhk,khd->qhd', cross_weights, keys_values[:, 1]).astype(jnp.bfloat16).reshape(ALEN, HEADS_C * HEAD)
        decoded = jnp.dot(cross_context, cross_out, preferred_element_type=jnp.float32).astype(jnp.bfloat16)
        return (encoded.reshape(PSG_Q, seq_len, D), decoded)
    encoded, decoded = lax.map(one_question, (question_ids, answer_ids, owner, slot, passage_score))
    return (encoded, decoded)
```

```python
import jax
import jax.numpy as jnp
import numpy as np
from jax import lax
from jax.sharding import PartitionSpec as P

HEAD = 64
EPSILON = 1e-06
F32 = jnp.float32
BF16 = jnp.bfloat16


def bucket_table(length, bucket_count):
    positions = np.arange(length)
    relative = positions[None, :] - positions[:, None]
    halfway = bucket_count // 2
    exact_span = halfway // 2
    upper_side = (relative > 0).astype(np.int64) * halfway
    distance = np.abs(relative)
    log_bucket = exact_span + (
        np.log(np.maximum(distance, 1) / exact_span)
        / np.log(128.0 / exact_span)
        * (halfway - exact_span)
    ).astype(np.int64)
    log_bucket = np.minimum(log_bucket, halfway - 1)
    return upper_side + np.where(distance < exact_span, distance, log_bucket)


def position_bias(bias_table, length):
    bucket_count = bias_table.shape[1]
    buckets = bucket_table(length, bucket_count).reshape(-1)
    onehot = (buckets[None, :] == np.arange(bucket_count)[:, None]).astype(np.float32)
    spread = jnp.dot(
        bias_table, jnp.asarray(onehot, dtype=bias_table.dtype), precision=lax.Precision.HIGHEST
    )
    return spread.reshape(bias_table.shape[0], length, length)


def norm_project(rows_in, gain_vector, weights):
    wide = rows_in.astype(F32)
    inverse = lax.rsqrt(jnp.mean(wide * wide, axis=-1, keepdims=True) + EPSILON)
    scaled = (wide * gain_vector).astype(BF16)
    projected = jnp.dot(scaled, weights, preferred_element_type=F32)
    return (projected * inverse).astype(BF16)


def softmax_rows(scores):
    maximum = jnp.max(scores, axis=-1, keepdims=True)
    exponents = jnp.exp(scores - maximum)
    return (exponents / jnp.sum(exponents, axis=-1, keepdims=True)).astype(BF16)


def dot32(a, b, dims):
    return lax.dot_general(a, b, (dims, ((), ())), preferred_element_type=F32)


def shards(
    question_ids, answer_ids, owner, slot, passage_score, memory, embedding, live_gain, live_qkv,
    rel_bias, live_out, enc_gain, cross_kv, dec_gain, cross_query, cross_out,
):
    n_cache = lax.axis_size("cache")
    n_psg = lax.axis_size("psg")
    me_c = lax.axis_index("cache")
    me_z = lax.axis_index("psg")
    width = live_gain.shape[0]
    plen = memory.shape[1]
    qlen = question_ids.shape[1]
    alen = answer_ids.shape[1]
    own_count = owner.shape[1]
    total = own_count * n_psg
    seq = plen + qlen
    heads = rel_bias.shape[0]
    cols = live_out.shape[0]
    scale = HEAD ** (-0.5)

    piece_rows = cols // n_cache
    piece = lax.dynamic_slice_in_dim(live_out, me_c * piece_rows, piece_rows, 0)
    pieces = lax.all_gather(piece, "psg", axis=0, tiled=False)
    out_full = [lax.all_gather(pieces[z], "cache", axis=0, tiled=True) for z in range(n_psg)]

    ints = jnp.concatenate(
        [question_ids[0], answer_ids[0], owner[0, :, 0], slot[0]], axis=0
    ).reshape(1, 1, -1)
    every = lax.all_gather(ints, ("cache", "psg"), axis=0, tiled=True).reshape(n_cache, n_psg, -1)
    tokens = every[:, 0, : qlen + alen]
    owners = every[:, :, qlen + alen : qlen + alen + own_count].reshape(n_cache, total)
    slots = every[:, :, qlen + alen + own_count :].reshape(n_cache, total)
    order = jnp.arange(total)
    earlier = (owners[:, :, None] == owners[:, None, :]) & (order[None, :] < order[:, None])[None]
    rank = jnp.sum(earlier, axis=2)
    mine = owners == me_c
    asked = jnp.sum(
        jnp.where(mine[:, None, :] & (rank[:, None, :] == jnp.arange(2)[None, :, None]),
                  slots[:, None, :], 0),
        axis=2,
    )
    place = lax.dynamic_index_in_dim(owners * 2 + rank, me_c, 0, False)
    looked_up = jnp.take(memory, asked.reshape(-1), axis=0).reshape((n_cache, 2) + memory.shape[1:])
    fetched = lax.all_to_all(looked_up, "cache", split_axis=0, concat_axis=0, tiled=True)
    slices = jnp.take(fetched.reshape((-1,) + memory.shape[1:]), place, axis=0)
    x_mem = lax.all_gather(slices, "psg", axis=2, tiled=True).reshape(total * plen, width)

    vocab = embedding.shape[0]
    onehot = (
        (tokens - me_c * vocab)[:, :, None] == jnp.arange(vocab, dtype=jnp.int32)
    ).astype(BF16)
    token_slice = lax.psum_scatter(
        jnp.einsum("qtv,vf->qtf", onehot, embedding, preferred_element_type=F32).astype(BF16),
        "cache", scatter_dimension=0, tiled=True,
    )
    token_full = lax.all_gather(token_slice, "psg", axis=2, tiled=True)[0]
    x_q = token_full[:qlen]
    answer = token_full[qlen:]
    score_all = lax.all_gather(passage_score[0], "psg", axis=0, tiled=True)

    q_dec = norm_project(answer, dec_gain, cross_query).reshape(alen, heads, HEAD)
    w_key = cross_kv[:, 0].reshape(width, heads, HEAD)
    w_val = cross_kv[:, 1].reshape(width, heads, HEAD)
    qg = (
        jnp.einsum("thd,fhd->htf", q_dec, w_key, preferred_element_type=F32) * enc_gain
    ).astype(BF16).reshape(heads * alen, width)
    ql = [dot32(qg, o, ((1,), (1,))).astype(BF16) for o in out_full]

    w_qkv = live_qkv.reshape(width, 3 * cols)
    mem_proj = norm_project(x_mem, live_gain, w_qkv).reshape(total, plen, 3 * cols)
    q_proj = norm_project(x_q, live_gain, w_qkv)
    proj = jnp.concatenate(
        [mem_proj, jnp.broadcast_to(q_proj[None], (total, qlen, 3 * cols))], axis=1
    ).reshape(total, seq, 3, heads, HEAD)
    scores = jnp.einsum(
        "pqhd,pkhd->phqk", proj[:, :, 0], proj[:, :, 1], preferred_element_type=F32
    ) * scale + position_bias(rel_bias, seq)[None]
    ctx = (
        jnp.einsum("phqk,pkhd->pqhd", softmax_rows(scores), proj[:, :, 2],
                   preferred_element_type=F32)
        .astype(BF16).reshape(total * seq, cols)
    )
    ctx_all = lax.all_gather(ctx, "psg", axis=0, tiled=False)

    own_rows = own_count * seq
    own_ctx = lax.dynamic_slice_in_dim(ctx_all, me_z * own_rows, own_rows, 1)
    attended = sum(
        dot32(own_ctx[z], out_full[z], ((1,), (0,))).astype(BF16).astype(F32) for z in range(n_psg)
    )
    own_mem = lax.dynamic_slice_in_dim(x_mem, me_z * own_count * plen, own_count * plen, 0)
    own_input = jnp.concatenate(
        [own_mem.reshape(own_count, plen, width),
         jnp.broadcast_to(x_q[None], (own_count, qlen, width))], axis=1,
    ).reshape(own_rows, width)
    encoded = (own_input.astype(F32) + attended).astype(BF16)
    enc32 = encoded.astype(F32)
    inv_own = lax.rsqrt(jnp.mean(enc32 * enc32, axis=-1) + EPSILON)
    inv = lax.all_gather(inv_own, "psg", axis=0, tiled=True)

    s_mem = dot32(qg, x_mem, ((1,), (1,))).reshape(-1, total, plen)
    s_q = jnp.broadcast_to(dot32(qg, x_q, ((1,), (1,)))[:, None], (heads * alen, total, qlen))
    s = jnp.concatenate([s_mem, s_q], axis=2).reshape(heads * alen, total * seq)
    for z in range(n_psg):
        s = s + dot32(ql[z], ctx_all[z], ((1,), (1,)))
    s = s * (inv * scale)[None] + jnp.repeat(score_all, seq)[None]
    top = jnp.max(s, axis=-1, keepdims=True)
    e = jnp.exp(s - top)
    sums = jnp.sum(e, axis=-1, keepdims=True)
    w = (e * inv[None] / sums).astype(BF16)
    w3 = w.reshape(-1, total, seq)
    w_mem = w3[:, :, :plen].reshape(-1, total * plen)
    w_q = jnp.sum(w3[:, :, plen:].astype(F32), axis=1).astype(BF16)
    zed = dot32(w_mem, x_mem, ((1,), (0,))) + dot32(w_q, x_q, ((1,), (0,)))
    for z in range(n_psg):
        part = dot32(w, ctx_all[z], ((1,), (0,))).astype(BF16)
        zed = zed + dot32(part, out_full[z], ((1,), (0,)))
    zed = (zed * enc_gain).astype(BF16).reshape(heads, alen, width)
    context = jnp.einsum("htf,fhd->thd", zed, w_val, preferred_element_type=F32).astype(BF16)
    decoded = lax.psum_scatter(
        dot32(context.reshape(alen, -1), cross_out, ((1,), (0,))).astype(BF16),
        "psg", scatter_dimension=1, tiled=True,
    )
    return encoded.reshape(1, own_count, seq, width), decoded[None]


def solution(mesh):
    return jax.shard_map(
        shards,
        mesh=mesh,
        in_specs=(
            P("cache", None), P("cache", None), P("cache", "psg", None), P("cache", "psg"),
            P("cache", "psg"), P("cache", None, "psg"), P("cache", "psg"), P(),
            P(None, None, "psg"), P("psg", None), P("psg", None), P(), P(None, None, "psg"), P(),
            P(None, "psg"), P("psg", None),
        ),
        out_specs=(P("cache", "psg", None, None), P("cache", None, "psg")),
        check_vma=False,
    )
```

```python
import functools

import jax
import jax.numpy as jnp
import numpy as np
from jax import lax
from jax.experimental import pallas as pl
from jax.experimental.pallas import tpu as pltpu
from jax.sharding import PartitionSpec as P

HEAD = 64
EPSILON = 1e-06
F32 = jnp.float32
BF16 = jnp.bfloat16


def bucket_table(length, bucket_count):
    positions = np.arange(length)
    relative = positions[None, :] - positions[:, None]
    halfway = bucket_count // 2
    exact_span = halfway // 2
    upper_side = (relative > 0).astype(np.int64) * halfway
    distance = np.abs(relative)
    log_bucket = exact_span + (
        np.log(np.maximum(distance, 1) / exact_span)
        / np.log(128.0 / exact_span)
        * (halfway - exact_span)
    ).astype(np.int64)
    log_bucket = np.minimum(log_bucket, halfway - 1)
    return upper_side + np.where(distance < exact_span, distance, log_bucket)


def position_bias(bias_table, length):
    bucket_count = bias_table.shape[1]
    buckets = bucket_table(length, bucket_count).reshape(-1)
    onehot = (buckets[None, :] == np.arange(bucket_count)[:, None]).astype(np.float32)
    spread = jnp.dot(
        bias_table, jnp.asarray(onehot, dtype=bias_table.dtype), precision=lax.Precision.HIGHEST
    )
    return spread.reshape(bias_table.shape[0], length, length)


def norm_project(rows_in, gain_vector, weights):
    wide = rows_in.astype(F32)
    inverse = lax.rsqrt(jnp.mean(wide * wide, axis=-1, keepdims=True) + EPSILON)
    scaled = (wide * gain_vector).astype(BF16)
    projected = jnp.dot(scaled, weights, preferred_element_type=F32)
    return (projected * inverse).astype(BF16)


def softmax_rows(scores):
    maximum = jnp.max(scores, axis=-1, keepdims=True)
    exponents = jnp.exp(scores - maximum)
    return (exponents / jnp.sum(exponents, axis=-1, keepdims=True)).astype(BF16)


def dot32(a, b, dims):
    return lax.dot_general(a, b, (dims, ((), ())), preferred_element_type=F32)


MESH = pl.DeviceIdType.MESH
VM = pl.BlockSpec(memory_space=pltpu.VMEM)
SM = pl.BlockSpec(memory_space=pltpu.SMEM)
ANY = pl.BlockSpec(memory_space=pl.ANY)


def params(collective_id, mib):
    return pltpu.CompilerParams(
        collective_id=collective_id, has_side_effects=True, vmem_limit_bytes=mib << 20
    )


class Place:
    def __init__(self):
        self.c = lax.axis_index("cache")
        self.z = lax.axis_index("psg")
        self.core = lax.rem(self.c, 2)
        self.x = lax.rem(lax.div(self.c, 2), 4)
        self.y = lax.div(self.c, 8)

    def cache(self, c):
        return {"cache": c, "psg": self.z}

    def chip(self, y, x):
        return self.cache((y * 4 + x) * 2 + self.core)

    def sibling(self):
        return self.cache(self.c + 1 - 2 * self.core)

    def up(self, z):
        return {"cache": self.c, "psg": z}


def turn(p, k):
    return lax.rem(p + k + 4, 4)


def greet_all(at):
    barrier = pltpu.get_barrier_semaphore()

    def greet(d, carry):
        pl.semaphore_signal(
            barrier, inc=1, device_id=at.cache(lax.rem(at.c + d, 32)), device_id_type=MESH
        )
        return carry

    lax.fori_loop(1, 32, greet, 0)
    for k in range(1, 4):
        pl.semaphore_signal(barrier, inc=1, device_id=at.up(turn(at.z, k)), device_id_type=MESH)
    pl.semaphore_wait(barrier, 34)


class Mover:
    def __init__(self, send, recv):
        self.send, self.recv, self.count, self.started = send, recv, 0, []

    def go(self, src, dst, device):
        i = self.count
        self.count += 1
        copy = pltpu.make_async_remote_copy(
            src_ref=src, dst_ref=dst, send_sem=self.send.at[i], recv_sem=self.recv.at[i],
            device_id=device, device_id_type=MESH,
        )
        copy.start()
        self.started.append(copy)
        return copy

    def finish_sends(self):
        for copy in self.started:
            copy.wait_send()


class Ring:
    def __init__(self, mover, pos, device, own, dst, units):
        self.mover, self.pos, self.device, self.dst, self.units = mover, pos, device, dst, units
        right, left = device(turn(pos, 1)), device(turn(pos, -1))
        self.to_right, self.to_left = {}, {}
        half = len(units) // 2
        self.first, self.last = units[:half], units[half:]
        for u, v in zip(units, self.last + self.first):
            self.to_right[u] = mover.go(own(u), dst(pos, u, 1), right)
            self.to_left[v] = mover.go(own(v), dst(pos, v, -1), left)

    def onward(self):
        right, left = self.device(turn(self.pos, 1)), self.device(turn(self.pos, -1))
        self.far = []
        for u, v in zip(self.first, self.last):
            self.to_right[u].wait_recv()
            self.far.append(
                self.mover.go(
                    self.dst(turn(self.pos, -1), u, 1), self.dst(turn(self.pos, -1), u, 2), right
                )
            )
            self.to_left[v].wait_recv()
            self.far.append(
                self.mover.go(
                    self.dst(turn(self.pos, 1), v, -1), self.dst(turn(self.pos, 1), v, 2), left
                )
            )

    def near(self):
        for u in self.last:
            self.to_right[u].wait_recv()
        for v in self.first:
            self.to_left[v].wait_recv()

    def end(self):
        for copy in self.far:
            copy.wait_recv()


class Spread:
    def __init__(self, at, mover, live_out, full, first, width):
        self.at, self.mover, self.full = at, mover, full
        self.quarter = width // 4
        rows = pl.ds(pl.multiple_of(at.c * 16, 16), 16)
        self.start = [
            mover.go(
                live_out.at[rows, pl.ds(first, width)],
                full.at[k - 1, at.y, at.x, at.core],
                at.up(turn(at.z, -k)),
            )
            for k in range(1, 4)
        ]

    def cols(self, u, n=1):
        return pl.ds(u * self.quarter, n * self.quarter)

    def phase_one(self):
        at, full = self.at, self.full
        for copy in self.start:
            copy.wait_recv()
        a = lambda pos, u, k=0: full.at[:, at.y, pos, at.core, :, self.cols(u)]
        b = lambda pos, u, k=0: full.at[:, pos, at.x, at.core, :, self.cols(u)]
        self.one = [
            Ring(self.mover, at.x, lambda p: at.chip(at.y, p), lambda u: a(at.x, u), a, [0, 1]),
            Ring(self.mover, at.y, lambda p: at.chip(p, at.x), lambda u: b(at.y, u), b, [2, 3]),
        ]

    def phase_one_onward(self):
        for ring in self.one:
            ring.onward()

    def phase_two(self):
        at, full = self.at, self.full
        for ring in self.one:
            ring.near()
            ring.end()
        a = lambda pos, u, k=0: full.at[:, pos, :, at.core, :, self.cols(u)]
        b = lambda pos, u, k=0: full.at[:, :, pos, at.core, :, self.cols(u)]
        self.two = [
            Ring(self.mover, at.y, lambda p: at.chip(p, at.x), lambda u: a(at.y, u), a, [0, 1]),
            Ring(self.mover, at.x, lambda p: at.chip(at.y, p), lambda u: b(at.x, u), b, [2, 3]),
        ]
        self.over = []
        self.cross(0)

    def cross(self, k):
        at, full = self.at, self.full
        a = full.at[:, turn(at.y, k), :, at.core, :, self.cols(0, 2)]
        b = full.at[:, :, turn(at.x, k), at.core, :, self.cols(2, 2)]
        for view in (a, b):
            self.over.append(self.mover.go(view, view, at.sibling()))

    def phase_two_onward(self):
        for ring in self.two:
            ring.onward()
        for ring in self.two:
            ring.near()
        self.cross(1)
        self.cross(-1)

    def finish(self):
        for ring in self.two:
            ring.end()
        self.cross(2)
        for copy in self.over:
            copy.wait_recv()


def index_kernel(mine, every, send, recv, send2, recv2):
    at = Place()
    every[at.c, at.z] = mine[...]
    greet_all(at)
    mover = Mover(send, recv)
    near = [
        mover.go(every.at[at.c, at.z], every.at[at.c, at.z], at.up(turn(at.z, k)))
        for k in range(1, 4)
    ]
    for copy in near:
        copy.wait_recv()

    def copy(d):
        return pltpu.make_async_remote_copy(
            src_ref=every.at[at.c], dst_ref=every.at[at.c], send_sem=send2.at[d],
            recv_sem=recv2.at[d], device_id=at.cache(lax.rem(at.c + d, 32)), device_id_type=MESH,
        )

    def go(d, carry):
        copy(d).start()
        return carry

    def wait(d, carry):
        copy(d).wait()
        return carry

    lax.fori_loop(1, 32, go, 0)
    lax.fori_loop(1, 32, wait, 0)
    mover.finish_sends()


def index_exchange(ints):
    return pl.pallas_call(
        index_kernel,
        out_shape=jax.ShapeDtypeStruct((32, 4, 1, 128), jnp.int32),
        in_specs=[VM],
        out_specs=VM,
        scratch_shapes=[
            pltpu.SemaphoreType.DMA((4,)), pltpu.SemaphoreType.DMA((4,)),
            pltpu.SemaphoreType.DMA((32,)), pltpu.SemaphoreType.DMA((32,)),
        ],
        compiler_params=params(1, 8),
    )(ints)


def fetch_kernel(
    asked, place, memory, tok, score, live_out,
    x_full, tokens, scores, full,
    out_buf, in_buf0, in_buf1, own, pair_buf, a_buf, b_buf, a2_buf, b2_buf, tok_sum,
    send, recv, a2a_send, a2a_recv, local_sem,
):
    at = Place()
    greet_all(at)
    mover = Mover(send, recv)
    spread = Spread(at, mover, live_out, full, 0, 2048)
    in_buf = (in_buf0, in_buf1)

    def passage_copy(h, d):
        q = lax.rem(at.c + d, 32)
        return pltpu.make_async_remote_copy(
            src_ref=out_buf.at[h, pl.ds(2 * q, 2)], dst_ref=in_buf[h].at[pl.ds(2 * at.c, 2)],
            send_sem=a2a_send.at[h, d], recv_sem=a2a_recv.at[h, d],
            device_id=at.cache(q), device_id_type=MESH,
        )

    def send_half(h):
        lanes = pl.ds(h * 512, 512)

        def one(d, carry):
            q = lax.rem(at.c + d, 32)
            out_buf[h, 2 * q] = memory[asked[2 * q], :, lanes]
            out_buf[h, 2 * q + 1] = memory[asked[2 * q + 1], :, lanes]
            passage_copy(h, d).start()
            return carry

        lax.fori_loop(1, 32, one, 0)
        in_buf[h][2 * at.c] = memory[asked[2 * at.c], :, lanes]
        in_buf[h][2 * at.c + 1] = memory[asked[2 * at.c + 1], :, lanes]

    def wait_half(h):
        def one(d, carry):
            passage_copy(h, d).wait_recv()
            return carry

        lax.fori_loop(1, 32, one, 0)

        def pack(j, carry):
            own[h, pl.ds(pl.multiple_of(16 * j, 16), 16)] = in_buf[h][place[j]]
            return carry

        lax.fori_loop(0, 32, pack, 0)

    def part(pos, unit, k=0):
        h, g = unit
        return x_full.at[
            pl.ds(g * 256, 256), pl.ds(pl.multiple_of(pos * 1024 + h * 512, 512), 512)
        ]

    def ring_half(h):
        keep = pltpu.make_async_copy(
            own.at[h], x_full.at[:, pl.ds(pl.multiple_of(at.z * 1024 + h * 512, 512), 512)],
            local_sem.at[h],
        )
        keep.start()
        ring = Ring(
            mover, at.z, at.up, lambda u: own.at[u[0], pl.ds(u[1] * 256, 256)], part,
            [(h, 0), (h, 1)],
        )
        return ring, keep

    send_half(0)
    other = 1 - at.core
    pair = mover.go(tok.at[:, :, other], pair_buf, at.sibling())
    send_half(1)

    pair.wait_recv()

    def add_pair(y, carry):
        for x in range(4):
            pair_buf[y, x] = pair_buf[y, x] + tok[y, x, at.core]
        return carry

    lax.fori_loop(0, 4, add_pair, 0)
    lo, hi = pl.ds(0, 512), pl.ds(512, 512)
    tok_a = [
        mover.go(
            pair_buf.at[:, turn(at.x, k), :, lo], a_buf.at[k - 1], at.chip(at.y, turn(at.x, k))
        )
        for k in range(1, 4)
    ]
    tok_b = [
        mover.go(
            pair_buf.at[turn(at.y, k), :, :, hi], b_buf.at[k - 1], at.chip(turn(at.y, k), at.x)
        )
        for k in range(1, 4)
    ]
    near_scores = [
        mover.go(score, scores.at[at.z], at.up(turn(at.z, k))) for k in range(1, 4)
    ]
    scores[at.z] = score[...]
    spread.phase_one()

    wait_half(0)
    ring0, keep0 = ring_half(0)
    for copy in tok_a + tok_b:
        copy.wait_recv()

    def add_line(i, carry):
        a_buf[0, i] = (a_buf[0, i] + a_buf[1, i]) + (a_buf[2, i] + pair_buf[i, at.x, :, lo])
        b_buf[0, i] = (b_buf[0, i] + b_buf[1, i]) + (b_buf[2, i] + pair_buf[at.y, i, :, hi])
        return carry

    lax.fori_loop(0, 4, add_line, 0)
    tok_a2 = [
        mover.go(a_buf.at[0, turn(at.y, k)], a2_buf.at[k - 1], at.chip(turn(at.y, k), at.x))
        for k in range(1, 4)
    ]
    tok_b2 = [
        mover.go(b_buf.at[0, turn(at.x, k)], b2_buf.at[k - 1], at.chip(at.y, turn(at.x, k)))
        for k in range(1, 4)
    ]
    wait_half(1)
    ring1, keep1 = ring_half(1)
    for copy in tok_a2 + tok_b2:
        copy.wait_recv()
    tok_sum[:, lo] = (a2_buf[0] + a2_buf[1]) + (a2_buf[2] + a_buf[0, at.y])
    tok_sum[:, hi] = (b2_buf[0] + b2_buf[1]) + (b2_buf[2] + b_buf[0, at.x])
    mine = pl.ds(pl.multiple_of(at.z * 1024, 1024), 1024)
    near_tokens = [
        mover.go(tok_sum, tokens.at[:, mine], at.up(turn(at.z, k))) for k in range(1, 4)
    ]
    tokens[:, mine] = tok_sum[...]
    ring0.onward()
    spread.phase_one_onward()
    ring1.onward()
    spread.phase_two()
    for copy in near_scores + near_tokens:
        copy.wait_recv()
    spread.phase_two_onward()
    for ring in (ring0, ring1):
        ring.near()
        ring.end()
    spread.finish()
    keep0.wait()
    keep1.wait()
    mover.finish_sends()

    def sent(d, carry):
        passage_copy(0, d).wait_send()
        passage_copy(1, d).wait_send()
        return carry

    lax.fori_loop(1, 32, sent, 0)


def fetch(asked, place, memory, tok, score, live_out):
    return pl.pallas_call(
        fetch_kernel,
        out_shape=(
            jax.ShapeDtypeStruct((512, 4096), BF16),
            jax.ShapeDtypeStruct((48, 4096), BF16),
            jax.ShapeDtypeStruct((4, 1, 128), F32),
            jax.ShapeDtypeStruct((3, 4, 4, 2, 16, 2048), BF16),
        ),
        in_specs=[SM, SM, VM, VM, VM, ANY],
        out_specs=(ANY, VM, VM, ANY),
        scratch_shapes=[
            pltpu.VMEM((2, 64, 16, 512), BF16), pltpu.VMEM((64, 16, 512), BF16),
            pltpu.VMEM((64, 16, 512), BF16),
            pltpu.VMEM((2, 512, 512), BF16), pltpu.VMEM((4, 4, 48, 1024), BF16),
            pltpu.VMEM((3, 4, 48, 512), BF16), pltpu.VMEM((3, 4, 48, 512), BF16),
            pltpu.VMEM((3, 48, 512), BF16), pltpu.VMEM((3, 48, 512), BF16),
            pltpu.VMEM((48, 1024), BF16),
            pltpu.SemaphoreType.DMA((80,)), pltpu.SemaphoreType.DMA((80,)),
            pltpu.SemaphoreType.DMA((2, 32)), pltpu.SemaphoreType.DMA((2, 32)),
            pltpu.SemaphoreType.DMA((2,)),
        ],
        compiler_params=params(2, 40),
    )(asked, place, memory, tok, score, live_out)


def context_kernel(ctx, live_out, others, full, send, recv):
    at = Place()
    greet_all(at)
    mover = Mover(send, recv)
    spread = Spread(at, mover, live_out, full, 2048, 2048)
    rows = lambda u: pl.ds(u * 256, 256)

    def part(pos, u, k):
        return others.at[{1: 2, -1: 0, 2: 1}[k], rows(u)]

    ring = Ring(mover, at.z, at.up, lambda u: ctx.at[rows(u)], part, [0, 1, 2, 3])
    spread.phase_one()
    spread.phase_one_onward()
    ring.onward()
    spread.phase_two()
    spread.phase_two_onward()
    ring.near()
    ring.end()
    spread.finish()
    mover.finish_sends()


def share_context(ctx, live_out):
    return pl.pallas_call(
        context_kernel,
        out_shape=(
            jax.ShapeDtypeStruct((3, 1024, 512), BF16),
            jax.ShapeDtypeStruct((3, 4, 4, 2, 16, 2048), BF16),
        ),
        in_specs=[ANY, ANY],
        out_specs=(ANY, ANY),
        scratch_shapes=[pltpu.SemaphoreType.DMA((64,)), pltpu.SemaphoreType.DMA((64,))],
        compiler_params=params(3, 8),
    )(ctx, live_out)


def greet_z(at):
    barrier = pltpu.get_barrier_semaphore()
    for k in range(1, 4):
        pl.semaphore_signal(barrier, inc=1, device_id=at.up(turn(at.z, k)), device_id_type=MESH)
    pl.semaphore_wait(barrier, 3)


def inverse_kernel(mine, every, send, recv):
    at = Place()
    every[at.z] = mine[...]
    greet_z(at)
    mover = Mover(send, recv)
    near = [mover.go(mine, every.at[at.z], at.up(turn(at.z, k))) for k in range(1, 4)]
    for copy in near:
        copy.wait_recv()
    mover.finish_sends()


def share_inverse(mine):
    return pl.pallas_call(
        inverse_kernel,
        out_shape=jax.ShapeDtypeStruct((4, 2, 128), F32),
        in_specs=[VM],
        out_specs=VM,
        scratch_shapes=[pltpu.SemaphoreType.DMA((4,)), pltpu.SemaphoreType.DMA((4,))],
        compiler_params=params(4, 4),
    )(mine)


def decoded_kernel(part, out, buf, send, recv):
    at = Place()
    greet_z(at)
    mover = Mover(send, recv)
    near = [
        mover.go(part.at[turn(at.z, k)], buf.at[k - 1], at.up(turn(at.z, k)))
        for k in range(1, 4)
    ]
    for copy in near:
        copy.wait_recv()
    total = part[at.z].astype(F32)
    for k in range(3):
        total = total + buf[k].astype(F32)
    out[...] = total.astype(BF16)
    mover.finish_sends()


def add_decoded(part):
    return pl.pallas_call(
        decoded_kernel,
        out_shape=jax.ShapeDtypeStruct((32, 1024), BF16),
        in_specs=[VM],
        out_specs=VM,
        scratch_shapes=[
            pltpu.VMEM((3, 32, 1024), BF16),
            pltpu.SemaphoreType.DMA((4,)), pltpu.SemaphoreType.DMA((4,)),
        ],
        compiler_params=params(5, 8),
    )(part)


def shards(
    question_ids, answer_ids, owner, slot, passage_score, memory, embedding, live_gain, live_qkv,
    rel_bias, live_out, enc_gain, cross_kv, dec_gain, cross_query, cross_out,
):
    n_cache = lax.axis_size("cache")
    n_psg = lax.axis_size("psg")
    me_c = lax.axis_index("cache")
    me_z = lax.axis_index("psg")
    width = live_gain.shape[0]
    plen = memory.shape[1]
    qlen = question_ids.shape[1]
    alen = answer_ids.shape[1]
    own_count = owner.shape[1]
    total = own_count * n_psg
    seq = plen + qlen
    heads = rel_bias.shape[0]
    cols = live_out.shape[0]
    scale = HEAD ** (-0.5)

    ints = jnp.concatenate(
        [question_ids[0], answer_ids[0], owner[0, :, 0], slot[0], jnp.zeros((64,), jnp.int32)]
    ).reshape(1, 128)
    every = index_exchange(ints).reshape(n_cache, n_psg, 128)
    tokens = every[:, 0, : qlen + alen]
    owners = every[:, :, qlen + alen : qlen + alen + own_count].reshape(n_cache, total)
    slots = every[:, :, qlen + alen + own_count : 64].reshape(n_cache, total)
    order = jnp.arange(total)
    earlier = (owners[:, :, None] == owners[:, None, :]) & (order[None, :] < order[:, None])[None]
    rank = jnp.sum(earlier, axis=2)
    mine = owners == me_c
    asked = jnp.sum(
        jnp.where(mine[:, None, :] & (rank[:, None, :] == jnp.arange(2)[None, :, None]),
                  slots[:, None, :], 0),
        axis=2,
    ).reshape(-1)
    place = lax.dynamic_index_in_dim(owners * 2 + rank, me_c, 0, False)
    vocab = embedding.shape[0]
    onehot = (
        (tokens - me_c * vocab)[:, :, None] == jnp.arange(vocab, dtype=jnp.int32)
    ).astype(BF16)
    tok = jnp.einsum("qtv,vf->qtf", onehot, embedding, preferred_element_type=F32).astype(BF16)
    score = jnp.pad(passage_score, ((0, 0), (0, 120)))
    x_mem, token_full, scores, full_left = fetch(
        asked, place, memory, tok.reshape(4, 4, 2, qlen + alen, -1), score, live_out
    )
    x_q = token_full[:qlen]
    answer = token_full[qlen:]
    score_all = scores[:, 0, :own_count].reshape(total)

    q_dec = norm_project(answer, dec_gain, cross_query).reshape(alen, heads, HEAD)
    kv = cross_kv.reshape(width, 2 * cols)
    w_key = kv[:, :cols].reshape(width, heads, HEAD)
    w_val = kv[:, cols:].reshape(width, heads, HEAD)
    qg = (
        jnp.einsum("thd,fhd->htf", q_dec, w_key, preferred_element_type=F32) * enc_gain
    ).astype(BF16).reshape(heads * alen, width)

    proj = []
    for i in range(3):
        w = live_qkv[:, i]
        m = norm_project(x_mem, live_gain, w).reshape(total, plen, cols)
        n = norm_project(x_q, live_gain, w)
        proj.append(
            jnp.concatenate([m, jnp.broadcast_to(n[None], (total, qlen, cols))], axis=1).reshape(
                total, seq, heads, HEAD
            )
        )
    scores = jnp.einsum(
        "pqhd,pkhd->phqk", proj[0], proj[1], preferred_element_type=F32
    ) * scale + position_bias(rel_bias, seq)[None]
    ctx = (
        jnp.einsum("phqk,pkhd->pqhd", softmax_rows(scores), proj[2],
                   preferred_element_type=F32)
        .astype(BF16).reshape(total * seq, cols)
    )
    others, full_right = share_context(ctx, live_out)
    ctx_all = [ctx] + [others[k] for k in range(3)]
    full_left = full_left.reshape(3, cols, width // 2)
    full_right = full_right.reshape(3, cols, width // 2)
    out_full = [live_out] + [
        jnp.concatenate([full_left[k], full_right[k]], axis=1) for k in range(3)
    ]
    ql = [dot32(qg, o, ((1,), (1,))).astype(BF16) for o in out_full]

    own_rows = own_count * seq
    own_ctx = [lax.dynamic_slice_in_dim(c, me_z * own_rows, own_rows, 0) for c in ctx_all]
    attended = sum(
        dot32(own_ctx[z], out_full[z], ((1,), (0,))).astype(BF16).astype(F32) for z in range(n_psg)
    )
    own_mem = lax.dynamic_slice_in_dim(x_mem, me_z * own_count * plen, own_count * plen, 0)
    own_input = jnp.concatenate(
        [own_mem.reshape(own_count, plen, width),
         jnp.broadcast_to(x_q[None], (own_count, qlen, width))], axis=1,
    ).reshape(own_rows, width)
    encoded = (own_input.astype(F32) + attended).astype(BF16)
    enc32 = encoded.astype(F32)
    inv_own = lax.rsqrt(jnp.mean(enc32 * enc32, axis=-1) + EPSILON)
    inv = share_inverse(inv_own.reshape(2, 128)).reshape(total * seq)

    s_mem = dot32(qg, x_mem, ((1,), (1,))).reshape(-1, total, plen)
    s_q = jnp.broadcast_to(dot32(qg, x_q, ((1,), (1,)))[:, None], (heads * alen, total, qlen))
    s = jnp.concatenate([s_mem, s_q], axis=2).reshape(heads * alen, total * seq)
    for z in range(n_psg):
        s = s + dot32(ql[z], ctx_all[z], ((1,), (1,)))
    s = s * (inv * scale)[None] + jnp.repeat(score_all, seq)[None]
    top = jnp.max(s, axis=-1, keepdims=True)
    e = jnp.exp(s - top)
    sums = jnp.sum(e, axis=-1, keepdims=True)
    w = (e * inv[None] / sums).astype(BF16)
    w3 = w.reshape(-1, total, seq)
    w_mem = w3[:, :, :plen].reshape(-1, total * plen)
    w_q = jnp.sum(w3[:, :, plen:].astype(F32), axis=1).astype(BF16)
    zed = dot32(w_mem, x_mem, ((1,), (0,))) + dot32(w_q, x_q, ((1,), (0,)))
    for z in range(n_psg):
        part = dot32(w, ctx_all[z], ((1,), (0,))).astype(BF16)
        zed = zed + dot32(part, out_full[z], ((1,), (0,)))
    zed = (zed * enc_gain).astype(BF16).reshape(heads, alen, width)
    context = jnp.einsum("htf,fhd->thd", zed, w_val, preferred_element_type=F32).astype(BF16)
    part = dot32(context.reshape(alen, -1), cross_out, ((1,), (0,))).astype(BF16)
    decoded = add_decoded(part.reshape(alen, n_psg, -1).transpose(1, 0, 2))
    return encoded.reshape(1, own_count, seq, width), decoded[None]


def solution(mesh):
    return jax.shard_map(
        shards,
        mesh=mesh,
        in_specs=(
            P("cache", None), P("cache", None), P("cache", "psg", None), P("cache", "psg"),
            P("cache", "psg"), P("cache", None, "psg"), P("cache", "psg"), P(),
            P(None, None, "psg"), P("psg", None), P("psg", None), P(), P(None, None, "psg"), P(),
            P(None, "psg"), P("psg", None),
        ),
        out_specs=(P("cache", "psg", None, None), P("cache", None, "psg")),
        check_vma=False,
    )
```

```python
import functools

import jax
import jax.numpy as jnp
import numpy as np
from jax import lax
from jax.experimental import pallas as pl
from jax.experimental.pallas import tpu as pltpu
from jax.sharding import PartitionSpec as P

HEAD = 64
EPSILON = 1e-06
F32 = jnp.float32
BF16 = jnp.bfloat16


def bucket_table(length, bucket_count):
    positions = np.arange(length)
    relative = positions[None, :] - positions[:, None]
    halfway = bucket_count // 2
    exact_span = halfway // 2
    upper_side = (relative > 0).astype(np.int64) * halfway
    distance = np.abs(relative)
    log_bucket = exact_span + (
        np.log(np.maximum(distance, 1) / exact_span)
        / np.log(128.0 / exact_span)
        * (halfway - exact_span)
    ).astype(np.int64)
    log_bucket = np.minimum(log_bucket, halfway - 1)
    return upper_side + np.where(distance < exact_span, distance, log_bucket)


def position_bias(bias_table, length):
    bucket_count = bias_table.shape[1]
    buckets = bucket_table(length, bucket_count).reshape(-1)
    onehot = (buckets[None, :] == np.arange(bucket_count)[:, None]).astype(np.float32)
    spread = jnp.dot(
        bias_table, jnp.asarray(onehot, dtype=bias_table.dtype), precision=lax.Precision.HIGHEST
    )
    return spread.reshape(bias_table.shape[0], length, length)


def dot32(a, b, dims):
    return lax.dot_general(a, b, (dims, ((), ())), preferred_element_type=F32)


MESH = pl.DeviceIdType.MESH
VM = pl.BlockSpec(memory_space=pltpu.VMEM)
SM = pl.BlockSpec(memory_space=pltpu.SMEM)
ANY = pl.BlockSpec(memory_space=pl.ANY)


def params(collective_id, mib):
    return pltpu.CompilerParams(
        collective_id=collective_id, has_side_effects=True, vmem_limit_bytes=mib << 20
    )


class Place:
    def __init__(self):
        self.c = lax.axis_index("cache")
        self.z = lax.axis_index("psg")
        self.core = lax.rem(self.c, 2)
        self.x = lax.rem(lax.div(self.c, 2), 4)
        self.y = lax.div(self.c, 8)

    def cache(self, c):
        return {"cache": c, "psg": self.z}

    def chip(self, y, x):
        return self.cache((y * 4 + x) * 2 + self.core)

    def sibling(self):
        return self.cache(self.c + 1 - 2 * self.core)

    def up(self, z):
        return {"cache": self.c, "psg": z}


def turn(p, k):
    return lax.rem(p + k + 4, 4)


def greet_all(at):
    barrier = pltpu.get_barrier_semaphore()

    def greet(d, carry):
        pl.semaphore_signal(
            barrier, inc=1, device_id=at.cache(lax.rem(at.c + d, 32)), device_id_type=MESH
        )
        return carry

    lax.fori_loop(1, 32, greet, 0)
    for k in range(1, 4):
        pl.semaphore_signal(barrier, inc=1, device_id=at.up(turn(at.z, k)), device_id_type=MESH)
    pl.semaphore_wait(barrier, 34)


class Mover:
    def __init__(self, send, recv):
        self.send, self.recv, self.count, self.started = send, recv, 0, []

    def go(self, src, dst, device):
        i = self.count
        self.count += 1
        copy = pltpu.make_async_remote_copy(
            src_ref=src, dst_ref=dst, send_sem=self.send.at[i], recv_sem=self.recv.at[i],
            device_id=device, device_id_type=MESH,
        )
        copy.start()
        self.started.append(copy)
        return copy

    def finish_sends(self):
        for copy in self.started:
            copy.wait_send()


class Ring:
    def __init__(self, mover, pos, device, own, dst, units, start=True):
        self.mover, self.pos, self.device, self.own, self.dst = mover, pos, device, own, dst
        self.right, self.left = device(turn(pos, 1)), device(turn(pos, -1))
        self.to_right, self.to_left = {}, {}
        half = len(units) // 2
        self.first, self.last = units[:half], units[half:]
        if start:
            for u, v in zip(units, self.last + self.first):
                self.begin_right(u)
                self.begin_left(v)

    def begin_right(self, u):
        self.to_right[u] = self.mover.go(self.own(u), self.dst(self.pos, u, 1), self.right)

    def begin_left(self, u):
        self.to_left[u] = self.mover.go(self.own(u), self.dst(self.pos, u, -1), self.left)

    def onward(self):
        before, after = turn(self.pos, -1), turn(self.pos, 1)
        self.far = []
        for u, v in zip(self.first, self.last):
            self.to_right[u].wait_recv()
            self.far.append(
                self.mover.go(self.dst(before, u, 1), self.dst(before, u, 2), self.right)
            )
            self.to_left[v].wait_recv()
            self.far.append(
                self.mover.go(self.dst(after, v, -1), self.dst(after, v, 2), self.left)
            )

    def near(self):
        for u in self.last:
            self.to_right[u].wait_recv()
        for v in self.first:
            self.to_left[v].wait_recv()

    def end(self):
        for copy in self.far:
            copy.wait_recv()


class Spread:
    def __init__(self, at, mover, live_out, full, first, width):
        self.at, self.mover, self.full = at, mover, full
        self.quarter = width // 4
        rows = pl.ds(pl.multiple_of(at.c * 16, 16), 16)
        self.start = [
            mover.go(
                live_out.at[rows, pl.ds(first, width)],
                full.at[k - 1, at.y, at.x, at.core],
                at.up(turn(at.z, -k)),
            )
            for k in range(1, 4)
        ]

    def cols(self, u, n=1):
        return pl.ds(u * self.quarter, n * self.quarter)

    def phase_one(self):
        at, full = self.at, self.full
        for copy in self.start:
            copy.wait_recv()
        a = lambda pos, u, k=0: full.at[:, at.y, pos, at.core, :, self.cols(u)]
        b = lambda pos, u, k=0: full.at[:, pos, at.x, at.core, :, self.cols(u)]
        self.one = [
            Ring(self.mover, at.x, lambda p: at.chip(at.y, p), lambda u: a(at.x, u), a, [0, 1]),
            Ring(self.mover, at.y, lambda p: at.chip(p, at.x), lambda u: b(at.y, u), b, [2, 3]),
        ]

    def phase_one_onward(self):
        for ring in self.one:
            ring.onward()

    def phase_two(self):
        at, full = self.at, self.full
        for ring in self.one:
            ring.near()
            ring.end()
        a = lambda pos, u, k=0: full.at[:, pos, :, at.core, :, self.cols(u)]
        b = lambda pos, u, k=0: full.at[:, :, pos, at.core, :, self.cols(u)]
        self.two = [
            Ring(self.mover, at.y, lambda p: at.chip(p, at.x), lambda u: a(at.y, u), a, [0, 1]),
            Ring(self.mover, at.x, lambda p: at.chip(at.y, p), lambda u: b(at.x, u), b, [2, 3]),
        ]
        self.over = []
        self.cross(0)

    def cross(self, k):
        at, full = self.at, self.full
        a = full.at[:, turn(at.y, k), :, at.core, :, self.cols(0, 2)]
        b = full.at[:, :, turn(at.x, k), at.core, :, self.cols(2, 2)]
        for view in (a, b):
            self.over.append(self.mover.go(view, view, at.sibling()))

    def phase_two_onward(self):
        for ring in self.two:
            ring.onward()
        for ring in self.two:
            ring.near()
        self.cross(1)
        self.cross(-1)

    def finish(self):
        for ring in self.two:
            ring.end()
        self.cross(2)
        for copy in self.over:
            copy.wait_recv()


def index_kernel(mine, every, send, recv, send2, recv2):
    at = Place()
    every[at.c, at.z] = mine[...]
    greet_all(at)
    mover = Mover(send, recv)
    near = [
        mover.go(every.at[at.c, at.z], every.at[at.c, at.z], at.up(turn(at.z, k)))
        for k in range(1, 4)
    ]
    for copy in near:
        copy.wait_recv()

    def copy(d):
        return pltpu.make_async_remote_copy(
            src_ref=every.at[at.c], dst_ref=every.at[at.c], send_sem=send2.at[d],
            recv_sem=recv2.at[d], device_id=at.cache(lax.rem(at.c + d, 32)), device_id_type=MESH,
        )

    def go(d, carry):
        copy(d).start()
        return carry

    def wait(d, carry):
        copy(d).wait()
        return carry

    lax.fori_loop(1, 32, go, 0)
    lax.fori_loop(1, 32, wait, 0)
    mover.finish_sends()


def index_exchange(ints):
    return pl.pallas_call(
        index_kernel,
        out_shape=jax.ShapeDtypeStruct((32, 4, 1, 128), jnp.int32),
        in_specs=[VM],
        out_specs=VM,
        scratch_shapes=[
            pltpu.SemaphoreType.DMA((4,)), pltpu.SemaphoreType.DMA((4,)),
            pltpu.SemaphoreType.DMA((32,)), pltpu.SemaphoreType.DMA((32,)),
        ],
        compiler_params=params(1, 8),
    )(ints)


def norm_rows(rows, gain):
    wide = rows.astype(F32)
    inverse = lax.rsqrt(jnp.mean(wide * wide, axis=-1, keepdims=True) + EPSILON)
    return (wide * gain).astype(BF16), inverse


def fetch_kernel(
    asked, place, memory, tok, score, live_out, w_qkv, cross_kv, cross_query,
    live_gain, enc_gain, dec_gain,
    x_out, tokens, scores, full, proj_mem, proj_q, qg, w_val_out,
    out_buf, in_buf0, in_buf1, own, pair_buf, a_buf, b_buf, a2_buf, b2_buf, tok_sum,
    x_full, weights, acc, squares, scaled, w_query, kv_buf, w_key, w_val,
    send, recv, a2a_send, a2a_recv, local_sem, kv_sem, out_sem,
):
    at = Place()
    load_weights = [
        pltpu.make_async_copy(w_qkv.at[i], weights.at[i], local_sem.at[i]) for i in range(3)
    ] + [pltpu.make_async_copy(cross_query, w_query, local_sem.at[3])]
    for copy in load_weights:
        copy.start()

    def kv_copy(i):
        slot = lax.rem(i, 2)
        return pltpu.make_async_copy(
            cross_kv.at[pl.ds(i * 256, 256)], kv_buf.at[slot], kv_sem.at[slot]
        )

    kv_copy(0).start()

    def split_kv(first, last):
        def one(i, carry):
            @pl.when(i < 15)
            def _():
                kv_copy(i + 1).start()

            kv_copy(i).wait()
            rows = pl.ds(pl.multiple_of(i * 256, 256), 256)
            slot = lax.rem(i, 2)
            w_key[rows] = kv_buf[slot, :, 0, :]
            w_val[rows] = kv_buf[slot, :, 1, :]
            return carry

        lax.fori_loop(first, last, one, 0)

    greet_all(at)
    mover = Mover(send, recv)
    spread = Spread(at, mover, live_out, full, 0, 2048)
    in_buf = (in_buf0, in_buf1)

    def passage_copy(h, d):
        q = lax.rem(at.c + d, 32)
        return pltpu.make_async_remote_copy(
            src_ref=out_buf.at[h, pl.ds(2 * q, 2)], dst_ref=in_buf[h].at[pl.ds(2 * at.c, 2)],
            send_sem=a2a_send.at[h, d], recv_sem=a2a_recv.at[h, d],
            device_id=at.cache(q), device_id_type=MESH,
        )

    def send_half(h):
        lanes = pl.ds(h * 512, 512)

        def one(d, carry):
            q = lax.rem(at.c + d, 32)
            out_buf[h, 2 * q] = memory[asked[2 * q], :, lanes]
            out_buf[h, 2 * q + 1] = memory[asked[2 * q + 1], :, lanes]
            passage_copy(h, d).start()
            return carry

        lax.fori_loop(1, 32, one, 0)
        in_buf[h][2 * at.c] = memory[asked[2 * at.c], :, lanes]
        in_buf[h][2 * at.c + 1] = memory[asked[2 * at.c + 1], :, lanes]

    def wait_half(h):
        def one(d, carry):
            passage_copy(h, d).wait_recv()
            return carry

        lax.fori_loop(1, 32, one, 0)

        def pack(j, carry):
            own[h, pl.ds(pl.multiple_of(16 * j, 16), 16)] = in_buf[h][place[j]]
            return carry

        lax.fori_loop(0, 32, pack, 0)

    def lanes_of(pos, h):
        return pl.ds(pl.multiple_of(pos * 1024 + h * 512, 512), 512)

    def part(pos, unit, k=0):
        h, g = unit
        return x_full.at[pl.ds(g * 256, 256), lanes_of(pos, h)]

    def ring_half(h):
        return Ring(
            mover, at.z, at.up, lambda u: own.at[u[0], pl.ds(u[1] * 256, 256)], part,
            [(h, 0), (h, 1)],
        )

    stored = []

    def multiply(k, h):
        pos = turn(at.z, k)
        lanes = lanes_of(pos, h)
        if k == 0:
            x_full[:, lanes] = own[h]
        keep = pltpu.make_async_copy(
            x_full.at[:, lanes], x_out.at[:, lanes], out_sem.at[len(stored)]
        )
        keep.start()
        first = not stored
        stored.append(keep)
        gain = live_gain[:, lanes]
        for r in range(2):
            rows = pl.ds(r * 256, 256)
            wide = x_full[rows, lanes].astype(F32)
            scaled[rows] = (wide * gain).astype(BF16)
            square = jnp.sum(wide * wide, axis=1, keepdims=True)
            squares[rows] = square if first else squares[rows] + square

        def one(i, carry):
            product = jnp.dot(scaled[...], weights[i, lanes], preferred_element_type=F32)
            acc[i] = product if first else acc[i] + product
            return carry

        lax.fori_loop(0, 3, one, 0)

    send_half(0)
    other = 1 - at.core
    pair = mover.go(tok.at[:, :, other], pair_buf, at.sibling())
    send_half(1)
    split_kv(0, 2)

    pair.wait_recv()

    def add_pair(y, carry):
        for x in range(4):
            pair_buf[y, x] = pair_buf[y, x] + tok[y, x, at.core]
        return carry

    lax.fori_loop(0, 4, add_pair, 0)
    lo, hi = pl.ds(0, 512), pl.ds(512, 512)
    tok_a = [
        mover.go(
            pair_buf.at[:, turn(at.x, k), :, lo], a_buf.at[k - 1], at.chip(at.y, turn(at.x, k))
        )
        for k in range(1, 4)
    ]
    tok_b = [
        mover.go(
            pair_buf.at[turn(at.y, k), :, :, hi], b_buf.at[k - 1], at.chip(turn(at.y, k), at.x)
        )
        for k in range(1, 4)
    ]
    near_scores = [
        mover.go(score, scores.at[at.z], at.up(turn(at.z, k))) for k in range(1, 4)
    ]
    scores[at.z] = score[...]
    spread.phase_one()
    split_kv(2, 5)

    wait_half(0)
    ring0 = ring_half(0)
    for copy in tok_a + tok_b:
        copy.wait_recv()

    def add_line(i, carry):
        a_buf[0, i] = (a_buf[0, i] + a_buf[1, i]) + (a_buf[2, i] + pair_buf[i, at.x, :, lo])
        b_buf[0, i] = (b_buf[0, i] + b_buf[1, i]) + (b_buf[2, i] + pair_buf[at.y, i, :, hi])
        return carry

    lax.fori_loop(0, 4, add_line, 0)
    tok_a2 = [
        mover.go(a_buf.at[0, turn(at.y, k)], a2_buf.at[k - 1], at.chip(turn(at.y, k), at.x))
        for k in range(1, 4)
    ]
    tok_b2 = [
        mover.go(b_buf.at[0, turn(at.x, k)], b2_buf.at[k - 1], at.chip(at.y, turn(at.x, k)))
        for k in range(1, 4)
    ]
    wait_half(1)
    ring1 = ring_half(1)
    for copy in load_weights:
        copy.wait()
    multiply(0, 0)
    for copy in tok_a2 + tok_b2:
        copy.wait_recv()
    tok_sum[:, lo] = (a2_buf[0] + a2_buf[1]) + (a2_buf[2] + a_buf[0, at.y])
    tok_sum[:, hi] = (b2_buf[0] + b2_buf[1]) + (b2_buf[2] + b_buf[0, at.x])
    mine = pl.ds(pl.multiple_of(at.z * 1024, 1024), 1024)
    near_tokens = [
        mover.go(tok_sum, tokens.at[:, mine], at.up(turn(at.z, k))) for k in range(1, 4)
    ]
    tokens[:, mine] = tok_sum[...]
    ring0.onward()
    spread.phase_one_onward()
    multiply(0, 1)
    ring1.onward()
    split_kv(5, 9)
    spread.phase_two()
    ring0.near()
    multiply(1, 0)
    multiply(-1, 0)
    spread.phase_two_onward()
    split_kv(9, 16)
    keep_values = pltpu.make_async_copy(w_val, w_val_out, local_sem.at[4])
    keep_values.start()
    for copy in near_scores + near_tokens:
        copy.wait_recv()

    rows, inverse = norm_rows(tokens[0:16], live_gain[...])

    def project(i, carry):
        total = jnp.dot(rows, weights[i], preferred_element_type=F32)
        proj_q[i] = (total * inverse).astype(BF16)
        return carry

    lax.fori_loop(0, 3, project, 0)
    rows_a, inverse_a = norm_rows(tokens[16:48], dec_gain[...])
    queries = jnp.dot(rows_a, w_query[...], preferred_element_type=F32) * inverse_a
    head = lax.broadcasted_iota(jnp.int32, (32, 512), 1) // HEAD
    for h in range(8):
        scaled[pl.ds(32 * h, 32)] = jnp.where(head == h, queries, 0.0).astype(BF16)

    def fold(n, carry):
        cols = pl.ds(pl.multiple_of(n * 1024, 1024), 1024)
        product = dot32(scaled[pl.ds(0, 256)], w_key[cols], ((1,), (1,)))
        qg[:, cols] = (product * enc_gain[:, cols]).astype(BF16)
        return carry

    lax.fori_loop(0, 4, fold, 0)
    ring1.near()
    multiply(1, 1)
    multiply(-1, 1)
    ring0.end()
    multiply(2, 0)
    ring1.end()
    multiply(2, 1)
    inverse_m = lax.rsqrt(squares[...] * (1.0 / 4096) + EPSILON)

    def close(i, carry):
        proj_mem[i] = (acc[i] * inverse_m).astype(BF16)
        return carry

    lax.fori_loop(0, 3, close, 0)
    spread.finish()
    for copy in stored:
        copy.wait()
    keep_values.wait()
    mover.finish_sends()

    def sent(d, carry):
        passage_copy(0, d).wait_send()
        passage_copy(1, d).wait_send()
        return carry

    lax.fori_loop(1, 32, sent, 0)


def fetch(*args):
    return pl.pallas_call(
        fetch_kernel,
        out_shape=(
            jax.ShapeDtypeStruct((512, 4096), BF16),
            jax.ShapeDtypeStruct((48, 4096), BF16),
            jax.ShapeDtypeStruct((4, 1, 128), F32),
            jax.ShapeDtypeStruct((3, 4, 4, 2, 16, 2048), BF16),
            jax.ShapeDtypeStruct((3, 512, 512), BF16),
            jax.ShapeDtypeStruct((3, 16, 512), BF16),
            jax.ShapeDtypeStruct((256, 4096), BF16),
            jax.ShapeDtypeStruct((4096, 512), BF16),
        ),
        in_specs=[SM, SM, VM, VM, VM, ANY, ANY, ANY, ANY, VM, VM, VM],
        out_specs=(ANY, VM, VM, ANY, VM, VM, VM, ANY),
        scratch_shapes=[
            pltpu.VMEM((2, 64, 16, 512), BF16), pltpu.VMEM((64, 16, 512), BF16),
            pltpu.VMEM((64, 16, 512), BF16),
            pltpu.VMEM((2, 512, 512), BF16), pltpu.VMEM((4, 4, 48, 1024), BF16),
            pltpu.VMEM((3, 4, 48, 512), BF16), pltpu.VMEM((3, 4, 48, 512), BF16),
            pltpu.VMEM((3, 48, 512), BF16), pltpu.VMEM((3, 48, 512), BF16),
            pltpu.VMEM((48, 1024), BF16),
            pltpu.VMEM((512, 4096), BF16), pltpu.VMEM((3, 4096, 512), BF16),
            pltpu.VMEM((3, 512, 512), F32), pltpu.VMEM((512, 1), F32),
            pltpu.VMEM((512, 512), BF16), pltpu.VMEM((4096, 512), BF16),
            pltpu.VMEM((2, 256, 2, 512), BF16), pltpu.VMEM((4096, 512), BF16),
            pltpu.VMEM((4096, 512), BF16),
            pltpu.SemaphoreType.DMA((80,)), pltpu.SemaphoreType.DMA((80,)),
            pltpu.SemaphoreType.DMA((2, 32)), pltpu.SemaphoreType.DMA((2, 32)),
            pltpu.SemaphoreType.DMA((5,)), pltpu.SemaphoreType.DMA((2,)),
            pltpu.SemaphoreType.DMA((8,)),
        ],
        compiler_params=params(2, 60),
    )(*args)


def reader_kernel(
    proj_mem, proj_q, bias, x_mem, tokens, qg, scores, left_in, live_out, w_val_in, cross_out_in,
    enc_gain,
    encoded, decoded,
    ctx, others, x_seq, left, right, own_out, w_val, w_out, ql, ql_part, s, w, zc, zed, heads_out,
    inv, parts, part_buf, send, recv, local_sem,
):
    at = Place()
    loads = [
        pltpu.make_async_copy(a, b, local_sem.at[i])
        for i, (a, b) in enumerate([
            (x_mem, x_seq.at[:, pl.ds(0, 16)]), (live_out, own_out), (left_in, left),
            (w_val_in, w_val), (cross_out_in, w_out),
        ])
    ]
    for copy in loads:
        copy.start()
    greet_all(at)
    mover = Mover(send, recv)
    spread = Spread(at, mover, live_out, right, 2048, 2048)
    scale = HEAD ** (-0.5)
    nt = ((1,), (1,))

    def chunk(j):
        return pl.ds(pl.multiple_of(j * 256, 256), 256)

    def part(pos, u, k):
        return others.at[{1: 2, -1: 0, 2: 1}[k], chunk(turn(pos, u))]

    ring = Ring(
        mover, at.z, at.up, lambda u: ctx.at[chunk(turn(at.z, u))], part, [1, 2, 3, 0], False
    )

    low = lax.broadcasted_iota(jnp.int32, (128, 128), 1) < HEAD

    def attend(j):
        def group(g, carry):
            first = j * 8 + g * 4

            def pair(i, p):
                lanes = pl.ds(128 * p, 128)
                pieces = []
                for n in range(4):
                    pieces.append(
                        proj_mem[i, pl.ds(pl.multiple_of((first + n) * 16, 16), 16), lanes]
                    )
                    pieces.append(proj_q[i, :, lanes])
                return jnp.concatenate(pieces, axis=0)

            for p in range(4):
                q, k, v = pair(0, p), pair(1, p), pair(2, p)
                both = []
                for e in range(2):
                    keep = low if e == 0 else jnp.logical_not(low)
                    sc = dot32(jnp.where(keep, q, jnp.zeros_like(q)), k, nt) * scale
                    sc = sc + bias[2 * p + e]
                    ex = jnp.exp(sc - jnp.max(sc, axis=1, keepdims=True))
                    ex = (ex / jnp.sum(ex, axis=1, keepdims=True)).astype(BF16)
                    both.append(jnp.dot(ex, v, preferred_element_type=F32))
                ctx[pl.ds(pl.multiple_of(first * 32, 128), 128), pl.ds(128 * p, 128)] = jnp.where(
                    low, both[0], both[1]
                ).astype(BF16)
            return carry

        lax.fori_loop(0, 2, group, 0)

    for n, u in enumerate((1, 3, 2, 0)):
        attend(turn(at.z, u))
        ring.begin_right(u)
        ring.begin_left(u)
        if n == 0:
            spread.phase_one()

    loads[0].wait()

    def fill(p, carry):
        x_seq[p, pl.ds(16, 16)] = tokens[pl.ds(0, 16)]
        return carry

    lax.fori_loop(0, 32, fill, 0)
    spread.phase_one_onward()

    def rows_of(j):
        return x_seq[pl.ds(j * 8, 8)].reshape(256, 4096)

    def score_inputs(j, carry):
        s[j] = dot32(qg[...], rows_of(j), nt)
        return carry

    lax.fori_loop(0, 4, score_inputs, 0)
    ring.onward()
    loads[1].wait()
    ql[0] = dot32(qg[...], own_out[...], nt).astype(BF16)

    def score_own(j, carry):
        s[j] = s[j] + dot32(ql[0], ctx[chunk(j)], nt)
        return carry

    lax.fori_loop(0, 4, score_own, 0)
    spread.phase_two()
    mine = chunk(at.z)

    def attend_own(n, carry):
        cols = pl.ds(pl.multiple_of(n * 1024, 1024), 1024)
        zed[:, cols] = (
            jnp.dot(ctx[mine], own_out[:, cols], preferred_element_type=F32)
            .astype(BF16).astype(F32)
        )
        return carry

    lax.fori_loop(0, 4, attend_own, 0)
    loads[2].wait()

    def fold_left(k, carry):
        ql_part[k] = dot32(qg[:, pl.ds(0, 2048)], left[k], nt)
        return carry

    lax.fori_loop(0, 3, fold_left, 0)
    spread.phase_two_onward()
    ring.near()
    ring.end()

    def group_rows(k, n):
        if n < 2:
            return left[k, :, pl.ds(n * 1024, 1024)]
        return right[k, :, :, :, :, pl.ds((n - 2) * 1024, 1024)].reshape(512, 1024)

    def attend_other(n):
        def one(k, carry):
            cols = pl.ds(n * 1024, 1024)
            zed[:, cols] = zed[:, cols] + (
                jnp.dot(others[k, mine], group_rows(k, n), preferred_element_type=F32)
                .astype(BF16).astype(F32)
            )
            return carry

        lax.fori_loop(0, 3, one, 0)

    attend_other(0)
    attend_other(1)
    spread.finish()
    attend_other(2)
    attend_other(3)

    own_rows = rows_of(at.z).astype(F32) + zed[...]
    own_rows = own_rows.astype(BF16)
    encoded[...] = own_rows
    own_rows = own_rows.astype(F32)
    norm = lax.rsqrt(jnp.sum(own_rows * own_rows, axis=1, keepdims=True) * (1.0 / 4096) + EPSILON)
    inv[at.z] = jnp.transpose(jnp.broadcast_to(norm, (256, 128)))[0:1]
    near = [mover.go(inv.at[at.z], inv.at[at.z], at.up(turn(at.z, k))) for k in range(1, 4)]

    def fold_right(k, carry):
        ql[k + 1] = (
            ql_part[k] + dot32(qg[:, pl.ds(2048, 2048)], right[k].reshape(512, 2048), nt)
        ).astype(BF16)
        return carry

    lax.fori_loop(0, 3, fold_right, 0)

    def score_others(j, carry):
        total = s[j]
        for k in range(3):
            total = total + dot32(ql[k + 1], others[k, chunk(j)], nt)
        s[j] = total
        return carry

    lax.fori_loop(0, 4, score_others, 0)
    for copy in near:
        copy.wait_recv()

    passage = lax.broadcasted_iota(jnp.int32, (1, 256), 1) // 32
    top = None
    for j in range(4):
        row = jnp.zeros((1, 256), F32)
        line = scores[j]
        for p in range(8):
            row = row + jnp.where(passage == p, line[:, p : p + 1], 0.0)
        total = s[j] * (inv[j] * scale) + row
        s[j] = total
        here = jnp.max(total, axis=1, keepdims=True)
        top = here if top is None else jnp.maximum(top, here)
    sums = jnp.zeros((256, 1), F32)
    for j in range(4):
        ex = jnp.exp(s[j] - top)
        s[j] = ex
        sums = sums + jnp.sum(ex, axis=1, keepdims=True)
    for j in range(4):
        w[j] = (s[j] * inv[j] / sums).astype(BF16)

    def mix(source):
        total = jnp.zeros((256, 512), F32)
        for j in range(4):
            total = total + jnp.dot(w[j], source[pl.ds(256 * j, 256)], preferred_element_type=F32)
        return total.astype(BF16)

    zc[0] = mix(ctx)

    def mix_other(k, carry):
        zc[k + 1] = mix(others.at[k])
        return carry

    lax.fori_loop(0, 3, mix_other, 0)
    for copy in loads[3:]:
        copy.wait()
    for n in range(4):
        cols = pl.ds(n * 1024, 1024)
        total = jnp.dot(zc[0], own_out[:, cols], preferred_element_type=F32)
        for j in range(4):
            total = total + jnp.dot(
                w[j], x_seq[pl.ds(8 * j, 8), :, cols].reshape(256, 1024),
                preferred_element_type=F32,
            )
        for k in range(3):
            total = total + jnp.dot(zc[k + 1], group_rows(k, n), preferred_element_type=F32)
        total = (total * enc_gain[:, cols]).astype(BF16)
        product = jnp.dot(total, w_val[cols], preferred_element_type=F32)
        heads_out[...] = product if n == 0 else heads_out[...] + product
    head = lax.broadcasted_iota(jnp.int32, (32, 512), 1) // HEAD
    context = jnp.zeros((32, 512), F32)
    for h in range(8):
        context = context + jnp.where(head == h, heads_out[pl.ds(32 * h, 32)], 0.0)
    context = context.astype(BF16)
    for j in range(4):
        parts[j] = jnp.dot(
            context, w_out[:, pl.ds(1024 * j, 1024)], preferred_element_type=F32
        ).astype(BF16)
    last = [
        mover.go(parts.at[turn(at.z, k)], part_buf.at[k - 1], at.up(turn(at.z, k)))
        for k in range(1, 4)
    ]
    for copy in last:
        copy.wait_recv()
    total = parts[at.z].astype(F32)
    for k in range(3):
        total = total + part_buf[k].astype(F32)
    decoded[...] = total.astype(BF16)
    mover.finish_sends()


def reader(*args):
    return pl.pallas_call(
        reader_kernel,
        out_shape=(
            jax.ShapeDtypeStruct((256, 4096), BF16),
            jax.ShapeDtypeStruct((32, 1024), BF16),
        ),
        in_specs=[VM, VM, VM, ANY, VM, VM, VM, ANY, ANY, ANY, ANY, VM],
        out_specs=(VM, VM),
        scratch_shapes=[
            pltpu.VMEM((1024, 512), BF16), pltpu.VMEM((3, 1024, 512), BF16),
            pltpu.VMEM((32, 32, 4096), BF16), pltpu.VMEM((3, 512, 2048), BF16),
            pltpu.VMEM((3, 4, 4, 2, 16, 2048), BF16), pltpu.VMEM((512, 4096), BF16),
            pltpu.VMEM((4096, 512), BF16), pltpu.VMEM((512, 4096), BF16),
            pltpu.VMEM((4, 256, 512), BF16), pltpu.VMEM((3, 256, 512), F32),
            pltpu.VMEM((4, 256, 256), F32), pltpu.VMEM((4, 256, 256), BF16),
            pltpu.VMEM((4, 256, 512), BF16), pltpu.VMEM((256, 4096), F32),
            pltpu.VMEM((256, 512), F32), pltpu.VMEM((4, 1, 256), F32),
            pltpu.VMEM((4, 32, 1024), BF16), pltpu.VMEM((3, 32, 1024), BF16),
            pltpu.SemaphoreType.DMA((64,)), pltpu.SemaphoreType.DMA((64,)),
            pltpu.SemaphoreType.DMA((5,)),
        ],
        compiler_params=params(3, 60),
    )(*args)


def shards(
    question_ids, answer_ids, owner, slot, passage_score, memory, embedding, live_gain, live_qkv,
    rel_bias, live_out, enc_gain, cross_kv, dec_gain, cross_query, cross_out,
):
    n_cache = lax.axis_size("cache")
    n_psg = lax.axis_size("psg")
    me_c = lax.axis_index("cache")
    width = live_gain.shape[0]
    plen = memory.shape[1]
    qlen = question_ids.shape[1]
    alen = answer_ids.shape[1]
    own_count = owner.shape[1]
    total = own_count * n_psg
    seq = plen + qlen
    cols = live_out.shape[0]

    ints = jnp.concatenate(
        [question_ids[0], answer_ids[0], owner[0, :, 0], slot[0], jnp.zeros((64,), jnp.int32)]
    ).reshape(1, 128)
    every = index_exchange(ints).reshape(n_cache, n_psg, 128)
    tokens = every[:, 0, : qlen + alen]
    owners = every[:, :, qlen + alen : qlen + alen + own_count].reshape(n_cache, total)
    slots = every[:, :, qlen + alen + own_count : 64].reshape(n_cache, total)
    order = jnp.arange(total)
    earlier = (owners[:, :, None] == owners[:, None, :]) & (order[None, :] < order[:, None])[None]
    rank = jnp.sum(earlier, axis=2)
    mine = owners == me_c
    asked = jnp.sum(
        jnp.where(mine[:, None, :] & (rank[:, None, :] == jnp.arange(2)[None, :, None]),
                  slots[:, None, :], 0),
        axis=2,
    ).reshape(-1)
    place = lax.dynamic_index_in_dim(owners * 2 + rank, me_c, 0, False)
    vocab = embedding.shape[0]
    onehot = (
        (tokens - me_c * vocab)[:, :, None] == jnp.arange(vocab, dtype=jnp.int32)
    ).astype(BF16)
    tok = jnp.einsum("qtv,vf->qtf", onehot, embedding, preferred_element_type=F32).astype(BF16)
    score = jnp.pad(passage_score, ((0, 0), (0, 120)))
    x_mem, token_full, scores, full_left, proj_mem, proj_q, qg, w_val = fetch(
        asked, place, memory, tok.reshape(4, 4, 2, qlen + alen, -1), score, live_out,
        jnp.transpose(live_qkv, (1, 0, 2)), cross_kv, cross_query,
        live_gain.reshape(1, width), enc_gain.reshape(1, width), dec_gain.reshape(1, width),
    )
    position = position_bias(rel_bias, seq)
    block = np.arange(128) // seq
    bias = jnp.where(
        jnp.asarray(block[:, None] == block[None, :])[None], jnp.tile(position, (1, 4, 4)), -1e30
    )
    encoded, decoded = reader(
        proj_mem, proj_q, bias, x_mem.reshape(total, plen, width), token_full, qg, scores,
        full_left.reshape(3, cols, width // 2), live_out, w_val, cross_out,
        enc_gain.reshape(1, width),
    )
    return encoded.reshape(1, own_count, seq, width), decoded[None]


def solution(mesh):
    return jax.shard_map(
        shards,
        mesh=mesh,
        in_specs=(
            P("cache", None), P("cache", None), P("cache", "psg", None), P("cache", "psg"),
            P("cache", "psg"), P("cache", None, "psg"), P("cache", "psg"), P(),
            P(None, None, "psg"), P("psg", None), P("psg", None), P(), P(None, None, "psg"), P(),
            P(None, "psg"), P("psg", None),
        ),
        out_specs=(P("cache", "psg", None, None), P("cache", None, "psg")),
        check_vma=False,
    )
```

```python
import functools

import jax
import jax.numpy as jnp
import numpy as np
from jax import lax
from jax.experimental import pallas as pl
from jax.experimental.pallas import tpu as pltpu
from jax.sharding import PartitionSpec as P

HEAD = 64
EPSILON = 1e-06
F32 = jnp.float32
BF16 = jnp.bfloat16


def bucket_table(length, bucket_count):
    positions = np.arange(length)
    relative = positions[None, :] - positions[:, None]
    halfway = bucket_count // 2
    exact_span = halfway // 2
    upper_side = (relative > 0).astype(np.int64) * halfway
    distance = np.abs(relative)
    log_bucket = exact_span + (
        np.log(np.maximum(distance, 1) / exact_span)
        / np.log(128.0 / exact_span)
        * (halfway - exact_span)
    ).astype(np.int64)
    log_bucket = np.minimum(log_bucket, halfway - 1)
    return upper_side + np.where(distance < exact_span, distance, log_bucket)


def position_bias(bias_table, length):
    bucket_count = bias_table.shape[1]
    buckets = bucket_table(length, bucket_count).reshape(-1)
    onehot = (buckets[None, :] == np.arange(bucket_count)[:, None]).astype(np.float32)
    spread = jnp.dot(
        bias_table, jnp.asarray(onehot, dtype=bias_table.dtype), precision=lax.Precision.HIGHEST
    )
    return spread.reshape(bias_table.shape[0], length, length)


def dot32(a, b, dims):
    return lax.dot_general(a, b, (dims, ((), ())), preferred_element_type=F32)


MESH = pl.DeviceIdType.MESH
VM = pl.BlockSpec(memory_space=pltpu.VMEM)
SM = pl.BlockSpec(memory_space=pltpu.SMEM)
ANY = pl.BlockSpec(memory_space=pl.ANY)


def params(collective_id, mib):
    return pltpu.CompilerParams(
        collective_id=collective_id, has_side_effects=True, vmem_limit_bytes=mib << 20
    )


class Place:
    def __init__(self):
        self.c = lax.axis_index("cache")
        self.z = lax.axis_index("psg")
        self.core = lax.rem(self.c, 2)
        self.x = lax.rem(lax.div(self.c, 2), 4)
        self.y = lax.div(self.c, 8)

    def cache(self, c):
        return {"cache": c, "psg": self.z}

    def chip(self, y, x):
        return self.cache((y * 4 + x) * 2 + self.core)

    def sibling(self):
        return self.cache(self.c + 1 - 2 * self.core)

    def up(self, z):
        return {"cache": self.c, "psg": z}


def turn(p, k):
    return lax.rem(p + k + 4, 4)


def greet_all(at):
    barrier = pltpu.get_barrier_semaphore()

    def greet(d, carry):
        pl.semaphore_signal(
            barrier, inc=1, device_id=at.cache(lax.rem(at.c + d, 32)), device_id_type=MESH
        )
        return carry

    lax.fori_loop(1, 32, greet, 0)
    for k in range(1, 4):
        pl.semaphore_signal(barrier, inc=1, device_id=at.up(turn(at.z, k)), device_id_type=MESH)
    pl.semaphore_wait(barrier, 34)


class Mover:
    def __init__(self, send, recv):
        self.send, self.recv, self.count, self.started = send, recv, 0, []

    def go(self, src, dst, device):
        i = self.count
        self.count += 1
        copy = pltpu.make_async_remote_copy(
            src_ref=src, dst_ref=dst, send_sem=self.send.at[i], recv_sem=self.recv.at[i],
            device_id=device, device_id_type=MESH,
        )
        copy.start()
        self.started.append(copy)
        return copy

    def finish_sends(self):
        for copy in self.started:
            copy.wait_send()


class Ring:
    def __init__(self, mover, pos, device, own, dst, units, start=True):
        self.mover, self.pos, self.device, self.own, self.dst = mover, pos, device, own, dst
        self.right, self.left = device(turn(pos, 1)), device(turn(pos, -1))
        self.to_right, self.to_left, self.far = {}, {}, {}
        half = len(units) // 2
        self.first, self.last = units[:half], units[half:]
        if start:
            for u, v in zip(units, self.last + self.first):
                self.begin_right(u)
                self.begin_left(v)

    def begin_right(self, u):
        self.to_right[u] = self.mover.go(self.own(u), self.dst(self.pos, u, 1), self.right)

    def begin_left(self, u):
        self.to_left[u] = self.mover.go(self.own(u), self.dst(self.pos, u, -1), self.left)

    def pass_right(self, u):
        self.to_right[u].wait_recv()
        before = turn(self.pos, -1)
        self.far[u] = self.mover.go(self.dst(before, u, 1), self.dst(before, u, 2), self.right)

    def pass_left(self, u):
        self.to_left[u].wait_recv()
        after = turn(self.pos, 1)
        self.far[u] = self.mover.go(self.dst(after, u, -1), self.dst(after, u, 2), self.left)

    def onward(self):
        for u, v in zip(self.first, self.last):
            self.pass_right(u)
            self.pass_left(v)

    def near(self):
        for u in self.last:
            self.to_right[u].wait_recv()
        for v in self.first:
            self.to_left[v].wait_recv()

    def end(self):
        for copy in self.far.values():
            copy.wait_recv()


class Spread:
    def __init__(self, at, mover, full, width):
        self.at, self.mover, self.full = at, mover, full
        self.quarter, self.width = width // 4, width

    def begin(self, live_out, first):
        at = self.at
        rows = pl.ds(pl.multiple_of(at.c * 16, 16), 16)
        self.start = [
            self.mover.go(
                live_out.at[rows, pl.ds(first, self.width)],
                self.full.at[k - 1, at.y, at.x, at.core],
                at.up(turn(at.z, -k)),
            )
            for k in range(1, 4)
        ]

    def cols(self, u, n=1):
        return pl.ds(u * self.quarter, n * self.quarter)

    def phase_one(self):
        at, full = self.at, self.full
        for copy in self.start:
            copy.wait_recv()
        a = lambda pos, u, k=0: full.at[:, at.y, pos, at.core, :, self.cols(u)]
        b = lambda pos, u, k=0: full.at[:, pos, at.x, at.core, :, self.cols(u)]
        self.one = [
            Ring(self.mover, at.x, lambda p: at.chip(at.y, p), lambda u: a(at.x, u), a, [0, 1]),
            Ring(self.mover, at.y, lambda p: at.chip(p, at.x), lambda u: b(at.y, u), b, [2, 3]),
        ]

    def phase_one_onward(self):
        for ring in self.one:
            ring.onward()

    def phase_one_end(self):
        for ring in self.one:
            ring.near()
            ring.end()

    def line(self, full, axis):
        at = self.at
        if axis == "x":
            return full.at[:, at.y, :, at.core, :, self.cols(0, 2)]
        return full.at[:, :, at.x, at.core, :, self.cols(2, 2)]

    def phase_two(self):
        at, full = self.at, self.full
        a = lambda pos, u, k=0: full.at[:, pos, :, at.core, :, self.cols(u)]
        b = lambda pos, u, k=0: full.at[:, :, pos, at.core, :, self.cols(u)]
        self.two = [
            Ring(self.mover, at.y, lambda p: at.chip(p, at.x), lambda u: a(at.y, u), a, [0, 1]),
            Ring(self.mover, at.x, lambda p: at.chip(at.y, p), lambda u: b(at.x, u), b, [2, 3]),
        ]
        self.over = []
        self.cross(0)

    def cross(self, k):
        at, full = self.at, self.full
        a = full.at[:, turn(at.y, k), :, at.core, :, self.cols(0, 2)]
        b = full.at[:, :, turn(at.x, k), at.core, :, self.cols(2, 2)]
        for view in (a, b):
            self.over.append(self.mover.go(view, view, at.sibling()))

    def phase_two_onward(self):
        for ring in self.two:
            ring.onward()
        for ring in self.two:
            ring.near()
        self.cross(1)
        self.cross(-1)

    def finish(self):
        for ring in self.two:
            ring.end()
        self.cross(2)
        for copy in self.over:
            copy.wait_recv()


def norm_rows(rows, gain):
    wide = rows.astype(F32)
    inverse = lax.rsqrt(jnp.mean(wide * wide, axis=-1, keepdims=True) + EPSILON)
    return (wide * gain).astype(BF16), inverse


def fetch_kernel(
    ints, position, memory, embedding, score, live_out, w_qkv, cross_kv, cross_query,
    live_gain, enc_gain, dec_gain,
    x_out, tokens, scores, full, full_next, proj_mem, proj_q, qg, w_val_out, bias,
    every, table, turned, plan, tok, table_w, out_buf, in_buf0, in_buf1, in_buf2, in_buf3, own, pair_buf, a_buf, b_buf, a2_buf, b2_buf, tok_sum,
    x_full, weights, acc, squares, scaled, w_query, kv_buf, w_key, w_val,
    send, recv, a2a_send, a2a_recv, line_send, line_recv, local_sem, kv_sem, out_sem,
):
    at = Place()
    every[at.c, at.z] = ints[...]
    table[32:128] = jnp.zeros((96, 128), jnp.int32)
    load_table = pltpu.make_async_copy(embedding, table_w, local_sem.at[5])
    load_table.start()
    load_weights = [
        pltpu.make_async_copy(w_qkv.at[i], weights.at[i], local_sem.at[i]) for i in range(3)
    ] + [pltpu.make_async_copy(cross_query, w_query, local_sem.at[3])]
    for copy in load_weights:
        copy.start()

    def kv_copy(i):
        slot = lax.rem(i, 2)
        return pltpu.make_async_copy(
            cross_kv.at[pl.ds(i * 256, 256)], kv_buf.at[slot], kv_sem.at[slot]
        )

    kv_copy(0).start()

    def split_kv(first, last):
        def one(i, carry):
            @pl.when(i < 15)
            def _():
                kv_copy(i + 1).start()

            kv_copy(i).wait()
            rows = pl.ds(pl.multiple_of(i * 256, 256), 256)
            slot = lax.rem(i, 2)
            w_key[rows] = kv_buf[slot, :, 0, :]
            gain = jnp.transpose(jnp.broadcast_to(enc_gain[:, rows], (128, 256)))[:, 0:1]
            w_val[rows] = (kv_buf[slot, :, 1, :].astype(F32) * gain).astype(BF16)
            return carry

        lax.fori_loop(first, last, one, 0)

    greet_all(at)
    mover = Mover(send, recv)
    in_buf = (in_buf0, in_buf1, in_buf2, in_buf3)

    near = [
        mover.go(every.at[at.c, at.z], every.at[at.c, at.z], at.up(turn(at.z, k)))
        for k in range(1, 4)
    ]

    def line_copy(d):
        return pltpu.make_async_remote_copy(
            src_ref=every.at[at.c], dst_ref=every.at[at.c], send_sem=line_send.at[d],
            recv_sem=line_recv.at[d], device_id=at.cache(lax.rem(at.c + d, 32)),
            device_id_type=MESH,
        )

    def send_line(d, carry):
        line_copy(d).start()
        return carry

    def wait_line(d, carry):
        line_copy(d).wait()
        return carry

    for copy in near:
        copy.wait_recv()
    lax.fori_loop(1, 32, send_line, 0)
    spread = Spread(at, mover, full, 2048)
    spread.begin(live_out, 0)
    spread_next = Spread(at, mover, full_next, 2048)
    spread_next.begin(live_out, 2048)
    lax.fori_loop(1, 32, wait_line, 0)
    for q in range(32):
        table[q : q + 1] = (every[q, 0] + every[q, 1]) + (every[q, 2] + every[q, 3])

    names = table[0:32]
    turned[...] = jnp.transpose(table[...].astype(F32))
    lane = lax.broadcasted_iota(jnp.int32, (32, 128), 1)
    rank = jnp.zeros((32, 128), jnp.int32)
    for shift in range(1, 32):
        same = jnp.logical_and(pltpu.roll(names, shift, 1) == names, lane >= shift)
        rank = rank + jnp.where(same, 1, 0)
    entries = pltpu.roll(names, 96, 1)
    found = []
    for r in range(2):
        hit = jnp.logical_and(jnp.logical_and(names == at.c, rank == r), lane < 32)
        entry = jnp.where(hit, entries, 0)
        for shift in (64, 32, 16, 8, 4, 2, 1):
            entry = entry + pltpu.roll(entry, shift, 1)
        found.append(entry)
    asks = jnp.where(lane == 32, found[0], found[1])
    table[0:32] = jnp.where(lane < 32, names * 2 + rank, asks)
    to_plan = pltpu.make_async_copy(table.at[pl.ds(0, 32)], plan, local_sem.at[6])
    to_plan.start()
    to_plan.wait()

    def passage_copy(h, d):
        q = lax.rem(at.c + d, 32)
        return pltpu.make_async_remote_copy(
            src_ref=out_buf.at[h, pl.ds(2 * q, 2)], dst_ref=in_buf[h].at[pl.ds(2 * at.c, 2)],
            send_sem=a2a_send.at[h, d], recv_sem=a2a_recv.at[h, d],
            device_id=at.cache(q), device_id_type=MESH,
        )

    def send_part(h):
        lanes = pl.ds(h * 256, 256)

        def one(d, carry):
            q = lax.rem(at.c + d, 32)
            out_buf[h, 2 * q] = memory[plan[q, 32], :, lanes]
            out_buf[h, 2 * q + 1] = memory[plan[q, 33], :, lanes]
            passage_copy(h, d).start()
            return carry

        lax.fori_loop(1, 32, one, 0)
        in_buf[h][2 * at.c] = memory[plan[at.c, 32], :, lanes]
        in_buf[h][2 * at.c + 1] = memory[plan[at.c, 33], :, lanes]

    def wait_part(h):
        def one(d, carry):
            passage_copy(h, d).wait_recv()
            return carry

        lax.fori_loop(1, 32, one, 0)

        def pack(j, carry):
            own[h, pl.ds(pl.multiple_of(16 * j, 16), 16)] = in_buf[h][plan[at.c, j]]
            return carry

        lax.fori_loop(0, 32, pack, 0)

    def lanes_of(pos, h):
        return pl.ds(pl.multiple_of(pos * 1024 + h * 512, 512), 512)

    def part(pos, unit, k=0):
        h, g = unit
        return x_full.at[
            pl.ds(g * 256, 256), pl.ds(pl.multiple_of(pos * 1024 + h * 256, 256), 256)
        ]

    def ring_part(h):
        return Ring(
            mover, at.z, at.up, lambda u: own.at[u[0], pl.ds(u[1] * 256, 256)], part,
            [(h, 0), (h, 1)],
        )

    stored = []

    def multiply(k, h):
        pos = turn(at.z, k)
        lanes = lanes_of(pos, h)
        if k == 0:
            x_full[:, lanes] = jnp.concatenate([own[2 * h], own[2 * h + 1]], axis=1)
        keep = pltpu.make_async_copy(
            x_full.at[:, lanes], x_out.at[:, lanes], out_sem.at[len(stored)]
        )
        keep.start()
        first = not stored
        stored.append(keep)
        gain = live_gain[:, lanes]
        for r in range(2):
            rows = pl.ds(r * 256, 256)
            wide = x_full[rows, lanes].astype(F32)
            scaled[rows] = (wide * gain).astype(BF16)
            square = jnp.sum(wide * wide, axis=1, keepdims=True)
            squares[rows] = square if first else squares[rows] + square

        def one(i, carry):
            product = jnp.dot(scaled[...], weights[i, lanes], preferred_element_type=F32)
            acc[i] = product if first else acc[i] + product
            return carry

        lax.fori_loop(0, 3, one, 0)

    send_part(0)
    send_part(1)

    load_table.wait()
    held = lax.broadcasted_iota(jnp.int32, (48, 1004), 1).astype(F32) + (at.c * 1004).astype(F32)
    for b in range(8):
        picks = [
            jnp.where(held == turned[64:112, q : q + 1], 1.0, 0.0).astype(BF16)
            for q in range(4 * b, 4 * b + 4)
        ]
        named = jnp.dot(
            jnp.concatenate(picks, axis=0), table_w[...], preferred_element_type=F32
        ).astype(BF16)
        for n in range(4):
            q = 4 * b + n
            tok[q // 8, (q // 2) % 4, q % 2] = named[48 * n : 48 * (n + 1)]
    other = 1 - at.core
    pair = mover.go(tok.at[:, :, other], pair_buf, at.sibling())
    send_part(2)
    send_part(3)
    split_kv(0, 2)

    pair.wait_recv()

    def add_pair(y, carry):
        for x in range(4):
            pair_buf[y, x] = pair_buf[y, x] + tok[y, x, at.core]
        return carry

    lax.fori_loop(0, 4, add_pair, 0)
    lo, hi = pl.ds(0, 512), pl.ds(512, 512)
    tok_a = [
        mover.go(
            pair_buf.at[:, turn(at.x, k), :, lo], a_buf.at[k - 1], at.chip(at.y, turn(at.x, k))
        )
        for k in range(1, 4)
    ]
    tok_b = [
        mover.go(
            pair_buf.at[turn(at.y, k), :, :, hi], b_buf.at[k - 1], at.chip(turn(at.y, k), at.x)
        )
        for k in range(1, 4)
    ]
    near_scores = [
        mover.go(score, scores.at[at.z], at.up(turn(at.z, k))) for k in range(1, 4)
    ]
    scores[at.z] = score[...]
    split_kv(2, 4)
    wait_part(0)
    rings = [ring_part(0)]
    split_kv(4, 5)
    wait_part(1)
    rings.append(ring_part(1))
    for copy in load_weights:
        copy.wait()
    multiply(0, 0)
    for copy in tok_a + tok_b:
        copy.wait_recv()

    def add_line(i, carry):
        a_buf[0, i] = (a_buf[0, i] + a_buf[1, i]) + (a_buf[2, i] + pair_buf[i, at.x, :, lo])
        b_buf[0, i] = (b_buf[0, i] + b_buf[1, i]) + (b_buf[2, i] + pair_buf[at.y, i, :, hi])
        return carry

    lax.fori_loop(0, 4, add_line, 0)
    tok_a2 = [
        mover.go(a_buf.at[0, turn(at.y, k)], a2_buf.at[k - 1], at.chip(turn(at.y, k), at.x))
        for k in range(1, 4)
    ]
    tok_b2 = [
        mover.go(b_buf.at[0, turn(at.x, k)], b2_buf.at[k - 1], at.chip(at.y, turn(at.x, k)))
        for k in range(1, 4)
    ]
    wait_part(2)
    rings.append(ring_part(2))
    split_kv(5, 6)
    wait_part(3)
    rings.append(ring_part(3))
    for copy in tok_a2 + tok_b2:
        copy.wait_recv()
    tok_sum[:, lo] = (a2_buf[0] + a2_buf[1]) + (a2_buf[2] + a_buf[0, at.y])
    tok_sum[:, hi] = (b2_buf[0] + b2_buf[1]) + (b2_buf[2] + b_buf[0, at.x])
    mine = pl.ds(pl.multiple_of(at.z * 1024, 1024), 1024)
    near_tokens = [
        mover.go(tok_sum, tokens.at[:, mine], at.up(turn(at.z, k))) for k in range(1, 4)
    ]
    tokens[:, mine] = tok_sum[...]
    rings[0].onward()
    rings[1].onward()
    spread.phase_one()
    spread_next.phase_one()
    multiply(0, 1)
    split_kv(6, 8)
    rings[0].near()
    rings[1].near()
    multiply(1, 0)
    spread.phase_one_onward()
    multiply(-1, 0)
    split_kv(8, 10)
    rings[2].onward()
    spread.phase_one_end()
    spread.phase_two()
    spread_next.phase_one_onward()
    split_kv(10, 13)
    rings[3].onward()
    rings[0].end()
    rings[1].end()
    multiply(2, 0)
    spread.phase_two_onward()
    split_kv(13, 16)
    block = lax.broadcasted_iota(jnp.int32, (128, 128), 0) // 32
    block = block == lax.broadcasted_iota(jnp.int32, (128, 128), 1) // 32

    def spread_bias(h, carry):
        line = jnp.concatenate([position[h]] * 4, axis=1)
        bias[h] = jnp.where(block, jnp.concatenate([line] * 4, axis=0), -1e30)
        return carry

    lax.fori_loop(0, 8, spread_bias, 0)
    keep_values = pltpu.make_async_copy(w_val, w_val_out, local_sem.at[4])
    keep_values.start()
    for copy in near_scores + near_tokens:
        copy.wait_recv()

    rows, inverse = norm_rows(tokens[0:16], live_gain[...])

    def project(i, carry):
        total = jnp.dot(rows, weights[i], preferred_element_type=F32)
        proj_q[i] = (total * inverse).astype(BF16)
        return carry

    lax.fori_loop(0, 3, project, 0)
    rows_a, inverse_a = norm_rows(tokens[16:48], dec_gain[...])
    queries = jnp.dot(rows_a, w_query[...], preferred_element_type=F32) * inverse_a
    head = lax.broadcasted_iota(jnp.int32, (32, 512), 1) // HEAD
    for h in range(8):
        scaled[pl.ds(32 * h, 32)] = jnp.where(head == h, queries, 0.0).astype(BF16)

    def fold(n, carry):
        cols = pl.ds(pl.multiple_of(n * 1024, 1024), 1024)
        product = dot32(scaled[pl.ds(0, 256)], w_key[cols], ((1,), (1,)))
        qg[:, cols] = (product * enc_gain[:, cols]).astype(BF16)
        return carry

    lax.fori_loop(0, 4, fold, 0)
    rings[2].near()
    rings[3].near()
    multiply(1, 1)
    multiply(-1, 1)
    rings[2].end()
    rings[3].end()
    multiply(2, 1)
    inverse_m = lax.rsqrt(squares[...] * (1.0 / 4096) + EPSILON)

    def close(i, carry):
        proj_mem[i] = (acc[i] * inverse_m).astype(BF16)
        return carry

    lax.fori_loop(0, 3, close, 0)
    spread.finish()
    spread_next.phase_one_end()
    for copy in stored:
        copy.wait()
    keep_values.wait()
    mover.finish_sends()

    def sent(d, carry):
        for h in range(4):
            passage_copy(h, d).wait_send()
        return carry

    lax.fori_loop(1, 32, sent, 0)


def fetch(*args):
    return pl.pallas_call(
        fetch_kernel,
        out_shape=(
            jax.ShapeDtypeStruct((512, 4096), BF16),
            jax.ShapeDtypeStruct((48, 4096), BF16),
            jax.ShapeDtypeStruct((4, 1, 128), F32),
            jax.ShapeDtypeStruct((3, 4, 4, 2, 16, 2048), BF16),
            jax.ShapeDtypeStruct((3, 4, 4, 2, 16, 2048), BF16),
            jax.ShapeDtypeStruct((3, 512, 512), BF16),
            jax.ShapeDtypeStruct((3, 16, 512), BF16),
            jax.ShapeDtypeStruct((256, 4096), BF16),
            jax.ShapeDtypeStruct((4096, 512), BF16),
            jax.ShapeDtypeStruct((8, 128, 128), F32),
        ),
        in_specs=[VM, VM, VM, ANY, VM, ANY, ANY, ANY, ANY, VM, VM, VM],
        out_specs=(ANY, VM, VM, ANY, ANY, VM, VM, VM, ANY, VM),
        scratch_shapes=[
            pltpu.VMEM((32, 4, 1, 128), jnp.int32), pltpu.VMEM((128, 128), jnp.int32),
            pltpu.VMEM((128, 128), F32), pltpu.SMEM((32, 128), jnp.int32),
            pltpu.VMEM((4, 4, 2, 48, 1024), BF16), pltpu.VMEM((1004, 1024), BF16),
            pltpu.VMEM((4, 64, 16, 256), BF16), pltpu.VMEM((64, 16, 256), BF16),
            pltpu.VMEM((64, 16, 256), BF16), pltpu.VMEM((64, 16, 256), BF16),
            pltpu.VMEM((64, 16, 256), BF16),
            pltpu.VMEM((4, 512, 256), BF16), pltpu.VMEM((4, 4, 48, 1024), BF16),
            pltpu.VMEM((3, 4, 48, 512), BF16), pltpu.VMEM((3, 4, 48, 512), BF16),
            pltpu.VMEM((3, 48, 512), BF16), pltpu.VMEM((3, 48, 512), BF16),
            pltpu.VMEM((48, 1024), BF16),
            pltpu.VMEM((512, 4096), BF16), pltpu.VMEM((3, 4096, 512), BF16),
            pltpu.VMEM((3, 512, 512), F32), pltpu.VMEM((512, 1), F32),
            pltpu.VMEM((512, 512), BF16), pltpu.VMEM((4096, 512), BF16),
            pltpu.VMEM((2, 256, 2, 512), BF16), pltpu.VMEM((4096, 512), BF16),
            pltpu.VMEM((4096, 512), BF16),
            pltpu.SemaphoreType.DMA((112,)), pltpu.SemaphoreType.DMA((112,)),
            pltpu.SemaphoreType.DMA((4, 32)), pltpu.SemaphoreType.DMA((4, 32)),
            pltpu.SemaphoreType.DMA((32,)), pltpu.SemaphoreType.DMA((32,)),
            pltpu.SemaphoreType.DMA((7,)), pltpu.SemaphoreType.DMA((2,)),
            pltpu.SemaphoreType.DMA((8,)),
        ],
        compiler_params=params(2, 60),
    )(*args)


def reader_kernel(
    proj_mem, proj_q, bias, x_mem, tokens, qg, scores, left_in, right_in, live_out, w_val_in,
    cross_out_in,
    encoded, decoded,
    ctx, others, x_seq, left, right, own_out, w_val, w_out, ql, ql_part, lv, lv_part, s, w, values,
    inv, parts, part_buf, send, recv, local_sem,
):
    at = Place()
    mover = Mover(send, recv)
    spread = Spread(at, mover, right, 2048)
    loads = [
        pltpu.make_async_copy(a, b, local_sem.at[i])
        for i, (a, b) in enumerate([
            (spread.line(right_in, "x"), spread.line(right, "x")),
            (spread.line(right_in, "y"), spread.line(right, "y")),
            (x_mem, x_seq.at[:, pl.ds(0, 16)]), (live_out, own_out), (w_val_in, w_val),
            (left_in, left), (cross_out_in, w_out),
        ])
    ]
    for copy in loads:
        copy.start()
    greet_all(at)
    scale = HEAD ** (-0.5)
    nt = ((1,), (1,))
    loads[0].wait()
    loads[1].wait()
    spread.phase_two()

    def chunk(j):
        return pl.ds(pl.multiple_of(j * 256, 256), 256)

    def part(pos, u, k):
        return others.at[{1: 2, -1: 0, 2: 1}[k], chunk(turn(pos, u))]

    ring = Ring(
        mover, at.z, at.up, lambda u: ctx.at[chunk(turn(at.z, u))], part, [2, 1, 3, 0], False
    )

    low = lax.broadcasted_iota(jnp.int32, (128, 128), 1) < HEAD

    def attend(j):
        def group(g, carry):
            first = j * 8 + g * 4

            def pair(i, p):
                lanes = pl.ds(128 * p, 128)
                pieces = []
                for n in range(4):
                    pieces.append(
                        proj_mem[i, pl.ds(pl.multiple_of((first + n) * 16, 16), 16), lanes]
                    )
                    pieces.append(proj_q[i, :, lanes])
                return jnp.concatenate(pieces, axis=0)

            for p in range(4):
                q, k, v = pair(0, p), pair(1, p), pair(2, p)
                both = []
                for e in range(2):
                    keep = low if e == 0 else jnp.logical_not(low)
                    sc = dot32(jnp.where(keep, q, jnp.zeros_like(q)), k, nt) * scale
                    sc = sc + bias[2 * p + e]
                    ex = jnp.exp(sc - jnp.max(sc, axis=1, keepdims=True))
                    ex = (ex / jnp.sum(ex, axis=1, keepdims=True)).astype(BF16)
                    both.append(jnp.dot(ex, v, preferred_element_type=F32))
                ctx[pl.ds(pl.multiple_of(first * 32, 128), 128), pl.ds(128 * p, 128)] = jnp.where(
                    low, both[0], both[1]
                ).astype(BF16)
            return carry

        lax.fori_loop(0, 2, group, 0)

    for u in (2, 3, 1, 0):
        attend(turn(at.z, u))
        ring.begin_right(u)
        ring.begin_left(u)

    loads[2].wait()

    def fill(p, carry):
        x_seq[p, pl.ds(16, 16)] = tokens[pl.ds(0, 16)]
        return carry

    lax.fori_loop(0, 32, fill, 0)
    ring.pass_right(2)

    def rows_of(j):
        return x_seq[pl.ds(j * 8, 8)].reshape(256, 4096)

    def score_inputs(j, carry):
        s[j] = dot32(qg[...], rows_of(j), nt)
        return carry

    lax.fori_loop(0, 4, score_inputs, 0)
    ring.pass_left(3)
    spread.phase_two_onward()
    loads[4].wait()
    of_question = jnp.dot(tokens[pl.ds(0, 16)], w_val[...], preferred_element_type=F32)

    def value_inputs(j, carry):
        rows = jnp.dot(
            x_seq[pl.ds(j * 8, 8), pl.ds(0, 16)].reshape(128, 4096), w_val[...],
            preferred_element_type=F32,
        )
        for p in range(8):
            values[j, pl.ds(32 * p, 16)] = rows[16 * p : 16 * p + 16]
            values[j, pl.ds(32 * p + 16, 16)] = of_question
        return carry

    lax.fori_loop(0, 4, value_inputs, 0)
    ring.pass_right(1)
    loads[3].wait()
    ql[0] = dot32(qg[...], own_out[...], nt).astype(BF16)
    lv[0] = jnp.dot(own_out[...], w_val[...], preferred_element_type=F32).astype(BF16)

    def absorb(j, k, rows):
        s[j] = s[j] + dot32(ql[k], rows, nt)
        values[j] = values[j] + jnp.dot(rows, lv[k], preferred_element_type=F32)

    def absorb_own(j, carry):
        absorb(j, 0, ctx[chunk(j)])
        return carry

    lax.fori_loop(0, 4, absorb_own, 0)
    loads[5].wait()
    half, rest = pl.ds(0, 2048), pl.ds(2048, 2048)

    def fold_left(k, carry):
        ql_part[k] = dot32(qg[:, half], left[k], nt)
        lv_part[k] = jnp.dot(left[k], w_val[half], preferred_element_type=F32)
        return carry

    lax.fori_loop(0, 3, fold_left, 0)
    ring.pass_left(0)
    spread.finish()

    def fold_right(k, carry):
        rows = right[k].reshape(512, 2048)
        ql[k + 1] = (ql_part[k] + dot32(qg[:, rest], rows, nt)).astype(BF16)
        lv[k + 1] = (
            lv_part[k] + jnp.dot(rows, w_val[rest], preferred_element_type=F32)
        ).astype(BF16)
        return carry

    lax.fori_loop(0, 3, fold_right, 0)

    ring.far[2].wait_recv()
    mine = chunk(at.z)

    def group_rows(k, n):
        if k == 0:
            return own_out[:, pl.ds(n * 1024, 1024)]
        if n < 2:
            return left[k - 1, :, pl.ds(n * 1024, 1024)]
        return right[k - 1, :, :, :, :, pl.ds((n - 2) * 1024, 1024)].reshape(512, 1024)

    squares = jnp.zeros((256, 1), F32)
    for n in range(4):
        cols = pl.ds(n * 1024, 1024)
        attended = None
        for k in range(4):
            rows = ctx[mine] if k == 0 else others[k - 1, mine]
            product = jnp.dot(rows, group_rows(k, n), preferred_element_type=F32)
            product = product.astype(BF16).astype(F32)
            attended = product if k == 0 else attended + product
        own_rows = x_seq[pl.ds(at.z * 8, 8), :, cols].reshape(256, 1024).astype(F32)
        own_rows = (own_rows + attended).astype(BF16)
        encoded[:, cols] = own_rows
        own_rows = own_rows.astype(F32)
        squares = squares + jnp.sum(own_rows * own_rows, axis=1, keepdims=True)
    norm = lax.rsqrt(squares * (1.0 / 4096) + EPSILON)
    inv[at.z] = jnp.transpose(jnp.broadcast_to(norm, (256, 128)))[0:1]
    near = [mover.go(inv.at[at.z], inv.at[at.z], at.up(turn(at.z, k))) for k in range(1, 4)]

    def absorb_other(k, u):
        j = turn(at.z, k + u)
        absorb(j, k, others[k - 1, chunk(j)])

    absorb_other(3, 2)
    absorb_other(1, 3)
    absorb_other(3, 1)
    absorb_other(2, 2)
    ring.to_left[2].wait_recv()
    absorb_other(1, 2)
    ring.to_right[3].wait_recv()
    absorb_other(3, 3)
    ring.to_left[1].wait_recv()
    absorb_other(1, 1)
    absorb_other(1, 0)
    ring.far[3].wait_recv()
    absorb_other(2, 3)
    ring.to_right[0].wait_recv()
    absorb_other(3, 0)
    ring.far[1].wait_recv()
    absorb_other(2, 1)
    ring.far[0].wait_recv()
    absorb_other(2, 0)
    for copy in near:
        copy.wait_recv()

    passage = lax.broadcasted_iota(jnp.int32, (1, 256), 1) // 32
    top = None
    for j in range(4):
        row = jnp.zeros((1, 256), F32)
        line = scores[j]
        for p in range(8):
            row = row + jnp.where(passage == p, line[:, p : p + 1], 0.0)
        total = s[j] * (inv[j] * scale) + row
        s[j] = total
        here = jnp.max(total, axis=1, keepdims=True)
        top = here if top is None else jnp.maximum(top, here)
    sums = jnp.zeros((256, 1), F32)
    for j in range(4):
        ex = jnp.exp(s[j] - top)
        s[j] = ex
        sums = sums + jnp.sum(ex, axis=1, keepdims=True)
    for j in range(4):
        w[j] = (s[j] * inv[j] / sums).astype(BF16)
    heads_out = jnp.zeros((256, 512), F32)
    for j in range(4):
        heads_out = heads_out + jnp.dot(
            w[j], values[j].astype(BF16), preferred_element_type=F32
        )
    head = lax.broadcasted_iota(jnp.int32, (32, 512), 1) // HEAD
    context = jnp.zeros((32, 512), F32)
    for h in range(8):
        context = context + jnp.where(head == h, heads_out[32 * h : 32 * h + 32], 0.0)
    context = context.astype(BF16)
    loads[6].wait()
    for j in range(4):
        parts[j] = jnp.dot(
            context, w_out[:, pl.ds(1024 * j, 1024)], preferred_element_type=F32
        ).astype(BF16)
    last = [
        mover.go(parts.at[turn(at.z, k)], part_buf.at[k - 1], at.up(turn(at.z, k)))
        for k in range(1, 4)
    ]
    for copy in last:
        copy.wait_recv()
    total = parts[at.z].astype(F32)
    for k in range(3):
        total = total + part_buf[k].astype(F32)
    decoded[...] = total.astype(BF16)
    mover.finish_sends()


def reader(*args):
    return pl.pallas_call(
        reader_kernel,
        out_shape=(
            jax.ShapeDtypeStruct((256, 4096), BF16),
            jax.ShapeDtypeStruct((32, 1024), BF16),
        ),
        in_specs=[VM, VM, VM, ANY, VM, VM, VM, ANY, ANY, ANY, ANY, ANY],
        out_specs=(VM, VM),
        scratch_shapes=[
            pltpu.VMEM((1024, 512), BF16), pltpu.VMEM((3, 1024, 512), BF16),
            pltpu.VMEM((32, 32, 4096), BF16), pltpu.VMEM((3, 512, 2048), BF16),
            pltpu.VMEM((3, 4, 4, 2, 16, 2048), BF16), pltpu.VMEM((512, 4096), BF16),
            pltpu.VMEM((4096, 512), BF16), pltpu.VMEM((512, 4096), BF16),
            pltpu.VMEM((4, 256, 512), BF16), pltpu.VMEM((3, 256, 512), F32),
            pltpu.VMEM((4, 512, 512), BF16), pltpu.VMEM((3, 512, 512), F32),
            pltpu.VMEM((4, 256, 256), F32), pltpu.VMEM((4, 256, 256), BF16),
            pltpu.VMEM((4, 256, 512), F32), pltpu.VMEM((4, 1, 256), F32),
            pltpu.VMEM((4, 32, 1024), BF16), pltpu.VMEM((3, 32, 1024), BF16),
            pltpu.SemaphoreType.DMA((64,)), pltpu.SemaphoreType.DMA((64,)),
            pltpu.SemaphoreType.DMA((7,)),
        ],
        compiler_params=params(3, 60),
    )(*args)


def shards(
    question_ids, answer_ids, owner, slot, passage_score, memory, embedding, live_gain, live_qkv,
    rel_bias, live_out, enc_gain, cross_kv, dec_gain, cross_query, cross_out,
):
    n_psg = lax.axis_size("psg")
    width = live_gain.shape[0]
    plen = memory.shape[1]
    qlen = question_ids.shape[1]
    own_count = owner.shape[1]
    total = own_count * n_psg
    seq = plen + qlen
    cols = live_out.shape[0]

    lane = np.arange(128)
    part = jnp.where(lane < 64, lane % 32 // own_count, 0)
    ints = jnp.concatenate(
        [owner[0, :, 0]] * n_psg + [slot[0]] * n_psg
        + [question_ids[0], answer_ids[0], jnp.zeros((16,), jnp.int32)]
    )
    ints = jnp.where(part == lax.axis_index("psg"), ints, 0).reshape(1, 128)
    score = jnp.pad(passage_score, ((0, 0), (0, 120)))
    x_mem, token_full, scores, left, right, proj_mem, proj_q, qg, w_val, bias = fetch(
        ints, position_bias(rel_bias, seq), memory, embedding, score, live_out,
        jnp.transpose(live_qkv, (1, 0, 2)), cross_kv, cross_query,
        live_gain.reshape(1, width), enc_gain.reshape(1, width), dec_gain.reshape(1, width),
    )
    encoded, decoded = reader(
        proj_mem, proj_q, bias, x_mem.reshape(total, plen, width), token_full, qg, scores,
        left.reshape(3, cols, width // 2), right, live_out, w_val, cross_out,
    )
    return encoded.reshape(1, own_count, seq, width), decoded[None]


def solution(mesh):
    return jax.shard_map(
        shards,
        mesh=mesh,
        in_specs=(
            P("cache", None), P("cache", None), P("cache", "psg", None), P("cache", "psg"),
            P("cache", "psg"), P("cache", None, "psg"), P("cache", "psg"), P(),
            P(None, None, "psg"), P("psg", None), P("psg", None), P(), P(None, None, "psg"), P(),
            P(None, "psg"), P("psg", None),
        ),
        out_specs=(P("cache", "psg", None, None), P("cache", None, "psg")),
        check_vma=False,
    )
```

```python
import functools

import jax
import jax.numpy as jnp
import numpy as np
from jax import lax
from jax.experimental import pallas as pl
from jax.experimental.pallas import tpu as pltpu
from jax.sharding import PartitionSpec as P

HEAD = 64
EPSILON = 1e-06
F32 = jnp.float32
BF16 = jnp.bfloat16


def bucket_table(length, bucket_count):
    positions = np.arange(length)
    relative = positions[None, :] - positions[:, None]
    halfway = bucket_count // 2
    exact_span = halfway // 2
    upper_side = (relative > 0).astype(np.int64) * halfway
    distance = np.abs(relative)
    log_bucket = exact_span + (
        np.log(np.maximum(distance, 1) / exact_span)
        / np.log(128.0 / exact_span)
        * (halfway - exact_span)
    ).astype(np.int64)
    log_bucket = np.minimum(log_bucket, halfway - 1)
    return upper_side + np.where(distance < exact_span, distance, log_bucket)


def spread_table(length, bucket_count):
    buckets = np.tile(bucket_table(length, bucket_count).T, (1, 4)).reshape(-1)
    return (buckets[None, :] == np.arange(bucket_count)[:, None]).astype(np.float32)


def dot32(a, b, dims):
    return lax.dot_general(a, b, (dims, ((), ())), preferred_element_type=F32)


MESH = pl.DeviceIdType.MESH
VM = pl.BlockSpec(memory_space=pltpu.VMEM)
SM = pl.BlockSpec(memory_space=pltpu.SMEM)
ANY = pl.BlockSpec(memory_space=pl.ANY)


def params(collective_id, mib):
    return pltpu.CompilerParams(
        collective_id=collective_id, has_side_effects=True, vmem_limit_bytes=mib << 20
    )


class Place:
    def __init__(self):
        self.c = lax.axis_index("cache")
        self.z = lax.axis_index("psg")
        self.core = lax.rem(self.c, 2)
        self.x = lax.rem(lax.div(self.c, 2), 4)
        self.y = lax.div(self.c, 8)

    def cache(self, c):
        return {"cache": c, "psg": self.z}

    def chip(self, y, x):
        return self.cache((y * 4 + x) * 2 + self.core)

    def sibling(self):
        return self.cache(self.c + 1 - 2 * self.core)

    def up(self, z):
        return {"cache": self.c, "psg": z}


def turn(p, k):
    return lax.rem(p + k + 4, 4)


def greet_all(at):
    barrier = pltpu.get_barrier_semaphore()

    def greet(d, carry):
        pl.semaphore_signal(
            barrier, inc=1, device_id=at.cache(lax.rem(at.c + d, 32)), device_id_type=MESH
        )
        return carry

    lax.fori_loop(1, 32, greet, 0)
    for k in range(1, 4):
        pl.semaphore_signal(barrier, inc=1, device_id=at.up(turn(at.z, k)), device_id_type=MESH)
    pl.semaphore_wait(barrier, 34)


class Mover:
    def __init__(self, send, recv):
        self.send, self.recv, self.count, self.started = send, recv, 0, []

    def go(self, src, dst, device):
        i = self.count
        self.count += 1
        copy = pltpu.make_async_remote_copy(
            src_ref=src, dst_ref=dst, send_sem=self.send.at[i], recv_sem=self.recv.at[i],
            device_id=device, device_id_type=MESH,
        )
        copy.start()
        self.started.append(copy)
        return copy

    def finish_sends(self):
        for copy in self.started:
            copy.wait_send()


class Ring:
    def __init__(self, mover, pos, device, own, dst, units, start=True):
        self.mover, self.pos, self.device, self.own, self.dst = mover, pos, device, own, dst
        self.right, self.left = device(turn(pos, 1)), device(turn(pos, -1))
        self.to_right, self.to_left, self.far = {}, {}, {}
        half = len(units) // 2
        self.first, self.last = units[:half], units[half:]
        if start:
            for u, v in zip(units, self.last + self.first):
                self.begin_right(u)
                self.begin_left(v)

    def begin_right(self, u):
        self.to_right[u] = self.mover.go(self.own(u), self.dst(self.pos, u, 1), self.right)

    def begin_left(self, u):
        self.to_left[u] = self.mover.go(self.own(u), self.dst(self.pos, u, -1), self.left)

    def pass_right(self, u):
        self.to_right[u].wait_recv()
        before = turn(self.pos, -1)
        self.far[u] = self.mover.go(self.dst(before, u, 1), self.dst(before, u, 2), self.right)

    def pass_left(self, u):
        self.to_left[u].wait_recv()
        after = turn(self.pos, 1)
        self.far[u] = self.mover.go(self.dst(after, u, -1), self.dst(after, u, 2), self.left)

    def onward(self):
        for u, v in zip(self.first, self.last):
            self.pass_right(u)
            self.pass_left(v)

    def near(self):
        for u in self.last:
            self.to_right[u].wait_recv()
        for v in self.first:
            self.to_left[v].wait_recv()

    def end(self):
        for copy in self.far.values():
            copy.wait_recv()


class Spread:
    def __init__(self, at, mover, full, width):
        self.at, self.mover, self.full = at, mover, full
        self.quarter, self.width = width // 4, width

    def begin(self, live_out, first):
        at = self.at
        rows = pl.ds(pl.multiple_of(at.c * 16, 16), 16)
        self.start = [
            self.mover.go(
                live_out.at[rows, pl.ds(first, self.width)],
                self.full.at[k - 1, at.y, at.x, at.core],
                at.up(turn(at.z, -k)),
            )
            for k in range(1, 4)
        ]

    def cols(self, u, n=1):
        return pl.ds(u * self.quarter, n * self.quarter)

    def phase_one(self):
        at, full = self.at, self.full
        for copy in self.start:
            copy.wait_recv()
        a = lambda pos, u, k=0: full.at[:, at.y, pos, at.core, :, self.cols(u)]
        b = lambda pos, u, k=0: full.at[:, pos, at.x, at.core, :, self.cols(u)]
        self.one = [
            Ring(self.mover, at.x, lambda p: at.chip(at.y, p), lambda u: a(at.x, u), a, [0, 1]),
            Ring(self.mover, at.y, lambda p: at.chip(p, at.x), lambda u: b(at.y, u), b, [2, 3]),
        ]

    def phase_one_onward(self):
        for ring in self.one:
            ring.onward()

    def phase_one_end(self):
        for ring in self.one:
            ring.near()
            ring.end()

    def line(self, full, axis):
        at = self.at
        if axis == "x":
            return full.at[:, at.y, :, at.core, :, self.cols(0, 2)]
        return full.at[:, :, at.x, at.core, :, self.cols(2, 2)]

    def phase_two(self):
        at, full = self.at, self.full
        a = lambda pos, u, k=0: full.at[:, pos, :, at.core, :, self.cols(u)]
        b = lambda pos, u, k=0: full.at[:, :, pos, at.core, :, self.cols(u)]
        self.two = [
            Ring(self.mover, at.y, lambda p: at.chip(p, at.x), lambda u: a(at.y, u), a, [0, 1]),
            Ring(self.mover, at.x, lambda p: at.chip(at.y, p), lambda u: b(at.x, u), b, [2, 3]),
        ]
        self.over = []
        self.cross(0)

    def cross(self, k):
        at, full = self.at, self.full
        a = full.at[:, turn(at.y, k), :, at.core, :, self.cols(0, 2)]
        b = full.at[:, :, turn(at.x, k), at.core, :, self.cols(2, 2)]
        for view in (a, b):
            self.over.append(self.mover.go(view, view, at.sibling()))

    def phase_two_onward(self):
        for ring in self.two:
            ring.onward()
        for ring in self.two:
            ring.near()
        self.cross(1)
        self.cross(-1)

    def finish(self):
        for ring in self.two:
            ring.end()
        self.cross(2)
        for copy in self.over:
            copy.wait_recv()


def norm_rows(rows, gain):
    wide = rows.astype(F32)
    inverse = lax.rsqrt(jnp.mean(wide * wide, axis=-1, keepdims=True) + EPSILON)
    return (wide * gain).astype(BF16), inverse


def fetch_kernel(
    question_ids, answer_ids, owner, slot, rel_bias, spread_of, memory, embedding, own_score,
    live_out, w_qkv, cross_kv, cross_query,
    live_gain, enc_gain, dec_gain,
    x_out, tokens, scores, full, full_next, proj_mem, proj_q, qg, w_val_out, bias,
    line_buf, score, by_key, every, table, turned, plan, tok, table_w, out_buf, in_buf0, in_buf1, in_buf2, in_buf3, own, pair_buf, a_buf, b_buf, a2_buf, b2_buf, tok_sum,
    x_full, weights, acc, squares, scaled, w_query, kv_buf, w_key, w_val,
    send, recv, a2a_send, a2a_recv, line_send, line_recv, local_sem, kv_sem, out_sem,
):
    at = Place()
    line_buf[...] = jnp.zeros((8, 128), jnp.int32)
    line_buf[0:1, 0:8] = owner[...]
    line_buf[0:1, 32:40] = slot[...]
    line_buf[1:2, 64:80] = question_ids[...]
    line_buf[1:2, 80:112] = answer_ids[...]
    placed = pltpu.roll(line_buf[0:1], 8 * at.z, 1)
    every[at.c, at.z] = placed + jnp.where(at.z == 0, line_buf[1:2], 0)
    score[...] = jnp.zeros((1, 128), F32)
    score[:, 0:8] = own_score[...]
    table[32:128] = jnp.zeros((96, 128), jnp.int32)
    load_table = pltpu.make_async_copy(embedding, table_w, local_sem.at[5])
    load_table.start()
    load_weights = [
        pltpu.make_async_copy(w_qkv.at[i], weights.at[i], local_sem.at[i]) for i in range(3)
    ] + [pltpu.make_async_copy(cross_query, w_query, local_sem.at[3])]
    for copy in load_weights:
        copy.start()

    def kv_copy(i):
        slot = lax.rem(i, 4)
        return pltpu.make_async_copy(
            cross_kv.at[pl.ds(i * 256, 256)], kv_buf.at[slot], kv_sem.at[slot]
        )

    for i in range(3):
        kv_copy(i).start()

    def split_kv(first, last):
        def one(i, carry):
            @pl.when(i < 13)
            def _():
                kv_copy(i + 3).start()

            kv_copy(i).wait()
            rows = pl.ds(pl.multiple_of(i * 256, 256), 256)
            slot = lax.rem(i, 4)
            w_key[rows] = kv_buf[slot, :, 0, :]
            gain = jnp.transpose(jnp.broadcast_to(enc_gain[:, rows], (128, 256)))[:, 0:1]
            w_val[rows] = (kv_buf[slot, :, 1, :].astype(F32) * gain).astype(BF16)
            return carry

        lax.fori_loop(first, last, one, 0)

    greet_all(at)
    mover = Mover(send, recv)
    in_buf = (in_buf0, in_buf1, in_buf2, in_buf3)

    near = [
        mover.go(every.at[at.c, at.z], every.at[at.c, at.z], at.up(turn(at.z, k)))
        for k in range(1, 4)
    ]

    def line_copy(d):
        return pltpu.make_async_remote_copy(
            src_ref=every.at[at.c], dst_ref=every.at[at.c], send_sem=line_send.at[d],
            recv_sem=line_recv.at[d], device_id=at.cache(lax.rem(at.c + d, 32)),
            device_id_type=MESH,
        )

    def send_line(d, carry):
        line_copy(d).start()
        return carry

    def wait_line(d, carry):
        line_copy(d).wait()
        return carry

    for copy in near:
        copy.wait_recv()
    lax.fori_loop(1, 32, send_line, 0)
    spread = Spread(at, mover, full, 2048)
    spread.begin(live_out, 0)
    spread_next = Spread(at, mover, full_next, 2048)
    spread_next.begin(live_out, 2048)
    lax.fori_loop(1, 32, wait_line, 0)
    for q in range(32):
        table[q : q + 1] = (every[q, 0] + every[q, 1]) + (every[q, 2] + every[q, 3])

    names = table[0:32]
    turned[...] = jnp.transpose(table[...].astype(F32))
    lane = lax.broadcasted_iota(jnp.int32, (32, 128), 1)
    rank = jnp.zeros((32, 128), jnp.int32)
    for shift in range(1, 32):
        same = jnp.logical_and(pltpu.roll(names, shift, 1) == names, lane >= shift)
        rank = rank + jnp.where(same, 1, 0)
    entries = pltpu.roll(names, 96, 1)
    found = []
    for r in range(2):
        hit = jnp.logical_and(jnp.logical_and(names == at.c, rank == r), lane < 32)
        entry = jnp.where(hit, entries, 0)
        for shift in (64, 32, 16, 8, 4, 2, 1):
            entry = entry + pltpu.roll(entry, shift, 1)
        found.append(entry)
    asks = jnp.where(lane == 32, found[0], found[1])
    table[0:32] = jnp.where(lane < 32, names * 2 + rank, asks)
    to_plan = pltpu.make_async_copy(table.at[pl.ds(0, 32)], plan, local_sem.at[6])
    to_plan.start()
    to_plan.wait()

    def passage_copy(h, d):
        q = lax.rem(at.c + d, 32)
        return pltpu.make_async_remote_copy(
            src_ref=out_buf.at[h, pl.ds(2 * q, 2)], dst_ref=in_buf[h].at[pl.ds(2 * at.c, 2)],
            send_sem=a2a_send.at[h, d], recv_sem=a2a_recv.at[h, d],
            device_id=at.cache(q), device_id_type=MESH,
        )

    def send_part(h):
        lanes = pl.ds(h * 256, 256)

        def one(d, carry):
            q = lax.rem(at.c + d, 32)
            out_buf[h, 2 * q] = memory[plan[q, 32], :, lanes]
            out_buf[h, 2 * q + 1] = memory[plan[q, 33], :, lanes]
            passage_copy(h, d).start()
            return carry

        lax.fori_loop(1, 32, one, 0)
        in_buf[h][2 * at.c] = memory[plan[at.c, 32], :, lanes]
        in_buf[h][2 * at.c + 1] = memory[plan[at.c, 33], :, lanes]

    def wait_part(h):
        def one(d, carry):
            passage_copy(h, d).wait_recv()
            return carry

        lax.fori_loop(1, 32, one, 0)

        def pack(j, carry):
            own[h, pl.ds(pl.multiple_of(16 * j, 16), 16)] = in_buf[h][plan[at.c, j]]
            return carry

        lax.fori_loop(0, 32, pack, 0)

    def lanes_of(pos, h):
        return pl.ds(pl.multiple_of(pos * 1024 + h * 512, 512), 512)

    def part(pos, unit, k=0):
        h, g = unit
        return x_full.at[
            pl.ds(g * 256, 256), pl.ds(pl.multiple_of(pos * 1024 + h * 256, 256), 256)
        ]

    def ring_part(h):
        return Ring(
            mover, at.z, at.up, lambda u: own.at[u[0], pl.ds(u[1] * 256, 256)], part,
            [(h, 0), (h, 1)],
        )

    stored = []

    def multiply(k, h):
        pos = turn(at.z, k)
        lanes = lanes_of(pos, h)
        if k == 0:
            x_full[:, lanes] = jnp.concatenate([own[2 * h], own[2 * h + 1]], axis=1)
        keep = pltpu.make_async_copy(
            x_full.at[:, lanes], x_out.at[:, lanes], out_sem.at[len(stored)]
        )
        keep.start()
        first = not stored
        stored.append(keep)
        gain = live_gain[:, lanes]
        for r in range(2):
            rows = pl.ds(r * 256, 256)
            wide = x_full[rows, lanes].astype(F32)
            scaled[rows] = (wide * gain).astype(BF16)
            square = jnp.sum(wide * wide, axis=1, keepdims=True)
            squares[rows] = square if first else squares[rows] + square

        def one(i, carry):
            product = jnp.dot(scaled[...], weights[i, lanes], preferred_element_type=F32)
            acc[i] = product if first else acc[i] + product
            return carry

        lax.fori_loop(0, 3, one, 0)

    def sent_part(h):
        def one(d, carry):
            passage_copy(h, d).wait_send()
            return carry

        lax.fori_loop(1, 32, one, 0)

    send_part(0)

    load_table.wait()
    held = lax.broadcasted_iota(jnp.int32, (48, 1004), 1).astype(F32) + (at.c * 1004).astype(F32)
    for b in range(8):
        picks = [
            jnp.where(held == turned[64:112, q : q + 1], 1.0, 0.0).astype(BF16)
            for q in range(4 * b, 4 * b + 4)
        ]
        named = jnp.dot(
            jnp.concatenate(picks, axis=0), table_w[...], preferred_element_type=F32
        ).astype(BF16)
        for n in range(4):
            q = 4 * b + n
            tok[q // 8, (q // 2) % 4, q % 2] = named[48 * n : 48 * (n + 1)]
    other = 1 - at.core
    pair = mover.go(tok.at[:, :, other], pair_buf, at.sibling())
    split_kv(0, 3)
    sent_part(0)
    send_part(1)

    pair.wait_recv()

    def add_pair(y, carry):
        for x in range(4):
            pair_buf[y, x] = pair_buf[y, x] + tok[y, x, at.core]
        return carry

    lax.fori_loop(0, 4, add_pair, 0)
    wait_part(0)
    rings = [ring_part(0)]
    sent_part(1)
    send_part(2)
    lo, hi = pl.ds(0, 512), pl.ds(512, 512)
    tok_a = [
        mover.go(
            pair_buf.at[:, turn(at.x, k), :, lo], a_buf.at[k - 1], at.chip(at.y, turn(at.x, k))
        )
        for k in range(1, 4)
    ]
    tok_b = [
        mover.go(
            pair_buf.at[turn(at.y, k), :, :, hi], b_buf.at[k - 1], at.chip(turn(at.y, k), at.x)
        )
        for k in range(1, 4)
    ]
    near_scores = [
        mover.go(score, scores.at[at.z], at.up(turn(at.z, k))) for k in range(1, 4)
    ]
    scores[at.z] = score[...]
    wait_part(1)
    rings.append(ring_part(1))
    for copy in load_weights:
        copy.wait()
    multiply(0, 0)
    sent_part(2)
    send_part(3)
    split_kv(3, 6)
    for copy in tok_a + tok_b:
        copy.wait_recv()

    def add_line(i, carry):
        a_buf[0, i] = (a_buf[0, i] + a_buf[1, i]) + (a_buf[2, i] + pair_buf[i, at.x, :, lo])
        b_buf[0, i] = (b_buf[0, i] + b_buf[1, i]) + (b_buf[2, i] + pair_buf[at.y, i, :, hi])
        return carry

    lax.fori_loop(0, 4, add_line, 0)
    tok_a2 = [
        mover.go(a_buf.at[0, turn(at.y, k)], a2_buf.at[k - 1], at.chip(turn(at.y, k), at.x))
        for k in range(1, 4)
    ]
    tok_b2 = [
        mover.go(b_buf.at[0, turn(at.x, k)], b2_buf.at[k - 1], at.chip(at.y, turn(at.x, k)))
        for k in range(1, 4)
    ]
    wait_part(2)
    rings.append(ring_part(2))
    rings[0].onward()
    wait_part(3)
    rings.append(ring_part(3))
    for copy in tok_a2 + tok_b2:
        copy.wait_recv()
    tok_sum[:, lo] = (a2_buf[0] + a2_buf[1]) + (a2_buf[2] + a_buf[0, at.y])
    tok_sum[:, hi] = (b2_buf[0] + b2_buf[1]) + (b2_buf[2] + b_buf[0, at.x])
    mine = pl.ds(pl.multiple_of(at.z * 1024, 1024), 1024)
    near_tokens = [
        mover.go(tok_sum, tokens.at[:, mine], at.up(turn(at.z, k))) for k in range(1, 4)
    ]
    tokens[:, mine] = tok_sum[...]
    rings[1].onward()
    spread.phase_one()
    spread_next.phase_one()
    multiply(0, 1)
    split_kv(6, 8)
    rings[0].near()
    rings[1].near()
    multiply(1, 0)
    spread.phase_one_onward()
    multiply(-1, 0)
    split_kv(8, 10)
    rings[2].onward()
    spread.phase_one_end()
    spread.phase_two()
    spread_next.phase_one_onward()
    split_kv(10, 13)
    rings[3].onward()
    rings[0].end()
    rings[1].end()
    multiply(2, 0)
    spread.phase_two_onward()
    split_kv(13, 16)
    def spread_bias(b, carry):
        cols = pl.ds(pl.multiple_of(b * 128, 128), 128)
        by_key[b] = jnp.dot(
            rel_bias[...], spread_of[:, cols], precision=lax.Precision.HIGHEST,
            preferred_element_type=F32,
        )
        return carry

    lax.fori_loop(0, 32, spread_bias, 0)
    for h in range(8):
        bias[h] = by_key[:, h, :]
    keep_values = pltpu.make_async_copy(w_val, w_val_out, local_sem.at[4])
    keep_values.start()
    for copy in near_scores + near_tokens:
        copy.wait_recv()

    rows, inverse = norm_rows(tokens[0:16], live_gain[...])

    def project(i, carry):
        total = jnp.dot(rows, weights[i], preferred_element_type=F32)
        proj_q[i] = (total * inverse).astype(BF16)
        return carry

    lax.fori_loop(0, 3, project, 0)
    rows_a, inverse_a = norm_rows(tokens[16:48], dec_gain[...])
    queries = jnp.dot(rows_a, w_query[...], preferred_element_type=F32) * inverse_a
    head = lax.broadcasted_iota(jnp.int32, (32, 512), 1) // HEAD
    for h in range(8):
        scaled[pl.ds(32 * h, 32)] = jnp.where(head == h, queries, 0.0).astype(BF16)

    def fold(n, carry):
        cols = pl.ds(pl.multiple_of(n * 1024, 1024), 1024)
        product = dot32(scaled[pl.ds(0, 256)], w_key[cols], ((1,), (1,)))
        qg[:, cols] = (product * enc_gain[:, cols]).astype(BF16)
        return carry

    lax.fori_loop(0, 4, fold, 0)
    rings[2].near()
    rings[3].near()
    multiply(1, 1)
    multiply(-1, 1)
    rings[2].end()
    rings[3].end()
    multiply(2, 1)
    inverse_m = lax.rsqrt(squares[...] * (1.0 / 4096) + EPSILON)

    def close(i, carry):
        proj_mem[i] = (acc[i] * inverse_m).astype(BF16)
        return carry

    lax.fori_loop(0, 3, close, 0)
    spread.finish()
    spread_next.phase_one_end()
    for copy in stored:
        copy.wait()
    keep_values.wait()
    mover.finish_sends()

    sent_part(3)


def fetch(*args):
    return pl.pallas_call(
        fetch_kernel,
        out_shape=(
            jax.ShapeDtypeStruct((512, 4096), BF16),
            jax.ShapeDtypeStruct((48, 4096), BF16),
            jax.ShapeDtypeStruct((4, 1, 128), F32),
            jax.ShapeDtypeStruct((3, 4, 4, 2, 16, 2048), BF16),
            jax.ShapeDtypeStruct((3, 4, 4, 2, 16, 2048), BF16),
            jax.ShapeDtypeStruct((3, 512, 512), BF16),
            jax.ShapeDtypeStruct((3, 16, 512), BF16),
            jax.ShapeDtypeStruct((256, 4096), BF16),
            jax.ShapeDtypeStruct((4096, 512), BF16),
            jax.ShapeDtypeStruct((8, 32, 128), F32),
        ),
        in_specs=[VM] * 7 + [ANY, VM, ANY, ANY, ANY, ANY, VM, VM, VM],
        out_specs=(ANY, VM, VM, ANY, ANY, VM, VM, VM, ANY, VM),
        scratch_shapes=[
            pltpu.VMEM((8, 128), jnp.int32), pltpu.VMEM((1, 128), F32),
            pltpu.VMEM((32, 8, 128), F32),
            pltpu.VMEM((32, 4, 1, 128), jnp.int32), pltpu.VMEM((128, 128), jnp.int32),
            pltpu.VMEM((128, 128), F32), pltpu.SMEM((32, 128), jnp.int32),
            pltpu.VMEM((4, 4, 2, 48, 1024), BF16), pltpu.VMEM((1004, 1024), BF16),
            pltpu.VMEM((4, 64, 16, 256), BF16), pltpu.VMEM((64, 16, 256), BF16),
            pltpu.VMEM((64, 16, 256), BF16), pltpu.VMEM((64, 16, 256), BF16),
            pltpu.VMEM((64, 16, 256), BF16),
            pltpu.VMEM((4, 512, 256), BF16), pltpu.VMEM((4, 4, 48, 1024), BF16),
            pltpu.VMEM((3, 4, 48, 512), BF16), pltpu.VMEM((3, 4, 48, 512), BF16),
            pltpu.VMEM((3, 48, 512), BF16), pltpu.VMEM((3, 48, 512), BF16),
            pltpu.VMEM((48, 1024), BF16),
            pltpu.VMEM((512, 4096), BF16), pltpu.VMEM((3, 4096, 512), BF16),
            pltpu.VMEM((3, 512, 512), F32), pltpu.VMEM((512, 1), F32),
            pltpu.VMEM((512, 512), BF16), pltpu.VMEM((4096, 512), BF16),
            pltpu.VMEM((4, 256, 2, 512), BF16), pltpu.VMEM((4096, 512), BF16),
            pltpu.VMEM((4096, 512), BF16),
            pltpu.SemaphoreType.DMA((112,)), pltpu.SemaphoreType.DMA((112,)),
            pltpu.SemaphoreType.DMA((4, 32)), pltpu.SemaphoreType.DMA((4, 32)),
            pltpu.SemaphoreType.DMA((32,)), pltpu.SemaphoreType.DMA((32,)),
            pltpu.SemaphoreType.DMA((7,)), pltpu.SemaphoreType.DMA((4,)),
            pltpu.SemaphoreType.DMA((8,)),
        ],
        compiler_params=params(2, 60),
    )(*args)


def reader_kernel(
    proj_mem, proj_q, bias, x_mem, tokens, qg, scores, left_in, right_in, live_out, w_val_in,
    cross_out_in,
    encoded, decoded,
    ctx, others, x_seq, left, right, own_out, w_val, w_out, ql, ql_part, lv, lv_part, s, w, values,
    inv, parts, part_buf, send, recv, local_sem,
):
    at = Place()
    mover = Mover(send, recv)
    spread = Spread(at, mover, right, 2048)
    loads = [
        pltpu.make_async_copy(a, b, local_sem.at[i])
        for i, (a, b) in enumerate([
            (spread.line(right_in, "x"), spread.line(right, "x")),
            (spread.line(right_in, "y"), spread.line(right, "y")),
            (x_mem, x_seq.at[:, pl.ds(0, 16)]), (live_out, own_out), (w_val_in, w_val),
            (left_in, left), (cross_out_in, w_out),
        ])
    ]
    for copy in loads:
        copy.start()
    greet_all(at)
    scale = HEAD ** (-0.5)
    nt = ((1,), (1,))
    loads[0].wait()
    loads[1].wait()
    spread.phase_two()

    def chunk(j):
        return pl.ds(pl.multiple_of(j * 256, 256), 256)

    def part(pos, u, k):
        return others.at[{1: 2, -1: 0, 2: 1}[k], chunk(turn(pos, u))]

    ring = Ring(
        mover, at.z, at.up, lambda u: ctx.at[chunk(turn(at.z, u))], part, [2, 1, 3, 0], False
    )

    low = lax.broadcasted_iota(jnp.int32, (128, 128), 1) < HEAD
    eye = lax.broadcasted_iota(jnp.int32, (128, 128), 0)
    eye = eye == lax.broadcasted_iota(jnp.int32, (128, 128), 1)
    eye = jnp.where(eye, 1.0, 0.0).astype(BF16)
    owner_lane = lax.broadcasted_iota(jnp.int32, (32, 128), 1) // 32

    def attend(j):
        def group(g, carry):
            first = j * 8 + g * 4

            def pair(i, p):
                lanes = pl.ds(128 * p, 128)
                pieces = []
                for n in range(4):
                    pieces.append(
                        proj_mem[i, pl.ds(pl.multiple_of((first + n) * 16, 16), 16), lanes]
                    )
                    pieces.append(proj_q[i, :, lanes])
                return jnp.concatenate(pieces, axis=0)

            for p in range(4):
                q, k, v = pair(0, p), pair(1, p), pair(2, p)
                both = []
                for e in range(2):
                    keep = low if e == 0 else jnp.logical_not(low)
                    full = dot32(k, jnp.where(keep, q, jnp.zeros_like(q)), nt)
                    sc = full[0:32]
                    for n in range(1, 4):
                        sc = jnp.where(owner_lane == n, full[32 * n : 32 * n + 32], sc)
                    sc = sc * scale + bias[2 * p + e]
                    ex = jnp.exp(sc - jnp.max(sc, axis=0, keepdims=True))
                    ex = ex * (1.0 / jnp.sum(ex, axis=0, keepdims=True))
                    full = jnp.concatenate(
                        [jnp.where(owner_lane == n, ex, 0.0) for n in range(4)], axis=0
                    ).astype(BF16)
                    by_query = dot32(eye, full, nt).astype(BF16)
                    both.append(jnp.dot(by_query, v, preferred_element_type=F32))
                ctx[pl.ds(pl.multiple_of(first * 32, 128), 128), pl.ds(128 * p, 128)] = jnp.where(
                    low, both[0], both[1]
                ).astype(BF16)
            return carry

        lax.fori_loop(0, 2, group, 0)

    for u in (2, 3, 1, 0):
        attend(turn(at.z, u))
        ring.begin_right(u)
        ring.begin_left(u)

    loads[2].wait()

    def fill(p, carry):
        x_seq[p, pl.ds(16, 16)] = tokens[pl.ds(0, 16)]
        return carry

    lax.fori_loop(0, 32, fill, 0)
    ring.pass_right(2)

    def rows_of(j):
        return x_seq[pl.ds(j * 8, 8)].reshape(256, 4096)

    def score_inputs(j, carry):
        s[j] = dot32(qg[...], rows_of(j), nt)
        return carry

    lax.fori_loop(0, 4, score_inputs, 0)
    ring.pass_left(3)
    spread.phase_two_onward()
    loads[4].wait()
    of_question = jnp.dot(tokens[pl.ds(0, 16)], w_val[...], preferred_element_type=F32)

    def value_inputs(j, carry):
        rows = jnp.dot(
            x_seq[pl.ds(j * 8, 8), pl.ds(0, 16)].reshape(128, 4096), w_val[...],
            preferred_element_type=F32,
        )
        for p in range(8):
            values[j, pl.ds(32 * p, 16)] = rows[16 * p : 16 * p + 16]
            values[j, pl.ds(32 * p + 16, 16)] = of_question
        return carry

    lax.fori_loop(0, 4, value_inputs, 0)
    ring.pass_right(1)
    loads[3].wait()
    ql[0] = dot32(qg[...], own_out[...], nt).astype(BF16)
    lv[0] = jnp.dot(own_out[...], w_val[...], preferred_element_type=F32).astype(BF16)

    def absorb(j, k, rows):
        s[j] = s[j] + dot32(ql[k], rows, nt)
        values[j] = values[j] + jnp.dot(rows, lv[k], preferred_element_type=F32)

    def absorb_own(j, carry):
        absorb(j, 0, ctx[chunk(j)])
        return carry

    lax.fori_loop(0, 4, absorb_own, 0)
    loads[5].wait()
    half, rest = pl.ds(0, 2048), pl.ds(2048, 2048)

    def fold_left(k, carry):
        ql_part[k] = dot32(qg[:, half], left[k], nt)
        lv_part[k] = jnp.dot(left[k], w_val[half], preferred_element_type=F32)
        return carry

    lax.fori_loop(0, 3, fold_left, 0)
    ring.pass_left(0)
    spread.finish()

    def fold_right(k, carry):
        rows = right[k].reshape(512, 2048)
        ql[k + 1] = (ql_part[k] + dot32(qg[:, rest], rows, nt)).astype(BF16)
        lv[k + 1] = (
            lv_part[k] + jnp.dot(rows, w_val[rest], preferred_element_type=F32)
        ).astype(BF16)
        return carry

    lax.fori_loop(0, 3, fold_right, 0)

    ring.far[2].wait_recv()
    mine = chunk(at.z)

    def group_rows(k, n):
        if k == 0:
            return own_out[:, pl.ds(n * 1024, 1024)]
        if n < 2:
            return left[k - 1, :, pl.ds(n * 1024, 1024)]
        return right[k - 1, :, :, :, :, pl.ds((n - 2) * 1024, 1024)].reshape(512, 1024)

    squares = jnp.zeros((256, 1), F32)
    for n in range(4):
        cols = pl.ds(n * 1024, 1024)
        attended = None
        for k in range(4):
            rows = ctx[mine] if k == 0 else others[k - 1, mine]
            product = jnp.dot(rows, group_rows(k, n), preferred_element_type=F32)
            product = product.astype(BF16).astype(F32)
            attended = product if k == 0 else attended + product
        own_rows = x_seq[pl.ds(at.z * 8, 8), :, cols].reshape(256, 1024).astype(F32)
        own_rows = (own_rows + attended).astype(BF16)
        encoded[:, cols] = own_rows
        own_rows = own_rows.astype(F32)
        squares = squares + jnp.sum(own_rows * own_rows, axis=1, keepdims=True)
    norm = lax.rsqrt(squares * (1.0 / 4096) + EPSILON)
    inv[at.z] = jnp.transpose(jnp.broadcast_to(norm, (256, 128)))[0:1]
    near = [mover.go(inv.at[at.z], inv.at[at.z], at.up(turn(at.z, k))) for k in range(1, 4)]

    def absorb_other(k, u):
        j = turn(at.z, k + u)
        absorb(j, k, others[k - 1, chunk(j)])

    absorb_other(3, 2)
    absorb_other(1, 3)
    absorb_other(3, 1)
    absorb_other(2, 2)
    ring.to_left[2].wait_recv()
    absorb_other(1, 2)
    ring.to_right[3].wait_recv()
    absorb_other(3, 3)
    ring.to_left[1].wait_recv()
    absorb_other(1, 1)
    absorb_other(1, 0)
    ring.far[3].wait_recv()
    absorb_other(2, 3)
    ring.to_right[0].wait_recv()
    absorb_other(3, 0)
    ring.far[1].wait_recv()
    absorb_other(2, 1)
    ring.far[0].wait_recv()
    absorb_other(2, 0)
    for copy in near:
        copy.wait_recv()

    passage = lax.broadcasted_iota(jnp.int32, (1, 256), 1) // 32
    top = None
    for j in range(4):
        row = jnp.zeros((1, 256), F32)
        line = scores[j]
        for p in range(8):
            row = row + jnp.where(passage == p, line[:, p : p + 1], 0.0)
        total = s[j] * (inv[j] * scale) + row
        s[j] = total
        here = jnp.max(total, axis=1, keepdims=True)
        top = here if top is None else jnp.maximum(top, here)
    sums = jnp.zeros((256, 1), F32)
    for j in range(4):
        ex = jnp.exp(s[j] - top)
        s[j] = ex
        sums = sums + jnp.sum(ex, axis=1, keepdims=True)
    for j in range(4):
        w[j] = (s[j] * inv[j] / sums).astype(BF16)
    heads_out = jnp.zeros((256, 512), F32)
    for j in range(4):
        heads_out = heads_out + jnp.dot(
            w[j], values[j].astype(BF16), preferred_element_type=F32
        )
    head = lax.broadcasted_iota(jnp.int32, (32, 512), 1) // HEAD
    context = jnp.zeros((32, 512), F32)
    for h in range(8):
        context = context + jnp.where(head == h, heads_out[32 * h : 32 * h + 32], 0.0)
    context = context.astype(BF16)
    loads[6].wait()
    for j in range(4):
        parts[j] = jnp.dot(
            context, w_out[:, pl.ds(1024 * j, 1024)], preferred_element_type=F32
        ).astype(BF16)
    last = [
        mover.go(parts.at[turn(at.z, k)], part_buf.at[k - 1], at.up(turn(at.z, k)))
        for k in range(1, 4)
    ]
    for copy in last:
        copy.wait_recv()
    total = parts[at.z].astype(F32)
    for k in range(3):
        total = total + part_buf[k].astype(F32)
    decoded[...] = total.astype(BF16)
    mover.finish_sends()


def reader(*args):
    return pl.pallas_call(
        reader_kernel,
        out_shape=(
            jax.ShapeDtypeStruct((256, 4096), BF16),
            jax.ShapeDtypeStruct((32, 1024), BF16),
        ),
        in_specs=[VM, VM, VM, ANY, VM, VM, VM, ANY, ANY, ANY, ANY, ANY],
        out_specs=(VM, VM),
        scratch_shapes=[
            pltpu.VMEM((1024, 512), BF16), pltpu.VMEM((3, 1024, 512), BF16),
            pltpu.VMEM((32, 32, 4096), BF16), pltpu.VMEM((3, 512, 2048), BF16),
            pltpu.VMEM((3, 4, 4, 2, 16, 2048), BF16), pltpu.VMEM((512, 4096), BF16),
            pltpu.VMEM((4096, 512), BF16), pltpu.VMEM((512, 4096), BF16),
            pltpu.VMEM((4, 256, 512), BF16), pltpu.VMEM((3, 256, 512), F32),
            pltpu.VMEM((4, 512, 512), BF16), pltpu.VMEM((3, 512, 512), F32),
            pltpu.VMEM((4, 256, 256), F32), pltpu.VMEM((4, 256, 256), BF16),
            pltpu.VMEM((4, 256, 512), F32), pltpu.VMEM((4, 1, 256), F32),
            pltpu.VMEM((4, 32, 1024), BF16), pltpu.VMEM((3, 32, 1024), BF16),
            pltpu.SemaphoreType.DMA((64,)), pltpu.SemaphoreType.DMA((64,)),
            pltpu.SemaphoreType.DMA((7,)),
        ],
        compiler_params=params(3, 60),
    )(*args)


def shards(
    question_ids, answer_ids, owner, slot, passage_score, memory, embedding, live_gain, live_qkv,
    rel_bias, live_out, enc_gain, cross_kv, dec_gain, cross_query, cross_out,
):
    n_psg = lax.axis_size("psg")
    width = live_gain.shape[0]
    plen = memory.shape[1]
    qlen = question_ids.shape[1]
    own_count = owner.shape[1]
    total = own_count * n_psg
    seq = plen + qlen
    cols = live_out.shape[0]

    spread_of = jnp.asarray(spread_table(seq, rel_bias.shape[1]))
    x_mem, token_full, scores, left, right, proj_mem, proj_q, qg, w_val, bias = fetch(
        question_ids, answer_ids, owner.reshape(1, own_count), slot, rel_bias, spread_of, memory,
        embedding, passage_score, live_out,
        jnp.transpose(live_qkv, (1, 0, 2)), cross_kv, cross_query,
        live_gain.reshape(1, width), enc_gain.reshape(1, width), dec_gain.reshape(1, width),
    )
    encoded, decoded = reader(
        proj_mem, proj_q, bias, x_mem.reshape(total, plen, width), token_full, qg, scores,
        left.reshape(3, cols, width // 2), right, live_out, w_val, cross_out,
    )
    return encoded.reshape(1, own_count, seq, width), decoded[None]


def solution(mesh):
    return jax.shard_map(
        shards,
        mesh=mesh,
        in_specs=(
            P("cache", None), P("cache", None), P("cache", "psg", None), P("cache", "psg"),
            P("cache", "psg"), P("cache", None, "psg"), P("cache", "psg"), P(),
            P(None, None, "psg"), P("psg", None), P("psg", None), P(), P(None, None, "psg"), P(),
            P(None, "psg"), P("psg", None),
        ),
        out_specs=(P("cache", "psg", None, None), P("cache", None, "psg")),
        check_vma=False,
    )
```

```python
import functools

import jax
import jax.numpy as jnp
import numpy as np
from jax import lax
from jax.experimental import pallas as pl
from jax.experimental.pallas import tpu as pltpu
from jax.sharding import PartitionSpec as P

HEAD = 64
EPSILON = 1e-06
F32 = jnp.float32
BF16 = jnp.bfloat16


def bucket_table(length, bucket_count):
    positions = np.arange(length)
    relative = positions[None, :] - positions[:, None]
    halfway = bucket_count // 2
    exact_span = halfway // 2
    upper_side = (relative > 0).astype(np.int64) * halfway
    distance = np.abs(relative)
    log_bucket = exact_span + (
        np.log(np.maximum(distance, 1) / exact_span)
        / np.log(128.0 / exact_span)
        * (halfway - exact_span)
    ).astype(np.int64)
    log_bucket = np.minimum(log_bucket, halfway - 1)
    return upper_side + np.where(distance < exact_span, distance, log_bucket)


def spread_table(length, bucket_count):
    buckets = np.tile(bucket_table(length, bucket_count).T, (1, 4)).reshape(-1)
    return (buckets[None, :] == np.arange(bucket_count)[:, None]).astype(np.float32)


def dot32(a, b, dims):
    return lax.dot_general(a, b, (dims, ((), ())), preferred_element_type=F32)


MESH = pl.DeviceIdType.MESH
VM = pl.BlockSpec(memory_space=pltpu.VMEM)
SM = pl.BlockSpec(memory_space=pltpu.SMEM)
ANY = pl.BlockSpec(memory_space=pl.ANY)


def params(collective_id, mib):
    return pltpu.CompilerParams(
        collective_id=collective_id, has_side_effects=True, vmem_limit_bytes=mib << 20
    )


class Place:
    def __init__(self):
        self.c = lax.axis_index("cache")
        self.z = lax.axis_index("psg")
        self.core = lax.rem(self.c, 2)
        self.x = lax.rem(lax.div(self.c, 2), 4)
        self.y = lax.div(self.c, 8)

    def cache(self, c):
        return {"cache": c, "psg": self.z}

    def chip(self, y, x):
        return self.cache((y * 4 + x) * 2 + self.core)

    def sibling(self):
        return self.cache(self.c + 1 - 2 * self.core)

    def up(self, z):
        return {"cache": self.c, "psg": z}


def turn(p, k):
    return lax.rem(p + k + 4, 4)


def greet_all(at):
    barrier = pltpu.get_barrier_semaphore()

    def greet(d, carry):
        pl.semaphore_signal(
            barrier, inc=1, device_id=at.cache(lax.rem(at.c + d, 32)), device_id_type=MESH
        )
        return carry

    lax.fori_loop(1, 32, greet, 0)
    for k in range(1, 4):
        pl.semaphore_signal(barrier, inc=1, device_id=at.up(turn(at.z, k)), device_id_type=MESH)
    pl.semaphore_wait(barrier, 34)


class Mover:
    def __init__(self, send, recv):
        self.send, self.recv, self.count, self.started = send, recv, 0, []

    def go(self, src, dst, device):
        i = self.count
        self.count += 1
        copy = pltpu.make_async_remote_copy(
            src_ref=src, dst_ref=dst, send_sem=self.send.at[i], recv_sem=self.recv.at[i],
            device_id=device, device_id_type=MESH,
        )
        copy.start()
        self.started.append(copy)
        return copy

    def finish_sends(self):
        for copy in self.started:
            copy.wait_send()


class Ring:
    def __init__(self, mover, pos, device, own, dst, units, start=True):
        self.mover, self.pos, self.device, self.own, self.dst = mover, pos, device, own, dst
        self.right, self.left = device(turn(pos, 1)), device(turn(pos, -1))
        self.to_right, self.to_left, self.far = {}, {}, {}
        half = len(units) // 2
        self.first, self.last = units[:half], units[half:]
        if start:
            for u, v in zip(units, self.last + self.first):
                self.begin_right(u)
                self.begin_left(v)

    def begin_right(self, u):
        self.to_right[u] = self.mover.go(self.own(u), self.dst(self.pos, u, 1), self.right)

    def begin_left(self, u):
        self.to_left[u] = self.mover.go(self.own(u), self.dst(self.pos, u, -1), self.left)

    def pass_right(self, u):
        self.to_right[u].wait_recv()
        before = turn(self.pos, -1)
        self.far[u] = self.mover.go(self.dst(before, u, 1), self.dst(before, u, 2), self.right)

    def pass_left(self, u):
        self.to_left[u].wait_recv()
        after = turn(self.pos, 1)
        self.far[u] = self.mover.go(self.dst(after, u, -1), self.dst(after, u, 2), self.left)

    def onward(self):
        for u, v in zip(self.first, self.last):
            self.pass_right(u)
            self.pass_left(v)

    def near(self):
        for u in self.last:
            self.to_right[u].wait_recv()
        for v in self.first:
            self.to_left[v].wait_recv()

    def end(self):
        for copy in self.far.values():
            copy.wait_recv()


class Spread:
    def __init__(self, at, mover, full, width):
        self.at, self.mover, self.full = at, mover, full
        self.quarter, self.width = width // 4, width

    def begin(self, live_out, first):
        at = self.at
        rows = pl.ds(pl.multiple_of(at.c * 16, 16), 16)
        self.start = [
            self.mover.go(
                live_out.at[rows, pl.ds(first, self.width)],
                self.full.at[k - 1, at.y, at.x, at.core],
                at.up(turn(at.z, -k)),
            )
            for k in range(1, 4)
        ]

    def cols(self, u, n=1):
        return pl.ds(u * self.quarter, n * self.quarter)

    def phase_one(self):
        at, full = self.at, self.full
        for copy in self.start:
            copy.wait_recv()
        a = lambda pos, u, k=0: full.at[:, at.y, pos, at.core, :, self.cols(u)]
        b = lambda pos, u, k=0: full.at[:, pos, at.x, at.core, :, self.cols(u)]
        self.one = [
            Ring(self.mover, at.x, lambda p: at.chip(at.y, p), lambda u: a(at.x, u), a, [0, 1]),
            Ring(self.mover, at.y, lambda p: at.chip(p, at.x), lambda u: b(at.y, u), b, [2, 3]),
        ]

    def phase_one_onward(self):
        for ring in self.one:
            ring.onward()

    def phase_one_end(self):
        for ring in self.one:
            ring.near()
            ring.end()

    def line(self, full, axis):
        at = self.at
        if axis == "x":
            return full.at[:, at.y, :, at.core, :, self.cols(0, 2)]
        return full.at[:, :, at.x, at.core, :, self.cols(2, 2)]

    def phase_two(self):
        at, full = self.at, self.full
        a = lambda pos, u, k=0: full.at[:, pos, :, at.core, :, self.cols(u)]
        b = lambda pos, u, k=0: full.at[:, :, pos, at.core, :, self.cols(u)]
        self.two = [
            Ring(self.mover, at.y, lambda p: at.chip(p, at.x), lambda u: a(at.y, u), a, [0, 1]),
            Ring(self.mover, at.x, lambda p: at.chip(at.y, p), lambda u: b(at.x, u), b, [2, 3]),
        ]
        self.over = []
        self.cross(0)

    def cross(self, k):
        at, full = self.at, self.full
        a = full.at[:, turn(at.y, k), :, at.core, :, self.cols(0, 2)]
        b = full.at[:, :, turn(at.x, k), at.core, :, self.cols(2, 2)]
        for view in (a, b):
            self.over.append(self.mover.go(view, view, at.sibling()))

    def phase_two_onward(self):
        for ring in self.two:
            ring.onward()
        for ring in self.two:
            ring.near()
        self.cross(1)
        self.cross(-1)

    def finish(self):
        for ring in self.two:
            ring.end()
        self.cross(2)
        for copy in self.over:
            copy.wait_recv()


def norm_rows(rows, gain):
    wide = rows.astype(F32)
    inverse = lax.rsqrt(jnp.mean(wide * wide, axis=-1, keepdims=True) + EPSILON)
    return (wide * gain).astype(BF16), inverse


def fetch_kernel(
    question_ids, answer_ids, owner, slot, rel_bias, spread_of, memory, embedding, own_score,
    live_out, w_qkv, cross_kv, cross_query,
    live_gain, enc_gain, dec_gain,
    x_out, tokens, scores, full, full_next, proj_mem, proj_q, qg, w_val_out, bias,
    line_buf, score, by_key, every, table, turned, plan, tok, table_w, out_buf, in_buf0, in_buf1, in_buf2, in_buf3, own, pair_buf, a_buf, b_buf, a2_buf, b2_buf, tok_sum,
    x_full, weights, acc, squares, scaled, w_query, kv_buf, w_key, w_val,
    send, recv, a2a_send, a2a_recv, line_send, line_recv, local_sem, kv_sem, out_sem,
):
    at = Place()
    line_buf[...] = jnp.zeros((8, 128), jnp.int32)
    line_buf[0:1, 0:8] = owner[...]
    line_buf[0:1, 32:40] = slot[...]
    line_buf[1:2, 64:80] = question_ids[...]
    line_buf[1:2, 80:112] = answer_ids[...]
    placed = pltpu.roll(line_buf[0:1], 8 * at.z, 1)
    every[at.c, at.z] = placed + jnp.where(at.z == 0, line_buf[1:2], 0)
    score[...] = jnp.zeros((1, 128), F32)
    score[:, 0:8] = own_score[...]
    table[32:128] = jnp.zeros((96, 128), jnp.int32)
    load_table = pltpu.make_async_copy(embedding, table_w, local_sem.at[5])
    load_table.start()
    load_weights = [
        pltpu.make_async_copy(w_qkv.at[i], weights.at[i], local_sem.at[i]) for i in range(3)
    ] + [pltpu.make_async_copy(cross_query, w_query, local_sem.at[3])]
    for copy in load_weights:
        copy.start()

    def kv_copy(i):
        slot = lax.rem(i, 4)
        return pltpu.make_async_copy(
            cross_kv.at[pl.ds(i * 256, 256)], kv_buf.at[slot], kv_sem.at[slot]
        )

    for i in range(3):
        kv_copy(i).start()

    def split_kv(first, last):
        def one(i, carry):
            @pl.when(i < 13)
            def _():
                kv_copy(i + 3).start()

            kv_copy(i).wait()
            rows = pl.ds(pl.multiple_of(i * 256, 256), 256)
            slot = lax.rem(i, 4)
            w_key[rows] = kv_buf[slot, :, 0, :]
            gain = jnp.transpose(jnp.broadcast_to(enc_gain[:, rows], (128, 256)))[:, 0:1]
            w_val[rows] = (kv_buf[slot, :, 1, :].astype(F32) * gain).astype(BF16)
            return carry

        lax.fori_loop(first, last, one, 0)

    greet_all(at)
    mover = Mover(send, recv)
    in_buf = (in_buf0, in_buf1, in_buf2, in_buf3)

    spread = Spread(at, mover, full, 2048)
    spread.begin(live_out, 0)
    spread_next = Spread(at, mover, full_next, 2048)
    spread_next.begin(live_out, 2048)

    near = [
        mover.go(every.at[at.c, at.z], every.at[at.c, at.z], at.up(turn(at.z, k)))
        for k in range(1, 4)
    ]

    def line_copy(d):
        return pltpu.make_async_remote_copy(
            src_ref=every.at[at.c], dst_ref=every.at[at.c], send_sem=line_send.at[d],
            recv_sem=line_recv.at[d], device_id=at.cache(lax.rem(at.c + d, 32)),
            device_id_type=MESH,
        )

    def send_line(d, carry):
        line_copy(d).start()
        return carry

    def wait_line(d, carry):
        line_copy(d).wait()
        return carry

    for copy in near:
        copy.wait_recv()
    lax.fori_loop(1, 32, send_line, 0)
    split_kv(0, 4)
    spread.phase_one()
    spread_next.phase_one()
    split_kv(4, 6)

    by_bucket = jnp.dot(
        rel_bias[...], spread_of[...], precision=lax.Precision.HIGHEST, preferred_element_type=F32
    )
    for b in range(32):
        by_key[b] = by_bucket[:, 128 * b : 128 * b + 128]
    for h in range(8):
        bias[h] = by_key[:, h, :]
    lax.fori_loop(1, 32, wait_line, 0)
    for q in range(32):
        table[q : q + 1] = (every[q, 0] + every[q, 1]) + (every[q, 2] + every[q, 3])

    names = table[0:32]
    turned[...] = jnp.transpose(table[...].astype(F32))
    lane = lax.broadcasted_iota(jnp.int32, (32, 128), 1)
    rank = jnp.zeros((32, 128), jnp.int32)
    for shift in range(1, 32):
        same = jnp.logical_and(pltpu.roll(names, shift, 1) == names, lane >= shift)
        rank = rank + jnp.where(same, 1, 0)
    entries = pltpu.roll(names, 96, 1)
    found = []
    for r in range(2):
        hit = jnp.logical_and(jnp.logical_and(names == at.c, rank == r), lane < 32)
        entry = jnp.where(hit, entries, 0)
        for shift in (64, 32, 16, 8, 4, 2, 1):
            entry = entry + pltpu.roll(entry, shift, 1)
        found.append(entry)
    asks = jnp.where(lane == 32, found[0], found[1])
    table[0:32] = jnp.where(lane < 32, names * 2 + rank, asks)
    to_plan = pltpu.make_async_copy(table.at[pl.ds(0, 32)], plan, local_sem.at[6])
    to_plan.start()
    to_plan.wait()

    def passage_copy(h, d):
        q = lax.rem(at.c + d, 32)
        return pltpu.make_async_remote_copy(
            src_ref=out_buf.at[h, pl.ds(2 * q, 2)], dst_ref=in_buf[h].at[pl.ds(2 * at.c, 2)],
            send_sem=a2a_send.at[h, d], recv_sem=a2a_recv.at[h, d],
            device_id=at.cache(q), device_id_type=MESH,
        )

    def send_part(h):
        lanes = pl.ds(h * 256, 256)

        def one(d, carry):
            q = lax.rem(at.c + d, 32)
            if h > 0:
                passage_copy(h - 1, d).wait_send()
            out_buf[h, 2 * q] = memory[plan[q, 32], :, lanes]
            out_buf[h, 2 * q + 1] = memory[plan[q, 33], :, lanes]
            passage_copy(h, d).start()
            return carry

        lax.fori_loop(1, 32, one, 0)
        in_buf[h][2 * at.c] = memory[plan[at.c, 32], :, lanes]
        in_buf[h][2 * at.c + 1] = memory[plan[at.c, 33], :, lanes]

    def wait_part(h):
        def one(d, carry):
            passage_copy(h, d).wait_recv()
            return carry

        lax.fori_loop(1, 32, one, 0)

        def pack(j, carry):
            own[h, pl.ds(pl.multiple_of(16 * j, 16), 16)] = in_buf[h][plan[at.c, j]]
            return carry

        lax.fori_loop(0, 32, pack, 0)

    def lanes_of(pos, h):
        return pl.ds(pl.multiple_of(pos * 1024 + h * 512, 512), 512)

    def part(pos, unit, k=0):
        h, g = unit
        return x_full.at[
            pl.ds(g * 256, 256), pl.ds(pl.multiple_of(pos * 1024 + h * 256, 256), 256)
        ]

    def ring_part(h):
        return Ring(
            mover, at.z, at.up, lambda u: own.at[u[0], pl.ds(u[1] * 256, 256)], part,
            [(h, 0), (h, 1)],
        )

    stored = []

    def multiply(k, h):
        pos = turn(at.z, k)
        lanes = lanes_of(pos, h)
        if k == 0:
            x_full[:, lanes] = jnp.concatenate([own[2 * h], own[2 * h + 1]], axis=1)
        keep = pltpu.make_async_copy(
            x_full.at[:, lanes], x_out.at[:, lanes], out_sem.at[len(stored)]
        )
        keep.start()
        first = not stored
        stored.append(keep)
        gain = live_gain[:, lanes]
        for r in range(2):
            rows = pl.ds(r * 256, 256)
            wide = x_full[rows, lanes].astype(F32)
            scaled[rows] = (wide * gain).astype(BF16)
            square = jnp.sum(wide * wide, axis=1, keepdims=True)
            squares[rows] = square if first else squares[rows] + square

        def one(i, carry):
            product = jnp.dot(scaled[...], weights[i, lanes], preferred_element_type=F32)
            acc[i] = product if first else acc[i] + product
            return carry

        lax.fori_loop(0, 3, one, 0)

    def sent_part(h):
        def one(d, carry):
            passage_copy(h, d).wait_send()
            return carry

        lax.fori_loop(1, 32, one, 0)

    send_part(0)

    load_table.wait()
    held = lax.broadcasted_iota(jnp.int32, (48, 1004), 1).astype(F32) + (at.c * 1004).astype(F32)
    for b in range(8):
        picks = [
            jnp.where(held == turned[64:112, q : q + 1], 1.0, 0.0).astype(BF16)
            for q in range(4 * b, 4 * b + 4)
        ]
        named = jnp.dot(
            jnp.concatenate(picks, axis=0), table_w[...], preferred_element_type=F32
        ).astype(BF16)
        for n in range(4):
            q = 4 * b + n
            tok[q // 8, (q // 2) % 4, q % 2] = named[48 * n : 48 * (n + 1)]
    other = 1 - at.core
    pair = mover.go(tok.at[:, :, other], pair_buf, at.sibling())
    spread.phase_one_onward()
    spread_next.phase_one_onward()
    send_part(1)

    pair.wait_recv()

    def add_pair(y, carry):
        for x in range(4):
            pair_buf[y, x] = pair_buf[y, x] + tok[y, x, at.core]
        return carry

    lax.fori_loop(0, 4, add_pair, 0)
    wait_part(0)
    rings = [ring_part(0)]
    send_part(2)
    wait_part(1)
    rings.append(ring_part(1))
    for copy in load_weights:
        copy.wait()
    multiply(0, 0)
    send_part(3)
    lo, hi = pl.ds(0, 512), pl.ds(512, 512)
    tok_a = [
        mover.go(
            pair_buf.at[:, turn(at.x, k), :, lo], a_buf.at[k - 1], at.chip(at.y, turn(at.x, k))
        )
        for k in range(1, 4)
    ]
    tok_b = [
        mover.go(
            pair_buf.at[turn(at.y, k), :, :, hi], b_buf.at[k - 1], at.chip(turn(at.y, k), at.x)
        )
        for k in range(1, 4)
    ]
    near_scores = [
        mover.go(score, scores.at[at.z], at.up(turn(at.z, k))) for k in range(1, 4)
    ]
    scores[at.z] = score[...]
    wait_part(2)
    rings.append(ring_part(2))
    rings[0].onward()
    wait_part(3)
    rings.append(ring_part(3))
    spread.phase_one_end()
    spread_next.phase_one_end()
    multiply(0, 1)
    rings[1].onward()
    for copy in tok_a + tok_b:
        copy.wait_recv()

    def add_line(i, carry):
        a_buf[0, i] = (a_buf[0, i] + a_buf[1, i]) + (a_buf[2, i] + pair_buf[i, at.x, :, lo])
        b_buf[0, i] = (b_buf[0, i] + b_buf[1, i]) + (b_buf[2, i] + pair_buf[at.y, i, :, hi])
        return carry

    lax.fori_loop(0, 4, add_line, 0)
    tok_a2 = [
        mover.go(a_buf.at[0, turn(at.y, k)], a2_buf.at[k - 1], at.chip(turn(at.y, k), at.x))
        for k in range(1, 4)
    ]
    tok_b2 = [
        mover.go(b_buf.at[0, turn(at.x, k)], b2_buf.at[k - 1], at.chip(at.y, turn(at.x, k)))
        for k in range(1, 4)
    ]
    spread.phase_two()
    split_kv(6, 9)
    rings[0].near()
    rings[1].near()
    multiply(1, 0)
    multiply(-1, 0)
    rings[2].onward()
    for copy in tok_a2 + tok_b2:
        copy.wait_recv()
    tok_sum[:, lo] = (a2_buf[0] + a2_buf[1]) + (a2_buf[2] + a_buf[0, at.y])
    tok_sum[:, hi] = (b2_buf[0] + b2_buf[1]) + (b2_buf[2] + b_buf[0, at.x])
    mine = pl.ds(pl.multiple_of(at.z * 1024, 1024), 1024)
    near_tokens = [
        mover.go(tok_sum, tokens.at[:, mine], at.up(turn(at.z, k))) for k in range(1, 4)
    ]
    tokens[:, mine] = tok_sum[...]
    rings[0].end()
    rings[1].end()
    multiply(2, 0)
    rings[3].onward()
    split_kv(9, 13)
    spread.phase_two_onward()
    split_kv(13, 16)
    keep_values = pltpu.make_async_copy(w_val, w_val_out, local_sem.at[4])
    keep_values.start()
    for copy in near_scores + near_tokens:
        copy.wait_recv()

    rows, inverse = norm_rows(tokens[0:16], live_gain[...])

    def project(i, carry):
        total = jnp.dot(rows, weights[i], preferred_element_type=F32)
        proj_q[i] = (total * inverse).astype(BF16)
        return carry

    lax.fori_loop(0, 3, project, 0)
    rows_a, inverse_a = norm_rows(tokens[16:48], dec_gain[...])
    queries = jnp.dot(rows_a, w_query[...], preferred_element_type=F32) * inverse_a
    head = lax.broadcasted_iota(jnp.int32, (32, 512), 1) // HEAD
    for h in range(8):
        scaled[pl.ds(32 * h, 32)] = jnp.where(head == h, queries, 0.0).astype(BF16)

    def fold(n, carry):
        cols = pl.ds(pl.multiple_of(n * 1024, 1024), 1024)
        product = dot32(scaled[pl.ds(0, 256)], w_key[cols], ((1,), (1,)))
        qg[:, cols] = (product * enc_gain[:, cols]).astype(BF16)
        return carry

    lax.fori_loop(0, 4, fold, 0)
    rings[2].near()
    rings[3].near()
    multiply(1, 1)
    multiply(-1, 1)
    rings[2].end()
    rings[3].end()
    multiply(2, 1)
    inverse_m = lax.rsqrt(squares[...] * (1.0 / 4096) + EPSILON)

    def close(i, carry):
        proj_mem[i] = (acc[i] * inverse_m).astype(BF16)
        return carry

    lax.fori_loop(0, 3, close, 0)
    spread.finish()
    for copy in stored:
        copy.wait()
    keep_values.wait()
    mover.finish_sends()

    sent_part(3)


def fetch(*args):
    return pl.pallas_call(
        fetch_kernel,
        out_shape=(
            jax.ShapeDtypeStruct((512, 4096), BF16),
            jax.ShapeDtypeStruct((48, 4096), BF16),
            jax.ShapeDtypeStruct((4, 1, 128), F32),
            jax.ShapeDtypeStruct((3, 4, 4, 2, 16, 2048), BF16),
            jax.ShapeDtypeStruct((3, 4, 4, 2, 16, 2048), BF16),
            jax.ShapeDtypeStruct((3, 512, 512), BF16),
            jax.ShapeDtypeStruct((3, 16, 512), BF16),
            jax.ShapeDtypeStruct((256, 4096), BF16),
            jax.ShapeDtypeStruct((4096, 512), BF16),
            jax.ShapeDtypeStruct((8, 32, 128), F32),
        ),
        in_specs=[VM] * 7 + [ANY, VM, ANY, ANY, ANY, ANY, VM, VM, VM],
        out_specs=(ANY, VM, VM, ANY, ANY, VM, VM, VM, ANY, VM),
        scratch_shapes=[
            pltpu.VMEM((8, 128), jnp.int32), pltpu.VMEM((1, 128), F32),
            pltpu.VMEM((32, 8, 128), F32),
            pltpu.VMEM((32, 4, 1, 128), jnp.int32), pltpu.VMEM((128, 128), jnp.int32),
            pltpu.VMEM((128, 128), F32), pltpu.SMEM((32, 128), jnp.int32),
            pltpu.VMEM((4, 4, 2, 48, 1024), BF16), pltpu.VMEM((1004, 1024), BF16),
            pltpu.VMEM((4, 64, 16, 256), BF16), pltpu.VMEM((64, 16, 256), BF16),
            pltpu.VMEM((64, 16, 256), BF16), pltpu.VMEM((64, 16, 256), BF16),
            pltpu.VMEM((64, 16, 256), BF16),
            pltpu.VMEM((4, 512, 256), BF16), pltpu.VMEM((4, 4, 48, 1024), BF16),
            pltpu.VMEM((3, 4, 48, 512), BF16), pltpu.VMEM((3, 4, 48, 512), BF16),
            pltpu.VMEM((3, 48, 512), BF16), pltpu.VMEM((3, 48, 512), BF16),
            pltpu.VMEM((48, 1024), BF16),
            pltpu.VMEM((512, 4096), BF16), pltpu.VMEM((3, 4096, 512), BF16),
            pltpu.VMEM((3, 512, 512), F32), pltpu.VMEM((512, 1), F32),
            pltpu.VMEM((512, 512), BF16), pltpu.VMEM((4096, 512), BF16),
            pltpu.VMEM((4, 256, 2, 512), BF16), pltpu.VMEM((4096, 512), BF16),
            pltpu.VMEM((4096, 512), BF16),
            pltpu.SemaphoreType.DMA((112,)), pltpu.SemaphoreType.DMA((112,)),
            pltpu.SemaphoreType.DMA((4, 32)), pltpu.SemaphoreType.DMA((4, 32)),
            pltpu.SemaphoreType.DMA((32,)), pltpu.SemaphoreType.DMA((32,)),
            pltpu.SemaphoreType.DMA((7,)), pltpu.SemaphoreType.DMA((4,)),
            pltpu.SemaphoreType.DMA((8,)),
        ],
        compiler_params=params(2, 60),
    )(*args)


def reader_kernel(
    proj_mem, proj_q, bias, x_mem, tokens, qg, scores, left_in, right_in, live_out, w_val_in,
    cross_out_in,
    encoded, decoded,
    ctx, others, x_seq, left, right, own_out, w_val, w_out, ql, ql_part, lv, lv_part, s, w, values,
    inv, parts, part_buf, send, recv, local_sem,
):
    at = Place()
    mover = Mover(send, recv)
    spread = Spread(at, mover, right, 2048)
    loads = [
        pltpu.make_async_copy(a, b, local_sem.at[i])
        for i, (a, b) in enumerate([
            (spread.line(right_in, "x"), spread.line(right, "x")),
            (spread.line(right_in, "y"), spread.line(right, "y")),
            (x_mem, x_seq.at[:, pl.ds(0, 16)]), (live_out, own_out), (w_val_in, w_val),
            (left_in, left), (cross_out_in, w_out),
        ])
    ]
    for copy in loads:
        copy.start()
    greet_all(at)
    scale = HEAD ** (-0.5)
    nt = ((1,), (1,))
    loads[0].wait()
    loads[1].wait()
    spread.phase_two()

    def chunk(j):
        return pl.ds(pl.multiple_of(j * 256, 256), 256)

    def part(pos, u, k):
        return others.at[{1: 2, -1: 0, 2: 1}[k], chunk(turn(pos, u))]

    ring = Ring(
        mover, at.z, at.up, lambda u: ctx.at[chunk(turn(at.z, u))], part, [2, 1, 3, 0], False
    )

    low = lax.broadcasted_iota(jnp.int32, (128, 128), 1) < HEAD
    owner_lane = lax.broadcasted_iota(jnp.int32, (32, 256), 1) // 32 % 4

    def attend(j):
        def group(g, carry):
            first = j * 8 + g * 4

            def pair(i, p):
                lanes = pl.ds(128 * p, 128)
                pieces = []
                for n in range(4):
                    pieces.append(
                        proj_mem[i, pl.ds(pl.multiple_of((first + n) * 16, 16), 16), lanes]
                    )
                    pieces.append(proj_q[i, :, lanes])
                return jnp.concatenate(pieces, axis=0)

            for p in range(4):
                q, k, v = pair(0, p), pair(1, p), pair(2, p)
                none = jnp.zeros_like(q)
                both = jnp.concatenate([jnp.where(low, q, none), jnp.where(low, none, q)], axis=0)
                full = dot32(k, both, nt)
                sc = full[0:32]
                for n in range(1, 4):
                    sc = jnp.where(owner_lane == n, full[32 * n : 32 * n + 32], sc)
                sc = sc * scale + jnp.concatenate([bias[2 * p], bias[2 * p + 1]], axis=1)
                ex = jnp.exp(sc - jnp.max(sc, axis=0, keepdims=True))
                ex = ex * (1.0 / jnp.sum(ex, axis=0, keepdims=True))
                full = jnp.concatenate(
                    [jnp.where(owner_lane == n, ex, 0.0) for n in range(4)], axis=0
                ).astype(BF16)
                out = dot32(full, v, ((0,), (0,)))
                ctx[pl.ds(pl.multiple_of(first * 32, 128), 128), pl.ds(128 * p, 128)] = jnp.where(
                    low, out[0:128], out[128:256]
                ).astype(BF16)
            return carry

        lax.fori_loop(0, 2, group, 0)

    for u in (2, 3, 1, 0):
        attend(turn(at.z, u))
        ring.begin_right(u)
        ring.begin_left(u)

    loads[2].wait()

    def fill(p, carry):
        x_seq[p, pl.ds(16, 16)] = tokens[pl.ds(0, 16)]
        return carry

    lax.fori_loop(0, 32, fill, 0)
    ring.pass_right(2)

    def rows_of(j):
        return x_seq[pl.ds(j * 8, 8)].reshape(256, 4096)

    def score_inputs(j, carry):
        s[j] = dot32(qg[...], rows_of(j), nt)
        return carry

    lax.fori_loop(0, 4, score_inputs, 0)
    ring.pass_left(3)
    spread.phase_two_onward()
    loads[4].wait()
    of_question = jnp.dot(tokens[pl.ds(0, 16)], w_val[...], preferred_element_type=F32)

    def value_inputs(j, carry):
        rows = jnp.dot(
            x_seq[pl.ds(j * 8, 8), pl.ds(0, 16)].reshape(128, 4096), w_val[...],
            preferred_element_type=F32,
        )
        for p in range(8):
            values[j, pl.ds(32 * p, 16)] = rows[16 * p : 16 * p + 16]
            values[j, pl.ds(32 * p + 16, 16)] = of_question
        return carry

    lax.fori_loop(0, 4, value_inputs, 0)
    ring.pass_right(1)
    loads[3].wait()
    ql[0] = dot32(qg[...], own_out[...], nt).astype(BF16)
    lv[0] = jnp.dot(own_out[...], w_val[...], preferred_element_type=F32).astype(BF16)

    def absorb(j, k, rows):
        s[j] = s[j] + dot32(ql[k], rows, nt)
        values[j] = values[j] + jnp.dot(rows, lv[k], preferred_element_type=F32)

    def absorb_own(j, carry):
        absorb(j, 0, ctx[chunk(j)])
        return carry

    lax.fori_loop(0, 4, absorb_own, 0)
    loads[5].wait()
    half, rest = pl.ds(0, 2048), pl.ds(2048, 2048)

    def fold_left(k, carry):
        ql_part[k] = dot32(qg[:, half], left[k], nt)
        lv_part[k] = jnp.dot(left[k], w_val[half], preferred_element_type=F32)
        return carry

    lax.fori_loop(0, 3, fold_left, 0)
    ring.pass_left(0)
    spread.finish()

    def fold_right(k, carry):
        rows = right[k].reshape(512, 2048)
        ql[k + 1] = (ql_part[k] + dot32(qg[:, rest], rows, nt)).astype(BF16)
        lv[k + 1] = (
            lv_part[k] + jnp.dot(rows, w_val[rest], preferred_element_type=F32)
        ).astype(BF16)
        return carry

    lax.fori_loop(0, 3, fold_right, 0)

    ring.far[2].wait_recv()
    mine = chunk(at.z)

    def group_rows(k, n):
        if k == 0:
            return own_out[:, pl.ds(n * 1024, 1024)]
        if n < 2:
            return left[k - 1, :, pl.ds(n * 1024, 1024)]
        return right[k - 1, :, :, :, :, pl.ds((n - 2) * 1024, 1024)].reshape(512, 1024)

    squares = jnp.zeros((256, 1), F32)
    for n in range(4):
        cols = pl.ds(n * 1024, 1024)
        attended = None
        for k in range(4):
            rows = ctx[mine] if k == 0 else others[k - 1, mine]
            product = jnp.dot(rows, group_rows(k, n), preferred_element_type=F32)
            product = product.astype(BF16).astype(F32)
            attended = product if k == 0 else attended + product
        own_rows = x_seq[pl.ds(at.z * 8, 8), :, cols].reshape(256, 1024).astype(F32)
        own_rows = (own_rows + attended).astype(BF16)
        encoded[:, cols] = own_rows
        own_rows = own_rows.astype(F32)
        squares = squares + jnp.sum(own_rows * own_rows, axis=1, keepdims=True)
    norm = lax.rsqrt(squares * (1.0 / 4096) + EPSILON)
    inv[at.z] = jnp.transpose(jnp.broadcast_to(norm, (256, 128)))[0:1]
    near = [mover.go(inv.at[at.z], inv.at[at.z], at.up(turn(at.z, k))) for k in range(1, 4)]

    def absorb_other(k, u):
        j = turn(at.z, k + u)
        absorb(j, k, others[k - 1, chunk(j)])

    absorb_other(3, 2)
    absorb_other(1, 3)
    absorb_other(3, 1)
    absorb_other(2, 2)
    ring.to_left[2].wait_recv()
    absorb_other(1, 2)
    ring.to_right[3].wait_recv()
    absorb_other(3, 3)
    ring.to_left[1].wait_recv()
    absorb_other(1, 1)
    absorb_other(1, 0)
    ring.far[3].wait_recv()
    absorb_other(2, 3)
    ring.to_right[0].wait_recv()
    absorb_other(3, 0)
    ring.far[1].wait_recv()
    absorb_other(2, 1)
    ring.far[0].wait_recv()
    absorb_other(2, 0)
    for copy in near:
        copy.wait_recv()

    passage = lax.broadcasted_iota(jnp.int32, (1, 256), 1) // 32
    top = None
    for j in range(4):
        row = jnp.zeros((1, 256), F32)
        line = scores[j]
        for p in range(8):
            row = row + jnp.where(passage == p, line[:, p : p + 1], 0.0)
        total = s[j] * (inv[j] * scale) + row
        s[j] = total
        here = jnp.max(total, axis=1, keepdims=True)
        top = here if top is None else jnp.maximum(top, here)
    sums = jnp.zeros((256, 1), F32)
    for j in range(4):
        ex = jnp.exp(s[j] - top)
        s[j] = ex
        sums = sums + jnp.sum(ex, axis=1, keepdims=True)
    for j in range(4):
        w[j] = (s[j] * inv[j] / sums).astype(BF16)
    heads_out = jnp.zeros((256, 512), F32)
    for j in range(4):
        heads_out = heads_out + jnp.dot(
            w[j], values[j].astype(BF16), preferred_element_type=F32
        )
    head = lax.broadcasted_iota(jnp.int32, (32, 512), 1) // HEAD
    context = jnp.zeros((32, 512), F32)
    for h in range(8):
        context = context + jnp.where(head == h, heads_out[32 * h : 32 * h + 32], 0.0)
    context = context.astype(BF16)
    loads[6].wait()
    for j in range(4):
        parts[j] = jnp.dot(
            context, w_out[:, pl.ds(1024 * j, 1024)], preferred_element_type=F32
        ).astype(BF16)
    last = [
        mover.go(parts.at[turn(at.z, k)], part_buf.at[k - 1], at.up(turn(at.z, k)))
        for k in range(1, 4)
    ]
    for copy in last:
        copy.wait_recv()
    total = parts[at.z].astype(F32)
    for k in range(3):
        total = total + part_buf[k].astype(F32)
    decoded[...] = total.astype(BF16)
    mover.finish_sends()


def reader(*args):
    return pl.pallas_call(
        reader_kernel,
        out_shape=(
            jax.ShapeDtypeStruct((256, 4096), BF16),
            jax.ShapeDtypeStruct((32, 1024), BF16),
        ),
        in_specs=[VM, VM, VM, ANY, VM, VM, VM, ANY, ANY, ANY, ANY, ANY],
        out_specs=(VM, VM),
        scratch_shapes=[
            pltpu.VMEM((1024, 512), BF16), pltpu.VMEM((3, 1024, 512), BF16),
            pltpu.VMEM((32, 32, 4096), BF16), pltpu.VMEM((3, 512, 2048), BF16),
            pltpu.VMEM((3, 4, 4, 2, 16, 2048), BF16), pltpu.VMEM((512, 4096), BF16),
            pltpu.VMEM((4096, 512), BF16), pltpu.VMEM((512, 4096), BF16),
            pltpu.VMEM((4, 256, 512), BF16), pltpu.VMEM((3, 256, 512), F32),
            pltpu.VMEM((4, 512, 512), BF16), pltpu.VMEM((3, 512, 512), F32),
            pltpu.VMEM((4, 256, 256), F32), pltpu.VMEM((4, 256, 256), BF16),
            pltpu.VMEM((4, 256, 512), F32), pltpu.VMEM((4, 1, 256), F32),
            pltpu.VMEM((4, 32, 1024), BF16), pltpu.VMEM((3, 32, 1024), BF16),
            pltpu.SemaphoreType.DMA((64,)), pltpu.SemaphoreType.DMA((64,)),
            pltpu.SemaphoreType.DMA((7,)),
        ],
        compiler_params=params(3, 60),
    )(*args)


def shards(
    question_ids, answer_ids, owner, slot, passage_score, memory, embedding, live_gain, live_qkv,
    rel_bias, live_out, enc_gain, cross_kv, dec_gain, cross_query, cross_out,
):
    n_psg = lax.axis_size("psg")
    width = live_gain.shape[0]
    plen = memory.shape[1]
    qlen = question_ids.shape[1]
    own_count = owner.shape[1]
    total = own_count * n_psg
    seq = plen + qlen
    cols = live_out.shape[0]

    spread_of = jnp.asarray(spread_table(seq, rel_bias.shape[1]))
    x_mem, token_full, scores, left, right, proj_mem, proj_q, qg, w_val, bias = fetch(
        question_ids, answer_ids, owner.reshape(1, own_count), slot, rel_bias, spread_of, memory,
        embedding, passage_score, live_out,
        jnp.transpose(live_qkv, (1, 0, 2)), cross_kv, cross_query,
        live_gain.reshape(1, width), enc_gain.reshape(1, width), dec_gain.reshape(1, width),
    )
    encoded, decoded = reader(
        proj_mem, proj_q, bias, x_mem.reshape(total, plen, width), token_full, qg, scores,
        left.reshape(3, cols, width // 2), right, live_out, w_val, cross_out,
    )
    return encoded.reshape(1, own_count, seq, width), decoded[None]


def solution(mesh):
    return jax.shard_map(
        shards,
        mesh=mesh,
        in_specs=(
            P("cache", None), P("cache", None), P("cache", "psg", None), P("cache", "psg"),
            P("cache", "psg"), P("cache", None, "psg"), P("cache", "psg"), P(),
            P(None, None, "psg"), P("psg", None), P("psg", None), P(), P(None, None, "psg"), P(),
            P(None, "psg"), P("psg", None),
        ),
        out_specs=(P("cache", "psg", None, None), P("cache", None, "psg")),
        check_vma=False,
    )
```

```python
import functools

import jax
import jax.numpy as jnp
import numpy as np
from jax import lax
from jax.experimental import pallas as pl
from jax.experimental.pallas import tpu as pltpu
from jax.sharding import PartitionSpec as P

HEAD = 64
EPSILON = 1e-06
F32 = jnp.float32
BF16 = jnp.bfloat16


def bucket_table(length, bucket_count):
    positions = np.arange(length)
    relative = positions[None, :] - positions[:, None]
    halfway = bucket_count // 2
    exact_span = halfway // 2
    upper_side = (relative > 0).astype(np.int64) * halfway
    distance = np.abs(relative)
    log_bucket = exact_span + (
        np.log(np.maximum(distance, 1) / exact_span)
        / np.log(128.0 / exact_span)
        * (halfway - exact_span)
    ).astype(np.int64)
    log_bucket = np.minimum(log_bucket, halfway - 1)
    return upper_side + np.where(distance < exact_span, distance, log_bucket)


def spread_table(length, bucket_count):
    buckets = np.tile(bucket_table(length, bucket_count).T, (1, 4)).reshape(-1)
    return (buckets[None, :] == np.arange(bucket_count)[:, None]).astype(np.float32)


def dot32(a, b, dims):
    return lax.dot_general(a, b, (dims, ((), ())), preferred_element_type=F32)


MESH = pl.DeviceIdType.MESH
VM = pl.BlockSpec(memory_space=pltpu.VMEM)
SM = pl.BlockSpec(memory_space=pltpu.SMEM)
ANY = pl.BlockSpec(memory_space=pl.ANY)


def params(collective_id, mib):
    return pltpu.CompilerParams(
        collective_id=collective_id, has_side_effects=True, vmem_limit_bytes=mib << 20
    )


class Place:
    def __init__(self):
        self.c = lax.axis_index("cache")
        self.z = lax.axis_index("psg")
        self.core = lax.rem(self.c, 2)
        self.x = lax.rem(lax.div(self.c, 2), 4)
        self.y = lax.div(self.c, 8)

    def cache(self, c):
        return {"cache": c, "psg": self.z}

    def chip(self, y, x):
        return self.cache((y * 4 + x) * 2 + self.core)

    def sibling(self):
        return self.cache(self.c + 1 - 2 * self.core)

    def up(self, z):
        return {"cache": self.c, "psg": z}


def turn(p, k):
    return lax.rem(p + k + 4, 4)


def greet_all(at):
    barrier = pltpu.get_barrier_semaphore()

    def greet(d, carry):
        pl.semaphore_signal(
            barrier, inc=1, device_id=at.cache(lax.rem(at.c + d, 32)), device_id_type=MESH
        )
        return carry

    lax.fori_loop(1, 32, greet, 0)
    for k in range(1, 4):
        pl.semaphore_signal(barrier, inc=1, device_id=at.up(turn(at.z, k)), device_id_type=MESH)
    pl.semaphore_wait(barrier, 34)


class Mover:
    def __init__(self, send, recv):
        self.send, self.recv, self.count, self.started = send, recv, 0, []

    def go(self, src, dst, device):
        i = self.count
        self.count += 1
        copy = pltpu.make_async_remote_copy(
            src_ref=src, dst_ref=dst, send_sem=self.send.at[i], recv_sem=self.recv.at[i],
            device_id=device, device_id_type=MESH,
        )
        copy.start()
        self.started.append(copy)
        return copy

    def finish_sends(self):
        for copy in self.started:
            copy.wait_send()


class Ring:
    def __init__(self, mover, pos, device, own, dst, units, start=True):
        self.mover, self.pos, self.device, self.own, self.dst = mover, pos, device, own, dst
        self.right, self.left = device(turn(pos, 1)), device(turn(pos, -1))
        self.to_right, self.to_left, self.far = {}, {}, {}
        half = len(units) // 2
        self.first, self.last = units[:half], units[half:]
        if start:
            for u, v in zip(units, self.last + self.first):
                self.begin_right(u)
                self.begin_left(v)

    def begin_right(self, u):
        self.to_right[u] = self.mover.go(self.own(u), self.dst(self.pos, u, 1), self.right)

    def begin_left(self, u):
        self.to_left[u] = self.mover.go(self.own(u), self.dst(self.pos, u, -1), self.left)

    def pass_right(self, u):
        self.to_right[u].wait_recv()
        before = turn(self.pos, -1)
        self.far[u] = self.mover.go(self.dst(before, u, 1), self.dst(before, u, 2), self.right)

    def pass_left(self, u):
        self.to_left[u].wait_recv()
        after = turn(self.pos, 1)
        self.far[u] = self.mover.go(self.dst(after, u, -1), self.dst(after, u, 2), self.left)

    def onward(self):
        for u, v in zip(self.first, self.last):
            self.pass_right(u)
            self.pass_left(v)

    def near(self):
        for u in self.last:
            self.to_right[u].wait_recv()
        for v in self.first:
            self.to_left[v].wait_recv()

    def end(self):
        for copy in self.far.values():
            copy.wait_recv()


class Spread:
    def __init__(self, at, mover, full, width):
        self.at, self.mover, self.full = at, mover, full
        self.quarter, self.width = width // 4, width

    def begin(self, live_out, first):
        at = self.at
        rows = pl.ds(pl.multiple_of(at.c * 16, 16), 16)
        self.start = [
            self.mover.go(
                live_out.at[rows, pl.ds(first, self.width)],
                self.full.at[k - 1, at.y, at.x, at.core],
                at.up(turn(at.z, -k)),
            )
            for k in range(1, 4)
        ]

    def cols(self, u, n=1):
        return pl.ds(u * self.quarter, n * self.quarter)

    def phase_one(self):
        at, full = self.at, self.full
        for copy in self.start:
            copy.wait_recv()
        a = lambda pos, u, k=0: full.at[:, at.y, pos, at.core, :, self.cols(u)]
        b = lambda pos, u, k=0: full.at[:, pos, at.x, at.core, :, self.cols(u)]
        self.one = [
            Ring(self.mover, at.x, lambda p: at.chip(at.y, p), lambda u: a(at.x, u), a, [0, 1]),
            Ring(self.mover, at.y, lambda p: at.chip(p, at.x), lambda u: b(at.y, u), b, [2, 3]),
        ]

    def phase_one_onward(self):
        for ring in self.one:
            ring.onward()

    def phase_one_end(self):
        for ring in self.one:
            ring.near()
            ring.end()

    def line(self, full, axis):
        at = self.at
        if axis == "x":
            return full.at[:, at.y, :, at.core, :, self.cols(0, 2)]
        return full.at[:, :, at.x, at.core, :, self.cols(2, 2)]

    def phase_two(self):
        at, full = self.at, self.full
        a = lambda pos, u, k=0: full.at[:, pos, :, at.core, :, self.cols(u)]
        b = lambda pos, u, k=0: full.at[:, :, pos, at.core, :, self.cols(u)]
        self.two = [
            Ring(self.mover, at.y, lambda p: at.chip(p, at.x), lambda u: a(at.y, u), a, [0, 1]),
            Ring(self.mover, at.x, lambda p: at.chip(at.y, p), lambda u: b(at.x, u), b, [2, 3]),
        ]
        self.over = []
        self.cross(0)

    def cross(self, k):
        at, full = self.at, self.full
        a = full.at[:, turn(at.y, k), :, at.core, :, self.cols(0, 2)]
        b = full.at[:, :, turn(at.x, k), at.core, :, self.cols(2, 2)]
        for view in (a, b):
            self.over.append(self.mover.go(view, view, at.sibling()))

    def phase_two_onward(self):
        for ring in self.two:
            ring.onward()
        for ring in self.two:
            ring.near()
        self.cross(1)
        self.cross(-1)

    def finish(self):
        for ring in self.two:
            ring.end()
        self.cross(2)
        for copy in self.over:
            copy.wait_recv()


def norm_rows(rows, gain):
    wide = rows.astype(F32)
    inverse = lax.rsqrt(jnp.mean(wide * wide, axis=-1, keepdims=True) + EPSILON)
    return (wide * gain).astype(BF16), inverse


def fetch_kernel(
    question_ids, answer_ids, owner, slot, rel_bias, spread_of, memory, embedding, own_score,
    live_out, w_qkv, cross_kv, cross_query,
    live_gain, enc_gain, dec_gain,
    x_out, tokens, scores, full, full_next, proj_mem, proj_q, qg, w_val_out, bias,
    line_buf, score, by_key, every, table, turned, plan, tok, table_w, out_buf, in_buf0, in_buf1, in_buf2, in_buf3, own, pair_buf, a_buf, b_buf, a2_buf, b2_buf, tok_sum,
    x_full, weights, acc, squares, scaled, w_query, kv_buf, w_key, w_val,
    send, recv, a2a_send, a2a_recv, line_send, line_recv, local_sem, kv_sem, out_sem,
):
    at = Place()
    line_buf[...] = jnp.zeros((8, 128), jnp.int32)
    line_buf[0:1, 0:8] = owner[...]
    line_buf[0:1, 32:40] = slot[...]
    line_buf[1:2, 64:80] = question_ids[...]
    line_buf[1:2, 80:112] = answer_ids[...]
    placed = pltpu.roll(line_buf[0:1], 8 * at.z, 1)
    every[at.c, at.z] = placed + jnp.where(at.z == 0, line_buf[1:2], 0)
    score[...] = jnp.zeros((1, 128), F32)
    score[:, 0:8] = own_score[...]
    table[32:128] = jnp.zeros((96, 128), jnp.int32)
    load_table = pltpu.make_async_copy(embedding, table_w, local_sem.at[5])
    load_table.start()
    load_weights = [
        pltpu.make_async_copy(w_qkv.at[i], weights.at[i], local_sem.at[i]) for i in range(3)
    ] + [pltpu.make_async_copy(cross_query, w_query, local_sem.at[3])]
    for copy in load_weights:
        copy.start()

    def kv_copy(i):
        slot = lax.rem(i, 4)
        return pltpu.make_async_copy(
            cross_kv.at[pl.ds(i * 256, 256)], kv_buf.at[slot], kv_sem.at[slot]
        )

    for i in range(3):
        kv_copy(i).start()

    def split_kv(first, last):
        def one(i, carry):
            @pl.when(i < 13)
            def _():
                kv_copy(i + 3).start()

            kv_copy(i).wait()
            rows = pl.ds(pl.multiple_of(i * 256, 256), 256)
            slot = lax.rem(i, 4)
            w_key[rows] = kv_buf[slot, :, 0, :]
            gain = jnp.transpose(jnp.broadcast_to(enc_gain[:, rows], (128, 256)))[:, 0:1]
            w_val[rows] = (kv_buf[slot, :, 1, :].astype(F32) * gain).astype(BF16)
            return carry

        lax.fori_loop(first, last, one, 0)

    greet_all(at)
    mover = Mover(send, recv)
    in_buf = (in_buf0, in_buf1, in_buf2, in_buf3)

    spread = Spread(at, mover, full, 2048)
    spread.begin(live_out, 0)
    spread_next = Spread(at, mover, full_next, 2048)
    spread_next.begin(live_out, 2048)

    near = [
        mover.go(every.at[at.c, at.z], every.at[at.c, at.z], at.up(turn(at.z, k)))
        for k in range(1, 4)
    ]

    def line_copy(d):
        return pltpu.make_async_remote_copy(
            src_ref=every.at[at.c], dst_ref=every.at[at.c], send_sem=line_send.at[d],
            recv_sem=line_recv.at[d], device_id=at.cache(lax.rem(at.c + d, 32)),
            device_id_type=MESH,
        )

    def send_line(d, carry):
        line_copy(d).start()
        return carry

    def wait_line(d, carry):
        line_copy(d).wait()
        return carry

    for copy in near:
        copy.wait_recv()
    lax.fori_loop(1, 32, send_line, 0)
    split_kv(0, 4)
    spread.phase_one()
    spread_next.phase_one()
    split_kv(4, 6)

    by_bucket = jnp.dot(
        rel_bias[...], spread_of[...], precision=lax.Precision.HIGHEST, preferred_element_type=F32
    )
    for b in range(32):
        by_key[b] = by_bucket[:, 128 * b : 128 * b + 128]
    for h in range(8):
        bias[h] = by_key[:, h, :]
    lax.fori_loop(1, 32, wait_line, 0)
    for q in range(32):
        table[q : q + 1] = (every[q, 0] + every[q, 1]) + (every[q, 2] + every[q, 3])

    names = table[0:32]
    turned[...] = jnp.transpose(table[...].astype(F32))
    lane = lax.broadcasted_iota(jnp.int32, (32, 128), 1)
    rank = jnp.zeros((32, 128), jnp.int32)
    for shift in range(1, 32):
        same = jnp.logical_and(pltpu.roll(names, shift, 1) == names, lane >= shift)
        rank = rank + jnp.where(same, 1, 0)
    entries = pltpu.roll(names, 96, 1)
    found = []
    for r in range(2):
        hit = jnp.logical_and(jnp.logical_and(names == at.c, rank == r), lane < 32)
        entry = jnp.where(hit, entries, 0)
        for shift in (64, 32, 16, 8, 4, 2, 1):
            entry = entry + pltpu.roll(entry, shift, 1)
        found.append(entry)
    asks = jnp.where(lane == 32, found[0], found[1])
    table[0:32] = jnp.where(lane < 32, names * 2 + rank, asks)
    to_plan = pltpu.make_async_copy(table.at[pl.ds(0, 32)], plan, local_sem.at[6])
    to_plan.start()
    to_plan.wait()

    def passage_copy(h, d):
        q = lax.rem(at.c + d, 32)
        return pltpu.make_async_remote_copy(
            src_ref=out_buf.at[h, pl.ds(2 * q, 2)], dst_ref=in_buf[h].at[pl.ds(2 * at.c, 2)],
            send_sem=a2a_send.at[h, d], recv_sem=a2a_recv.at[h, d],
            device_id=at.cache(q), device_id_type=MESH,
        )

    def send_part(h):
        lanes = pl.ds(h * 256, 256)

        def one(d, carry):
            q = lax.rem(at.c + d, 32)
            if h > 0:
                passage_copy(h - 1, d).wait_send()
            out_buf[h, 2 * q] = memory[plan[q, 32], :, lanes]
            out_buf[h, 2 * q + 1] = memory[plan[q, 33], :, lanes]
            passage_copy(h, d).start()
            return carry

        lax.fori_loop(1, 32, one, 0)
        in_buf[h][2 * at.c] = memory[plan[at.c, 32], :, lanes]
        in_buf[h][2 * at.c + 1] = memory[plan[at.c, 33], :, lanes]

    def wait_part(h):
        def one(d, carry):
            passage_copy(h, d).wait_recv()
            return carry

        lax.fori_loop(1, 32, one, 0)

        def pack(j, carry):
            own[h, pl.ds(pl.multiple_of(16 * j, 16), 16)] = in_buf[h][plan[at.c, j]]
            return carry

        lax.fori_loop(0, 32, pack, 0)

    def lanes_of(pos, h):
        return pl.ds(pl.multiple_of(pos * 1024 + h * 512, 512), 512)

    def part(pos, unit, k=0):
        h, g = unit
        return x_full.at[
            pl.ds(g * 256, 256), pl.ds(pl.multiple_of(pos * 1024 + h * 256, 256), 256)
        ]

    def ring_part(h):
        return Ring(
            mover, at.z, at.up, lambda u: own.at[u[0], pl.ds(u[1] * 256, 256)], part,
            [(h, 0), (h, 1)],
        )

    stored = []

    def multiply(k, h):
        pos = turn(at.z, k)
        lanes = lanes_of(pos, h)
        if k == 0:
            x_full[:, lanes] = jnp.concatenate([own[2 * h], own[2 * h + 1]], axis=1)
        keep = pltpu.make_async_copy(
            x_full.at[:, lanes], x_out.at[:, lanes], out_sem.at[len(stored)]
        )
        keep.start()
        first = not stored
        stored.append(keep)
        gain = live_gain[:, lanes]
        for r in range(2):
            rows = pl.ds(r * 256, 256)
            wide = x_full[rows, lanes].astype(F32)
            scaled[rows] = (wide * gain).astype(BF16)
            square = jnp.sum(wide * wide, axis=1, keepdims=True)
            squares[rows] = square if first else squares[rows] + square

        def one(i, carry):
            product = jnp.dot(scaled[...], weights[i, lanes], preferred_element_type=F32)
            acc[i] = product if first else acc[i] + product
            return carry

        lax.fori_loop(0, 3, one, 0)

    def sent_part(h):
        def one(d, carry):
            passage_copy(h, d).wait_send()
            return carry

        lax.fori_loop(1, 32, one, 0)

    send_part(0)

    load_table.wait()
    held = lax.broadcasted_iota(jnp.int32, (48, 1004), 1).astype(F32) + (at.c * 1004).astype(F32)
    for b in range(8):
        picks = [
            jnp.where(held == turned[64:112, q : q + 1], 1.0, 0.0).astype(BF16)
            for q in range(4 * b, 4 * b + 4)
        ]
        named = jnp.dot(
            jnp.concatenate(picks, axis=0), table_w[...], preferred_element_type=F32
        ).astype(BF16)
        for n in range(4):
            q = 4 * b + n
            tok[q // 8, (q // 2) % 4, q % 2] = named[48 * n : 48 * (n + 1)]
    other = 1 - at.core
    pair = mover.go(tok.at[:, :, other], pair_buf, at.sibling())
    spread.phase_one_onward()
    spread_next.phase_one_onward()
    send_part(1)

    pair.wait_recv()

    def add_pair(y, carry):
        for x in range(4):
            pair_buf[y, x] = pair_buf[y, x] + tok[y, x, at.core]
        return carry

    lax.fori_loop(0, 4, add_pair, 0)
    wait_part(0)
    rings = [ring_part(0)]
    send_part(2)
    wait_part(1)
    rings.append(ring_part(1))
    for copy in load_weights:
        copy.wait()
    multiply(0, 0)
    send_part(3)
    lo, hi = pl.ds(0, 512), pl.ds(512, 512)
    tok_a = [
        mover.go(
            pair_buf.at[:, turn(at.x, k), :, lo], a_buf.at[k - 1], at.chip(at.y, turn(at.x, k))
        )
        for k in range(1, 4)
    ]
    tok_b = [
        mover.go(
            pair_buf.at[turn(at.y, k), :, :, hi], b_buf.at[k - 1], at.chip(turn(at.y, k), at.x)
        )
        for k in range(1, 4)
    ]
    near_scores = [
        mover.go(score, scores.at[at.z], at.up(turn(at.z, k))) for k in range(1, 4)
    ]
    scores[at.z] = score[...]
    wait_part(2)
    rings.append(ring_part(2))
    rings[0].onward()
    wait_part(3)
    rings.append(ring_part(3))
    spread.phase_one_end()
    spread_next.phase_one_end()
    multiply(0, 1)
    rings[1].onward()
    for copy in tok_a + tok_b:
        copy.wait_recv()

    def add_line(i, carry):
        a_buf[0, i] = (a_buf[0, i] + a_buf[1, i]) + (a_buf[2, i] + pair_buf[i, at.x, :, lo])
        b_buf[0, i] = (b_buf[0, i] + b_buf[1, i]) + (b_buf[2, i] + pair_buf[at.y, i, :, hi])
        return carry

    lax.fori_loop(0, 4, add_line, 0)
    tok_a2 = [
        mover.go(a_buf.at[0, turn(at.y, k)], a2_buf.at[k - 1], at.chip(turn(at.y, k), at.x))
        for k in range(1, 4)
    ]
    tok_b2 = [
        mover.go(b_buf.at[0, turn(at.x, k)], b2_buf.at[k - 1], at.chip(at.y, turn(at.x, k)))
        for k in range(1, 4)
    ]
    spread.phase_two()
    split_kv(6, 9)
    rings[0].near()
    rings[1].near()
    multiply(1, 0)
    multiply(-1, 0)
    rings[2].onward()
    for copy in tok_a2 + tok_b2:
        copy.wait_recv()
    tok_sum[:, lo] = (a2_buf[0] + a2_buf[1]) + (a2_buf[2] + a_buf[0, at.y])
    tok_sum[:, hi] = (b2_buf[0] + b2_buf[1]) + (b2_buf[2] + b_buf[0, at.x])
    mine = pl.ds(pl.multiple_of(at.z * 1024, 1024), 1024)
    near_tokens = [
        mover.go(tok_sum, tokens.at[:, mine], at.up(turn(at.z, k))) for k in range(1, 4)
    ]
    tokens[:, mine] = tok_sum[...]
    rings[0].end()
    rings[1].end()
    multiply(2, 0)
    rings[3].onward()
    split_kv(9, 13)
    spread.phase_two_onward()
    split_kv(13, 16)
    keep_values = pltpu.make_async_copy(w_val, w_val_out, local_sem.at[4])
    keep_values.start()
    for copy in near_scores + near_tokens:
        copy.wait_recv()

    rows, inverse = norm_rows(tokens[0:16], live_gain[...])

    def project(i, carry):
        total = jnp.dot(rows, weights[i], preferred_element_type=F32)
        proj_q[i] = (total * inverse).astype(BF16)
        return carry

    lax.fori_loop(0, 3, project, 0)
    rows_a, inverse_a = norm_rows(tokens[16:48], dec_gain[...])
    queries = jnp.dot(rows_a, w_query[...], preferred_element_type=F32) * inverse_a
    head = lax.broadcasted_iota(jnp.int32, (32, 512), 1) // HEAD
    for h in range(8):
        scaled[pl.ds(32 * h, 32)] = jnp.where(head == h, queries, 0.0).astype(BF16)

    def fold(n, carry):
        cols = pl.ds(pl.multiple_of(n * 1024, 1024), 1024)
        product = dot32(scaled[pl.ds(0, 256)], w_key[cols], ((1,), (1,)))
        qg[:, cols] = (product * enc_gain[:, cols]).astype(BF16)
        return carry

    lax.fori_loop(0, 4, fold, 0)
    rings[2].near()
    rings[3].near()
    multiply(1, 1)
    multiply(-1, 1)
    rings[2].end()
    rings[3].end()
    multiply(2, 1)
    inverse_m = lax.rsqrt(squares[...] * (1.0 / 4096) + EPSILON)

    def close(i, carry):
        proj_mem[i] = (acc[i] * inverse_m).astype(BF16)
        return carry

    lax.fori_loop(0, 3, close, 0)
    spread.finish()
    for copy in stored:
        copy.wait()
    keep_values.wait()
    mover.finish_sends()

    sent_part(3)


def fetch(*args):
    return pl.pallas_call(
        fetch_kernel,
        out_shape=(
            jax.ShapeDtypeStruct((512, 4096), BF16),
            jax.ShapeDtypeStruct((48, 4096), BF16),
            jax.ShapeDtypeStruct((4, 1, 128), F32),
            jax.ShapeDtypeStruct((3, 4, 4, 2, 16, 2048), BF16),
            jax.ShapeDtypeStruct((3, 4, 4, 2, 16, 2048), BF16),
            jax.ShapeDtypeStruct((3, 512, 512), BF16),
            jax.ShapeDtypeStruct((3, 16, 512), BF16),
            jax.ShapeDtypeStruct((256, 4096), BF16),
            jax.ShapeDtypeStruct((4096, 512), BF16),
            jax.ShapeDtypeStruct((8, 32, 128), F32),
        ),
        in_specs=[VM] * 7 + [ANY, VM, ANY, ANY, ANY, ANY, VM, VM, VM],
        out_specs=(ANY, VM, VM, ANY, ANY, VM, VM, VM, ANY, VM),
        scratch_shapes=[
            pltpu.VMEM((8, 128), jnp.int32), pltpu.VMEM((1, 128), F32),
            pltpu.VMEM((32, 8, 128), F32),
            pltpu.VMEM((32, 4, 1, 128), jnp.int32), pltpu.VMEM((128, 128), jnp.int32),
            pltpu.VMEM((128, 128), F32), pltpu.SMEM((32, 128), jnp.int32),
            pltpu.VMEM((4, 4, 2, 48, 1024), BF16), pltpu.VMEM((1004, 1024), BF16),
            pltpu.VMEM((4, 64, 16, 256), BF16), pltpu.VMEM((64, 16, 256), BF16),
            pltpu.VMEM((64, 16, 256), BF16), pltpu.VMEM((64, 16, 256), BF16),
            pltpu.VMEM((64, 16, 256), BF16),
            pltpu.VMEM((4, 512, 256), BF16), pltpu.VMEM((4, 4, 48, 1024), BF16),
            pltpu.VMEM((3, 4, 48, 512), BF16), pltpu.VMEM((3, 4, 48, 512), BF16),
            pltpu.VMEM((3, 48, 512), BF16), pltpu.VMEM((3, 48, 512), BF16),
            pltpu.VMEM((48, 1024), BF16),
            pltpu.VMEM((512, 4096), BF16), pltpu.VMEM((3, 4096, 512), BF16),
            pltpu.VMEM((3, 512, 512), F32), pltpu.VMEM((512, 1), F32),
            pltpu.VMEM((512, 512), BF16), pltpu.VMEM((4096, 512), BF16),
            pltpu.VMEM((4, 256, 2, 512), BF16), pltpu.VMEM((4096, 512), BF16),
            pltpu.VMEM((4096, 512), BF16),
            pltpu.SemaphoreType.DMA((112,)), pltpu.SemaphoreType.DMA((112,)),
            pltpu.SemaphoreType.DMA((4, 32)), pltpu.SemaphoreType.DMA((4, 32)),
            pltpu.SemaphoreType.DMA((32,)), pltpu.SemaphoreType.DMA((32,)),
            pltpu.SemaphoreType.DMA((7,)), pltpu.SemaphoreType.DMA((4,)),
            pltpu.SemaphoreType.DMA((8,)),
        ],
        compiler_params=params(2, 60),
    )(*args)


def reader_kernel(
    proj_mem, proj_q, bias, x_mem, tokens, qg, scores, left_in, right_in, live_out, w_val_in,
    cross_out_in,
    encoded_out, decoded,
    encoded, ctx, others, x_seq, left, right, own_out, w_val, w_out, ql, ql_part, lv, lv_part, s, w, values,
    inv, parts, part_buf, send, recv, local_sem,
):
    at = Place()
    mover = Mover(send, recv)
    spread = Spread(at, mover, right, 2048)
    loads = [
        pltpu.make_async_copy(a, b, local_sem.at[i])
        for i, (a, b) in enumerate([
            (spread.line(right_in, "x"), spread.line(right, "x")),
            (spread.line(right_in, "y"), spread.line(right, "y")),
            (x_mem, x_seq.at[:, pl.ds(0, 16)]), (live_out, own_out), (w_val_in, w_val),
            (left_in, left), (cross_out_in, w_out),
        ])
    ]
    for copy in loads:
        copy.start()
    greet_all(at)
    scale = HEAD ** (-0.5)
    nt = ((1,), (1,))
    def chunk(j):
        return pl.ds(pl.multiple_of(j * 256, 256), 256)

    def part(pos, u, k):
        return others.at[{1: 2, -1: 0, 2: 1}[k], chunk(turn(pos, u))]

    ring = Ring(
        mover, at.z, at.up, lambda u: ctx.at[chunk(turn(at.z, u))], part, [2, 1, 3, 0], False
    )

    low = lax.broadcasted_iota(jnp.int32, (128, 128), 1) < HEAD
    owner_lane = lax.broadcasted_iota(jnp.int32, (32, 256), 1) // 32 % 4

    def attend(j):
        def group(g, carry):
            first = j * 8 + g * 4

            def pair(i, p):
                lanes = pl.ds(128 * p, 128)
                pieces = []
                for n in range(4):
                    pieces.append(
                        proj_mem[i, pl.ds(pl.multiple_of((first + n) * 16, 16), 16), lanes]
                    )
                    pieces.append(proj_q[i, :, lanes])
                return jnp.concatenate(pieces, axis=0)

            for p in range(4):
                q, k, v = pair(0, p), pair(1, p), pair(2, p)
                none = jnp.zeros_like(q)
                both = jnp.concatenate([jnp.where(low, q, none), jnp.where(low, none, q)], axis=0)
                full = dot32(k, both, nt)
                sc = full[0:32]
                for n in range(1, 4):
                    sc = jnp.where(owner_lane == n, full[32 * n : 32 * n + 32], sc)
                sc = sc * scale + jnp.concatenate([bias[2 * p], bias[2 * p + 1]], axis=1)
                ex = jnp.exp(sc - jnp.max(sc, axis=0, keepdims=True))
                ex = ex * (1.0 / jnp.sum(ex, axis=0, keepdims=True))
                full = jnp.concatenate(
                    [jnp.where(owner_lane == n, ex, 0.0) for n in range(4)], axis=0
                ).astype(BF16)
                out = dot32(full, v, ((0,), (0,)))
                ctx[pl.ds(pl.multiple_of(first * 32, 128), 128), pl.ds(128 * p, 128)] = jnp.where(
                    low, out[0:128], out[128:256]
                ).astype(BF16)
            return carry

        lax.fori_loop(0, 2, group, 0)

    for u in (2, 3, 1, 0):
        attend(turn(at.z, u))
        ring.begin_right(u)
        ring.begin_left(u)
        if u == 2:
            loads[0].wait()
            loads[1].wait()
            spread.phase_two()

    loads[2].wait()

    def fill(p, carry):
        x_seq[p, pl.ds(16, 16)] = tokens[pl.ds(0, 16)]
        return carry

    lax.fori_loop(0, 32, fill, 0)

    def rows_of(j):
        return x_seq[pl.ds(j * 8, 8)].reshape(256, 4096)

    def score_inputs(j, carry):
        s[j] = dot32(qg[...], rows_of(j), nt)
        return carry

    lax.fori_loop(0, 4, score_inputs, 0)
    loads[4].wait()
    of_question = jnp.dot(tokens[pl.ds(0, 16)], w_val[...], preferred_element_type=F32)

    def value_inputs(j, carry):
        rows = jnp.dot(
            x_seq[pl.ds(j * 8, 8), pl.ds(0, 16)].reshape(128, 4096), w_val[...],
            preferred_element_type=F32,
        )
        for p in range(8):
            values[j, pl.ds(32 * p, 16)] = rows[16 * p : 16 * p + 16]
            values[j, pl.ds(32 * p + 16, 16)] = of_question
        return carry

    lax.fori_loop(0, 4, value_inputs, 0)
    loads[3].wait()
    ql[0] = dot32(qg[...], own_out[...], nt).astype(BF16)
    lv[0] = jnp.dot(own_out[...], w_val[...], preferred_element_type=F32).astype(BF16)

    def absorb(j, k, rows):
        s[j] = s[j] + dot32(ql[k], rows, nt)
        values[j] = values[j] + jnp.dot(rows, lv[k], preferred_element_type=F32)

    def absorb_own(j, carry):
        absorb(j, 0, ctx[chunk(j)])
        return carry

    lax.fori_loop(0, 4, absorb_own, 0)
    spread.phase_two_onward()
    loads[5].wait()
    half, rest = pl.ds(0, 2048), pl.ds(2048, 2048)

    def fold_left(k, carry):
        ql_part[k] = dot32(qg[:, half], left[k], nt)
        lv_part[k] = jnp.dot(left[k], w_val[half], preferred_element_type=F32)
        return carry

    lax.fori_loop(0, 3, fold_left, 0)
    ring.pass_right(2)
    ring.pass_left(3)
    ring.pass_right(1)
    spread.finish()

    def fold_right(k, carry):
        rows = right[k].reshape(512, 2048)
        ql[k + 1] = (ql_part[k] + dot32(qg[:, rest], rows, nt)).astype(BF16)
        lv[k + 1] = (
            lv_part[k] + jnp.dot(rows, w_val[rest], preferred_element_type=F32)
        ).astype(BF16)
        return carry

    lax.fori_loop(0, 3, fold_right, 0)

    ring.pass_left(0)

    ring.far[2].wait_recv()
    mine = chunk(at.z)

    def group_rows(k, n):
        if k == 0:
            return own_out[:, pl.ds(n * 1024, 1024)]
        if n < 2:
            return left[k - 1, :, pl.ds(n * 1024, 1024)]
        return right[k - 1, :, :, :, :, pl.ds((n - 2) * 1024, 1024)].reshape(512, 1024)

    squares = jnp.zeros((256, 1), F32)
    for n in range(4):
        cols = pl.ds(n * 1024, 1024)
        attended = None
        for k in range(4):
            rows = ctx[mine] if k == 0 else others[k - 1, mine]
            product = jnp.dot(rows, group_rows(k, n), preferred_element_type=F32)
            product = product.astype(BF16).astype(F32)
            attended = product if k == 0 else attended + product
        own_rows = x_seq[pl.ds(at.z * 8, 8), :, cols].reshape(256, 1024).astype(F32)
        own_rows = (own_rows + attended).astype(BF16)
        encoded[:, cols] = own_rows
        own_rows = own_rows.astype(F32)
        squares = squares + jnp.sum(own_rows * own_rows, axis=1, keepdims=True)
    keep = pltpu.make_async_copy(encoded, encoded_out, local_sem.at[7])
    keep.start()
    norm = lax.rsqrt(squares * (1.0 / 4096) + EPSILON)
    inv[at.z] = jnp.transpose(jnp.broadcast_to(norm, (256, 128)))[0:1]
    near = [mover.go(inv.at[at.z], inv.at[at.z], at.up(turn(at.z, k))) for k in range(1, 4)]

    def absorb_other(k, u):
        j = turn(at.z, k + u)
        absorb(j, k, others[k - 1, chunk(j)])

    absorb_other(3, 2)
    absorb_other(1, 3)
    absorb_other(3, 1)
    absorb_other(2, 2)
    ring.to_left[2].wait_recv()
    absorb_other(1, 2)
    ring.to_right[3].wait_recv()
    absorb_other(3, 3)
    ring.to_left[1].wait_recv()
    absorb_other(1, 1)
    absorb_other(1, 0)
    ring.far[3].wait_recv()
    absorb_other(2, 3)
    ring.to_right[0].wait_recv()
    absorb_other(3, 0)
    ring.far[1].wait_recv()
    absorb_other(2, 1)
    ring.far[0].wait_recv()
    absorb_other(2, 0)
    for copy in near:
        copy.wait_recv()

    passage = lax.broadcasted_iota(jnp.int32, (1, 256), 1) // 32
    top = None
    for j in range(4):
        row = jnp.zeros((1, 256), F32)
        line = scores[j]
        for p in range(8):
            row = row + jnp.where(passage == p, line[:, p : p + 1], 0.0)
        total = s[j] * (inv[j] * scale) + row
        s[j] = total
        here = jnp.max(total, axis=1, keepdims=True)
        top = here if top is None else jnp.maximum(top, here)
    sums = jnp.zeros((256, 1), F32)
    for j in range(4):
        ex = jnp.exp(s[j] - top)
        s[j] = ex
        sums = sums + jnp.sum(ex, axis=1, keepdims=True)
    for j in range(4):
        w[j] = (s[j] * inv[j] / sums).astype(BF16)
    heads_out = jnp.zeros((256, 512), F32)
    for j in range(4):
        heads_out = heads_out + jnp.dot(
            w[j], values[j].astype(BF16), preferred_element_type=F32
        )
    head = lax.broadcasted_iota(jnp.int32, (32, 512), 1) // HEAD
    context = jnp.zeros((32, 512), F32)
    for h in range(8):
        context = context + jnp.where(head == h, heads_out[32 * h : 32 * h + 32], 0.0)
    context = context.astype(BF16)
    loads[6].wait()
    for j in range(4):
        parts[j] = jnp.dot(
            context, w_out[:, pl.ds(1024 * j, 1024)], preferred_element_type=F32
        ).astype(BF16)
    last = [
        mover.go(parts.at[turn(at.z, k)], part_buf.at[k - 1], at.up(turn(at.z, k)))
        for k in range(1, 4)
    ]
    for copy in last:
        copy.wait_recv()
    total = parts[at.z].astype(F32)
    for k in range(3):
        total = total + part_buf[k].astype(F32)
    decoded[...] = total.astype(BF16)
    keep.wait()
    mover.finish_sends()


def reader(*args):
    return pl.pallas_call(
        reader_kernel,
        out_shape=(
            jax.ShapeDtypeStruct((256, 4096), BF16),
            jax.ShapeDtypeStruct((32, 1024), BF16),
        ),
        in_specs=[VM, VM, VM, ANY, VM, VM, VM, ANY, ANY, ANY, ANY, ANY],
        out_specs=(ANY, VM),
        scratch_shapes=[
            pltpu.VMEM((256, 4096), BF16),
            pltpu.VMEM((1024, 512), BF16), pltpu.VMEM((3, 1024, 512), BF16),
            pltpu.VMEM((32, 32, 4096), BF16), pltpu.VMEM((3, 512, 2048), BF16),
            pltpu.VMEM((3, 4, 4, 2, 16, 2048), BF16), pltpu.VMEM((512, 4096), BF16),
            pltpu.VMEM((4096, 512), BF16), pltpu.VMEM((512, 4096), BF16),
            pltpu.VMEM((4, 256, 512), BF16), pltpu.VMEM((3, 256, 512), F32),
            pltpu.VMEM((4, 512, 512), BF16), pltpu.VMEM((3, 512, 512), F32),
            pltpu.VMEM((4, 256, 256), F32), pltpu.VMEM((4, 256, 256), BF16),
            pltpu.VMEM((4, 256, 512), F32), pltpu.VMEM((4, 1, 256), F32),
            pltpu.VMEM((4, 32, 1024), BF16), pltpu.VMEM((3, 32, 1024), BF16),
            pltpu.SemaphoreType.DMA((64,)), pltpu.SemaphoreType.DMA((64,)),
            pltpu.SemaphoreType.DMA((8,)),
        ],
        compiler_params=params(3, 60),
    )(*args)


def shards(
    question_ids, answer_ids, owner, slot, passage_score, memory, embedding, live_gain, live_qkv,
    rel_bias, live_out, enc_gain, cross_kv, dec_gain, cross_query, cross_out,
):
    n_psg = lax.axis_size("psg")
    width = live_gain.shape[0]
    plen = memory.shape[1]
    qlen = question_ids.shape[1]
    own_count = owner.shape[1]
    total = own_count * n_psg
    seq = plen + qlen
    cols = live_out.shape[0]

    spread_of = jnp.asarray(spread_table(seq, rel_bias.shape[1]))
    x_mem, token_full, scores, left, right, proj_mem, proj_q, qg, w_val, bias = fetch(
        question_ids, answer_ids, owner.reshape(1, own_count), slot, rel_bias, spread_of, memory,
        embedding, passage_score, live_out,
        jnp.transpose(live_qkv, (1, 0, 2)), cross_kv, cross_query,
        live_gain.reshape(1, width), enc_gain.reshape(1, width), dec_gain.reshape(1, width),
    )
    encoded, decoded = reader(
        proj_mem, proj_q, bias, x_mem.reshape(total, plen, width), token_full, qg, scores,
        left.reshape(3, cols, width // 2), right, live_out, w_val, cross_out,
    )
    return encoded.reshape(1, own_count, seq, width), decoded[None]


def solution(mesh):
    return jax.shard_map(
        shards,
        mesh=mesh,
        in_specs=(
            P("cache", None), P("cache", None), P("cache", "psg", None), P("cache", "psg"),
            P("cache", "psg"), P("cache", None, "psg"), P("cache", "psg"), P(),
            P(None, None, "psg"), P("psg", None), P("psg", None), P(), P(None, None, "psg"), P(),
            P(None, "psg"), P("psg", None),
        ),
        out_specs=(P("cache", "psg", None, None), P("cache", None, "psg")),
        check_vma=False,
    )
```

```python
import functools

import jax
import jax.numpy as jnp
import numpy as np
from jax import lax
from jax.experimental import pallas as pl
from jax.experimental.pallas import tpu as pltpu
from jax.sharding import PartitionSpec as P

HEAD = 64
EPSILON = 1e-06
F32 = jnp.float32
BF16 = jnp.bfloat16


def bucket_table(length, bucket_count):
    positions = np.arange(length)
    relative = positions[None, :] - positions[:, None]
    halfway = bucket_count // 2
    exact_span = halfway // 2
    upper_side = (relative > 0).astype(np.int64) * halfway
    distance = np.abs(relative)
    log_bucket = exact_span + (
        np.log(np.maximum(distance, 1) / exact_span)
        / np.log(128.0 / exact_span)
        * (halfway - exact_span)
    ).astype(np.int64)
    log_bucket = np.minimum(log_bucket, halfway - 1)
    return upper_side + np.where(distance < exact_span, distance, log_bucket)


def spread_table(length, bucket_count):
    buckets = np.tile(bucket_table(length, bucket_count).T, (1, 4)).reshape(-1)
    return (buckets[None, :] == np.arange(bucket_count)[:, None]).astype(np.float32)


def dot32(a, b, dims):
    return lax.dot_general(a, b, (dims, ((), ())), preferred_element_type=F32)


MESH = pl.DeviceIdType.MESH
VM = pl.BlockSpec(memory_space=pltpu.VMEM)
SM = pl.BlockSpec(memory_space=pltpu.SMEM)
ANY = pl.BlockSpec(memory_space=pl.ANY)


def params(collective_id, mib):
    return pltpu.CompilerParams(
        collective_id=collective_id, has_side_effects=True, vmem_limit_bytes=mib << 20
    )


class Place:
    def __init__(self):
        self.c = lax.axis_index("cache")
        self.z = lax.axis_index("psg")
        self.core = lax.rem(self.c, 2)
        self.x = lax.rem(lax.div(self.c, 2), 4)
        self.y = lax.div(self.c, 8)

    def cache(self, c):
        return {"cache": c, "psg": self.z}

    def chip(self, y, x):
        return self.cache((y * 4 + x) * 2 + self.core)

    def sibling(self):
        return self.cache(self.c + 1 - 2 * self.core)

    def up(self, z):
        return {"cache": self.c, "psg": z}


def turn(p, k):
    return lax.rem(p + k + 4, 4)


def greet_all(at):
    barrier = pltpu.get_barrier_semaphore()

    def greet(d, carry):
        pl.semaphore_signal(
            barrier, inc=1, device_id=at.cache(lax.rem(at.c + d, 32)), device_id_type=MESH
        )
        return carry

    lax.fori_loop(1, 32, greet, 0)
    for k in range(1, 4):
        pl.semaphore_signal(barrier, inc=1, device_id=at.up(turn(at.z, k)), device_id_type=MESH)
    pl.semaphore_wait(barrier, 34)


class Mover:
    def __init__(self, send, recv):
        self.send, self.recv, self.count, self.started = send, recv, 0, []

    def go(self, src, dst, device):
        i = self.count
        self.count += 1
        copy = pltpu.make_async_remote_copy(
            src_ref=src, dst_ref=dst, send_sem=self.send.at[i], recv_sem=self.recv.at[i],
            device_id=device, device_id_type=MESH,
        )
        copy.start()
        self.started.append(copy)
        return copy

    def finish_sends(self):
        for copy in self.started:
            copy.wait_send()


class Ring:
    def __init__(self, mover, pos, device, own, dst, units, start=True):
        self.mover, self.pos, self.device, self.own, self.dst = mover, pos, device, own, dst
        self.right, self.left = device(turn(pos, 1)), device(turn(pos, -1))
        self.to_right, self.to_left, self.far = {}, {}, {}
        half = len(units) // 2
        self.first, self.last = units[:half], units[half:]
        if start:
            for u, v in zip(units, self.last + self.first):
                self.begin_right(u)
                self.begin_left(v)

    def begin_right(self, u):
        self.to_right[u] = self.mover.go(self.own(u), self.dst(self.pos, u, 1), self.right)

    def begin_left(self, u):
        self.to_left[u] = self.mover.go(self.own(u), self.dst(self.pos, u, -1), self.left)

    def pass_right(self, u):
        self.to_right[u].wait_recv()
        before = turn(self.pos, -1)
        self.far[u] = self.mover.go(self.dst(before, u, 1), self.dst(before, u, 2), self.right)

    def pass_left(self, u):
        self.to_left[u].wait_recv()
        after = turn(self.pos, 1)
        self.far[u] = self.mover.go(self.dst(after, u, -1), self.dst(after, u, 2), self.left)

    def onward(self):
        for u, v in zip(self.first, self.last):
            self.pass_right(u)
            self.pass_left(v)

    def near(self):
        for u in self.last:
            self.to_right[u].wait_recv()
        for v in self.first:
            self.to_left[v].wait_recv()

    def end(self):
        for copy in self.far.values():
            copy.wait_recv()


class Spread:
    def __init__(self, at, mover, full, width):
        self.at, self.mover, self.full = at, mover, full
        self.quarter, self.width = width // 4, width

    def begin(self, live_out, first):
        at = self.at
        rows = pl.ds(pl.multiple_of(at.c * 16, 16), 16)
        self.start = [
            self.mover.go(
                live_out.at[rows, pl.ds(first, self.width)],
                self.full.at[k - 1, at.y, at.x, at.core],
                at.up(turn(at.z, -k)),
            )
            for k in range(1, 4)
        ]

    def cols(self, u, n=1):
        return pl.ds(u * self.quarter, n * self.quarter)

    def phase_one(self):
        at, full = self.at, self.full
        for copy in self.start:
            copy.wait_recv()
        a = lambda pos, u, k=0: full.at[:, at.y, pos, at.core, :, self.cols(u)]
        b = lambda pos, u, k=0: full.at[:, pos, at.x, at.core, :, self.cols(u)]
        self.one = [
            Ring(self.mover, at.x, lambda p: at.chip(at.y, p), lambda u: a(at.x, u), a, [0, 1]),
            Ring(self.mover, at.y, lambda p: at.chip(p, at.x), lambda u: b(at.y, u), b, [2, 3]),
        ]

    def phase_one_onward(self):
        for ring in self.one:
            ring.onward()

    def phase_one_end(self):
        for ring in self.one:
            ring.near()
            ring.end()

    def line(self, full, axis):
        at = self.at
        if axis == "x":
            return full.at[:, at.y, :, at.core, :, self.cols(0, 2)]
        return full.at[:, :, at.x, at.core, :, self.cols(2, 2)]

    def phase_two(self):
        at, full = self.at, self.full
        a = lambda pos, u, k=0: full.at[:, pos, :, at.core, :, self.cols(u)]
        b = lambda pos, u, k=0: full.at[:, :, pos, at.core, :, self.cols(u)]
        self.two = [
            Ring(self.mover, at.y, lambda p: at.chip(p, at.x), lambda u: a(at.y, u), a, [0, 1]),
            Ring(self.mover, at.x, lambda p: at.chip(at.y, p), lambda u: b(at.x, u), b, [2, 3]),
        ]
        self.over = []
        self.cross(0)

    def cross(self, k):
        at, full = self.at, self.full
        a = full.at[:, turn(at.y, k), :, at.core, :, self.cols(0, 2)]
        b = full.at[:, :, turn(at.x, k), at.core, :, self.cols(2, 2)]
        for view in (a, b):
            self.over.append(self.mover.go(view, view, at.sibling()))

    def phase_two_onward(self):
        for ring in self.two:
            ring.onward()
        for ring in self.two:
            ring.near()
        self.cross(1)
        self.cross(-1)

    def finish(self):
        for ring in self.two:
            ring.end()
        self.cross(2)
        for copy in self.over:
            copy.wait_recv()


def norm_rows(rows, gain):
    wide = rows.astype(F32)
    inverse = lax.rsqrt(jnp.mean(wide * wide, axis=-1, keepdims=True) + EPSILON)
    return (wide * gain).astype(BF16), inverse


def fetch_kernel(
    question_ids, answer_ids, owner, slot, rel_bias, spread_of, memory, embedding, own_score,
    live_out, w_qkv, cross_kv, cross_query,
    live_gain, enc_gain, dec_gain,
    x_out, tokens, scores, full, full_next, proj_mem, proj_q, qg_out, w_val_out, bias,
    line_buf, score, by_key, every, table, turned, plan, tok, table_w, out_buf, in_buf0, in_buf1, in_buf2, in_buf3, own, pair_buf, a_buf, b_buf, a2_buf, b2_buf, tok_sum,
    qg, x_full, weights, acc, squares, scaled, w_query, kv_buf, w_key, w_val,
    send, recv, a2a_send, a2a_recv, line_send, line_recv, local_sem, kv_sem, out_sem,
):
    at = Place()
    line_buf[...] = jnp.zeros((8, 128), jnp.int32)
    line_buf[0:1, 0:8] = owner[...]
    line_buf[0:1, 32:40] = slot[...]
    line_buf[1:2, 64:80] = question_ids[...]
    line_buf[1:2, 80:112] = answer_ids[...]
    placed = pltpu.roll(line_buf[0:1], 8 * at.z, 1)
    every[at.c, at.z] = placed + jnp.where(at.z == 0, line_buf[1:2], 0)
    score[...] = jnp.zeros((1, 128), F32)
    score[:, 0:8] = own_score[...]
    table[32:128] = jnp.zeros((96, 128), jnp.int32)
    load_table = pltpu.make_async_copy(embedding, table_w, local_sem.at[5])
    load_table.start()
    load_weights = [
        pltpu.make_async_copy(w_qkv.at[i], weights.at[i], local_sem.at[i]) for i in range(3)
    ] + [pltpu.make_async_copy(cross_query, w_query, local_sem.at[3])]
    for copy in load_weights:
        copy.start()

    def kv_copy(i):
        slot = lax.rem(i, 4)
        return pltpu.make_async_copy(
            cross_kv.at[pl.ds(i * 256, 256)], kv_buf.at[slot], kv_sem.at[slot]
        )

    for i in range(3):
        kv_copy(i).start()

    def split_kv(first, last):
        def one(i, carry):
            @pl.when(i < 13)
            def _():
                kv_copy(i + 3).start()

            kv_copy(i).wait()
            rows = pl.ds(pl.multiple_of(i * 256, 256), 256)
            slot = lax.rem(i, 4)
            w_key[rows] = kv_buf[slot, :, 0, :]
            gain = jnp.transpose(jnp.broadcast_to(enc_gain[:, rows], (128, 256)))[:, 0:1]
            w_val[rows] = (kv_buf[slot, :, 1, :].astype(F32) * gain).astype(BF16)
            return carry

        lax.fori_loop(first, last, one, 0)

    greet_all(at)
    mover = Mover(send, recv)
    in_buf = (in_buf0, in_buf1, in_buf2, in_buf3)

    spread = Spread(at, mover, full, 2048)
    spread.begin(live_out, 0)
    spread_next = Spread(at, mover, full_next, 2048)
    spread_next.begin(live_out, 2048)

    near = [
        mover.go(every.at[at.c, at.z], every.at[at.c, at.z], at.up(turn(at.z, k)))
        for k in range(1, 4)
    ]

    def line_copy(d):
        return pltpu.make_async_remote_copy(
            src_ref=every.at[at.c], dst_ref=every.at[at.c], send_sem=line_send.at[d],
            recv_sem=line_recv.at[d], device_id=at.cache(lax.rem(at.c + d, 32)),
            device_id_type=MESH,
        )

    def send_line(d, carry):
        line_copy(d).start()
        return carry

    def wait_line(d, carry):
        line_copy(d).wait()
        return carry

    for copy in near:
        copy.wait_recv()
    lax.fori_loop(1, 32, send_line, 0)
    split_kv(0, 4)
    spread.phase_one()
    spread_next.phase_one()
    split_kv(4, 6)

    by_bucket = jnp.dot(
        rel_bias[...], spread_of[...], precision=lax.Precision.HIGHEST, preferred_element_type=F32
    )
    for b in range(32):
        by_key[b] = by_bucket[:, 128 * b : 128 * b + 128]
    for h in range(8):
        bias[h] = by_key[:, h, :]
    lax.fori_loop(1, 32, wait_line, 0)
    for q in range(32):
        table[q : q + 1] = (every[q, 0] + every[q, 1]) + (every[q, 2] + every[q, 3])

    names = table[0:32]
    turned[...] = jnp.transpose(table[...].astype(F32))
    lane = lax.broadcasted_iota(jnp.int32, (32, 128), 1)
    rank = jnp.zeros((32, 128), jnp.int32)
    for shift in range(1, 32):
        same = jnp.logical_and(pltpu.roll(names, shift, 1) == names, lane >= shift)
        rank = rank + jnp.where(same, 1, 0)
    entries = pltpu.roll(names, 96, 1)
    found = []
    for r in range(2):
        hit = jnp.logical_and(jnp.logical_and(names == at.c, rank == r), lane < 32)
        entry = jnp.where(hit, entries, 0)
        for shift in (64, 32, 16, 8, 4, 2, 1):
            entry = entry + pltpu.roll(entry, shift, 1)
        found.append(entry)
    asks = jnp.where(lane == 32, found[0], found[1])
    table[0:32] = jnp.where(lane < 32, names * 2 + rank, asks)
    to_plan = pltpu.make_async_copy(table.at[pl.ds(0, 32)], plan, local_sem.at[6])
    to_plan.start()
    to_plan.wait()

    def passage_copy(h, d):
        q = lax.rem(at.c + d, 32)
        return pltpu.make_async_remote_copy(
            src_ref=out_buf.at[h, pl.ds(2 * q, 2)], dst_ref=in_buf[h].at[pl.ds(2 * at.c, 2)],
            send_sem=a2a_send.at[h, d], recv_sem=a2a_recv.at[h, d],
            device_id=at.cache(q), device_id_type=MESH,
        )

    def send_part(h):
        lanes = pl.ds(h * 256, 256)

        def one(d, carry):
            q = lax.rem(at.c + d, 32)
            if h > 0:
                passage_copy(h - 1, d).wait_send()
            out_buf[h, 2 * q] = memory[plan[q, 32], :, lanes]
            out_buf[h, 2 * q + 1] = memory[plan[q, 33], :, lanes]
            passage_copy(h, d).start()
            return carry

        lax.fori_loop(1, 32, one, 0)
        in_buf[h][2 * at.c] = memory[plan[at.c, 32], :, lanes]
        in_buf[h][2 * at.c + 1] = memory[plan[at.c, 33], :, lanes]

    def wait_part(h):
        def one(d, carry):
            passage_copy(h, d).wait_recv()
            return carry

        lax.fori_loop(1, 32, one, 0)

        def pack(j, carry):
            own[h, pl.ds(pl.multiple_of(16 * j, 16), 16)] = in_buf[h][plan[at.c, j]]
            return carry

        lax.fori_loop(0, 32, pack, 0)

    def lanes_of(pos, h):
        return pl.ds(pl.multiple_of(pos * 1024 + h * 512, 512), 512)

    def part(pos, unit, k=0):
        h, g = unit
        return x_full.at[
            pl.ds(g * 256, 256), pl.ds(pl.multiple_of(pos * 1024 + h * 256, 256), 256)
        ]

    def ring_part(h):
        return Ring(
            mover, at.z, at.up, lambda u: own.at[u[0], pl.ds(u[1] * 256, 256)], part,
            [(h, 0), (h, 1)],
        )

    stored = []

    def multiply(k, h):
        pos = turn(at.z, k)
        lanes = lanes_of(pos, h)
        if k == 0:
            x_full[:, lanes] = jnp.concatenate([own[2 * h], own[2 * h + 1]], axis=1)
        keep = pltpu.make_async_copy(
            x_full.at[:, lanes], x_out.at[:, lanes], out_sem.at[len(stored)]
        )
        keep.start()
        first = not stored
        stored.append(keep)
        gain = live_gain[:, lanes]
        for r in range(2):
            rows = pl.ds(r * 256, 256)
            wide = x_full[rows, lanes].astype(F32)
            scaled[rows] = (wide * gain).astype(BF16)
            square = jnp.sum(wide * wide, axis=1, keepdims=True)
            squares[rows] = square if first else squares[rows] + square

        def one(i, carry):
            product = jnp.dot(scaled[...], weights[i, lanes], preferred_element_type=F32)
            acc[i] = product if first else acc[i] + product
            return carry

        lax.fori_loop(0, 3, one, 0)

    def sent_part(h):
        def one(d, carry):
            passage_copy(h, d).wait_send()
            return carry

        lax.fori_loop(1, 32, one, 0)

    send_part(0)

    load_table.wait()
    held = lax.broadcasted_iota(jnp.int32, (48, 1004), 1).astype(F32) + (at.c * 1004).astype(F32)
    for b in range(8):
        picks = [
            jnp.where(held == turned[64:112, q : q + 1], 1.0, 0.0).astype(BF16)
            for q in range(4 * b, 4 * b + 4)
        ]
        named = jnp.dot(
            jnp.concatenate(picks, axis=0), table_w[...], preferred_element_type=F32
        ).astype(BF16)
        for n in range(4):
            q = 4 * b + n
            tok[q // 8, (q // 2) % 4, q % 2] = named[48 * n : 48 * (n + 1)]
    other = 1 - at.core
    pair = mover.go(tok.at[:, :, other], pair_buf, at.sibling())
    spread.phase_one_onward()
    spread_next.phase_one_onward()
    send_part(1)

    pair.wait_recv()

    def add_pair(y, carry):
        for x in range(4):
            pair_buf[y, x] = pair_buf[y, x] + tok[y, x, at.core]
        return carry

    lax.fori_loop(0, 4, add_pair, 0)
    wait_part(0)
    rings = [ring_part(0)]
    send_part(2)
    wait_part(1)
    rings.append(ring_part(1))
    send_part(3)
    lo, hi = pl.ds(0, 512), pl.ds(512, 512)
    tok_a = [
        mover.go(
            pair_buf.at[:, turn(at.x, k), :, lo], a_buf.at[k - 1], at.chip(at.y, turn(at.x, k))
        )
        for k in range(1, 4)
    ]
    tok_b = [
        mover.go(
            pair_buf.at[turn(at.y, k), :, :, hi], b_buf.at[k - 1], at.chip(turn(at.y, k), at.x)
        )
        for k in range(1, 4)
    ]
    near_scores = [
        mover.go(score, scores.at[at.z], at.up(turn(at.z, k))) for k in range(1, 4)
    ]
    scores[at.z] = score[...]
    wait_part(2)
    rings.append(ring_part(2))
    rings[0].onward()
    wait_part(3)
    rings.append(ring_part(3))
    rings[1].onward()
    spread.phase_one_end()
    spread_next.phase_one_end()
    for copy in load_weights:
        copy.wait()
    multiply(0, 0)
    multiply(0, 1)
    for copy in tok_a + tok_b:
        copy.wait_recv()

    def add_line(i, carry):
        a_buf[0, i] = (a_buf[0, i] + a_buf[1, i]) + (a_buf[2, i] + pair_buf[i, at.x, :, lo])
        b_buf[0, i] = (b_buf[0, i] + b_buf[1, i]) + (b_buf[2, i] + pair_buf[at.y, i, :, hi])
        return carry

    lax.fori_loop(0, 4, add_line, 0)
    tok_a2 = [
        mover.go(a_buf.at[0, turn(at.y, k)], a2_buf.at[k - 1], at.chip(turn(at.y, k), at.x))
        for k in range(1, 4)
    ]
    tok_b2 = [
        mover.go(b_buf.at[0, turn(at.x, k)], b2_buf.at[k - 1], at.chip(at.y, turn(at.x, k)))
        for k in range(1, 4)
    ]
    spread.phase_two()
    split_kv(6, 9)
    rings[0].near()
    rings[1].near()
    multiply(1, 0)
    multiply(-1, 0)
    rings[2].onward()
    for copy in tok_a2 + tok_b2:
        copy.wait_recv()
    tok_sum[:, lo] = (a2_buf[0] + a2_buf[1]) + (a2_buf[2] + a_buf[0, at.y])
    tok_sum[:, hi] = (b2_buf[0] + b2_buf[1]) + (b2_buf[2] + b_buf[0, at.x])
    mine = pl.ds(pl.multiple_of(at.z * 1024, 1024), 1024)
    near_tokens = [
        mover.go(tok_sum, tokens.at[:, mine], at.up(turn(at.z, k))) for k in range(1, 4)
    ]
    tokens[:, mine] = tok_sum[...]
    rings[0].end()
    rings[1].end()
    multiply(2, 0)
    rings[3].onward()
    split_kv(9, 13)
    spread.phase_two_onward()
    split_kv(13, 16)
    keep_values = pltpu.make_async_copy(w_val, w_val_out, local_sem.at[4])
    keep_values.start()
    for copy in near_scores + near_tokens:
        copy.wait_recv()

    rows, inverse = norm_rows(tokens[0:16], live_gain[...])

    def project(i, carry):
        total = jnp.dot(rows, weights[i], preferred_element_type=F32)
        proj_q[i] = (total * inverse).astype(BF16)
        return carry

    lax.fori_loop(0, 3, project, 0)
    rows_a, inverse_a = norm_rows(tokens[16:48], dec_gain[...])
    queries = jnp.dot(rows_a, w_query[...], preferred_element_type=F32) * inverse_a
    head = lax.broadcasted_iota(jnp.int32, (32, 512), 1) // HEAD
    for h in range(8):
        scaled[pl.ds(32 * h, 32)] = jnp.where(head == h, queries, 0.0).astype(BF16)

    def fold(n, carry):
        cols = pl.ds(pl.multiple_of(n * 1024, 1024), 1024)
        product = dot32(scaled[pl.ds(0, 256)], w_key[cols], ((1,), (1,)))
        qg[:, cols] = (product * enc_gain[:, cols]).astype(BF16)
        return carry

    lax.fori_loop(0, 4, fold, 0)
    keep_folded = pltpu.make_async_copy(qg, qg_out, local_sem.at[7])
    keep_folded.start()
    rings[2].near()
    rings[3].near()
    multiply(1, 1)
    multiply(-1, 1)
    rings[2].end()
    rings[3].end()
    multiply(2, 1)
    inverse_m = lax.rsqrt(squares[...] * (1.0 / 4096) + EPSILON)

    def close(i, carry):
        proj_mem[i] = (acc[i] * inverse_m).astype(BF16)
        return carry

    lax.fori_loop(0, 3, close, 0)
    spread.finish()
    for copy in stored:
        copy.wait()
    keep_values.wait()
    keep_folded.wait()
    mover.finish_sends()

    sent_part(3)


def fetch(*args):
    return pl.pallas_call(
        fetch_kernel,
        out_shape=(
            jax.ShapeDtypeStruct((512, 4096), BF16),
            jax.ShapeDtypeStruct((48, 4096), BF16),
            jax.ShapeDtypeStruct((4, 1, 128), F32),
            jax.ShapeDtypeStruct((3, 4, 4, 2, 16, 2048), BF16),
            jax.ShapeDtypeStruct((3, 4, 4, 2, 16, 2048), BF16),
            jax.ShapeDtypeStruct((3, 512, 512), BF16),
            jax.ShapeDtypeStruct((3, 16, 512), BF16),
            jax.ShapeDtypeStruct((256, 4096), BF16),
            jax.ShapeDtypeStruct((4096, 512), BF16),
            jax.ShapeDtypeStruct((8, 32, 128), F32),
        ),
        in_specs=[VM] * 7 + [ANY, VM, ANY, ANY, ANY, ANY, VM, VM, VM],
        out_specs=(ANY, VM, VM, ANY, ANY, VM, VM, ANY, ANY, VM),
        scratch_shapes=[
            pltpu.VMEM((8, 128), jnp.int32), pltpu.VMEM((1, 128), F32),
            pltpu.VMEM((32, 8, 128), F32),
            pltpu.VMEM((32, 4, 1, 128), jnp.int32), pltpu.VMEM((128, 128), jnp.int32),
            pltpu.VMEM((128, 128), F32), pltpu.SMEM((32, 128), jnp.int32),
            pltpu.VMEM((4, 4, 2, 48, 1024), BF16), pltpu.VMEM((1004, 1024), BF16),
            pltpu.VMEM((4, 64, 16, 256), BF16), pltpu.VMEM((64, 16, 256), BF16),
            pltpu.VMEM((64, 16, 256), BF16), pltpu.VMEM((64, 16, 256), BF16),
            pltpu.VMEM((64, 16, 256), BF16),
            pltpu.VMEM((4, 512, 256), BF16), pltpu.VMEM((4, 4, 48, 1024), BF16),
            pltpu.VMEM((3, 4, 48, 512), BF16), pltpu.VMEM((3, 4, 48, 512), BF16),
            pltpu.VMEM((3, 48, 512), BF16), pltpu.VMEM((3, 48, 512), BF16),
            pltpu.VMEM((48, 1024), BF16),
            pltpu.VMEM((256, 4096), BF16),
            pltpu.VMEM((512, 4096), BF16), pltpu.VMEM((3, 4096, 512), BF16),
            pltpu.VMEM((3, 512, 512), F32), pltpu.VMEM((512, 1), F32),
            pltpu.VMEM((512, 512), BF16), pltpu.VMEM((4096, 512), BF16),
            pltpu.VMEM((4, 256, 2, 512), BF16), pltpu.VMEM((4096, 512), BF16),
            pltpu.VMEM((4096, 512), BF16),
            pltpu.SemaphoreType.DMA((112,)), pltpu.SemaphoreType.DMA((112,)),
            pltpu.SemaphoreType.DMA((4, 32)), pltpu.SemaphoreType.DMA((4, 32)),
            pltpu.SemaphoreType.DMA((32,)), pltpu.SemaphoreType.DMA((32,)),
            pltpu.SemaphoreType.DMA((8,)), pltpu.SemaphoreType.DMA((4,)),
            pltpu.SemaphoreType.DMA((8,)),
        ],
        compiler_params=params(2, 60),
    )(*args)


def reader_kernel(
    proj_mem, proj_q, bias, x_mem, tokens, qg_in, scores, left_in, right_in, live_out, w_val_in,
    cross_out_in,
    encoded_out, decoded,
    qg, encoded, ctx, others, x_seq, left, right, own_out, w_val, w_out, ql, ql_part, lv, lv_part, s, w, values,
    inv, parts, part_buf, send, recv, local_sem,
):
    at = Place()
    mover = Mover(send, recv)
    spread = Spread(at, mover, right, 2048)
    loads = [
        pltpu.make_async_copy(a, b, local_sem.at[i])
        for i, (a, b) in enumerate([
            (spread.line(right_in, "x"), spread.line(right, "x")),
            (spread.line(right_in, "y"), spread.line(right, "y")),
            (x_mem, x_seq.at[:, pl.ds(0, 16)]), (live_out, own_out), (w_val_in, w_val),
            (left_in, left), (cross_out_in, w_out), (qg_in, qg),
        ])
    ]
    for copy in loads:
        copy.start()
    greet_all(at)
    scale = HEAD ** (-0.5)
    nt = ((1,), (1,))
    def chunk(j):
        return pl.ds(pl.multiple_of(j * 256, 256), 256)

    def part(pos, u, k):
        return others.at[{1: 2, -1: 0, 2: 1}[k], chunk(turn(pos, u))]

    ring = Ring(
        mover, at.z, at.up, lambda u: ctx.at[chunk(turn(at.z, u))], part, [2, 1, 3, 0], False
    )

    low = lax.broadcasted_iota(jnp.int32, (128, 128), 1) < HEAD
    owner_lane = lax.broadcasted_iota(jnp.int32, (32, 256), 1) // 32 % 4

    def attend(j):
        def group(g, carry):
            first = j * 8 + g * 4

            def pair(i, p):
                lanes = pl.ds(128 * p, 128)
                pieces = []
                for n in range(4):
                    pieces.append(
                        proj_mem[i, pl.ds(pl.multiple_of((first + n) * 16, 16), 16), lanes]
                    )
                    pieces.append(proj_q[i, :, lanes])
                return jnp.concatenate(pieces, axis=0)

            for p in range(4):
                q, k, v = pair(0, p), pair(1, p), pair(2, p)
                none = jnp.zeros_like(q)
                both = jnp.concatenate([jnp.where(low, q, none), jnp.where(low, none, q)], axis=0)
                full = dot32(k, both, nt)
                sc = full[0:32]
                for n in range(1, 4):
                    sc = jnp.where(owner_lane == n, full[32 * n : 32 * n + 32], sc)
                sc = sc * scale + jnp.concatenate([bias[2 * p], bias[2 * p + 1]], axis=1)
                ex = jnp.exp(sc - jnp.max(sc, axis=0, keepdims=True))
                ex = ex * (1.0 / jnp.sum(ex, axis=0, keepdims=True))
                full = jnp.concatenate(
                    [jnp.where(owner_lane == n, ex, 0.0) for n in range(4)], axis=0
                ).astype(BF16)
                out = dot32(full, v, ((0,), (0,)))
                ctx[pl.ds(pl.multiple_of(first * 32, 128), 128), pl.ds(128 * p, 128)] = jnp.where(
                    low, out[0:128], out[128:256]
                ).astype(BF16)
            return carry

        lax.fori_loop(0, 2, group, 0)

    for u in (2, 3, 1, 0):
        attend(turn(at.z, u))
        ring.begin_right(u)
        ring.begin_left(u)
        if u == 2:
            loads[0].wait()
            loads[1].wait()
            spread.phase_two()

    loads[2].wait()
    loads[7].wait()

    def fill(p, carry):
        x_seq[p, pl.ds(16, 16)] = tokens[pl.ds(0, 16)]
        return carry

    lax.fori_loop(0, 32, fill, 0)

    def rows_of(j):
        return x_seq[pl.ds(j * 8, 8)].reshape(256, 4096)

    def score_inputs(j, carry):
        s[j] = dot32(qg[...], rows_of(j), nt)
        return carry

    lax.fori_loop(0, 4, score_inputs, 0)
    loads[4].wait()
    of_question = jnp.dot(tokens[pl.ds(0, 16)], w_val[...], preferred_element_type=F32)

    def value_inputs(j, carry):
        rows = jnp.dot(
            x_seq[pl.ds(j * 8, 8), pl.ds(0, 16)].reshape(128, 4096), w_val[...],
            preferred_element_type=F32,
        )
        for p in range(8):
            values[j, pl.ds(32 * p, 16)] = rows[16 * p : 16 * p + 16]
            values[j, pl.ds(32 * p + 16, 16)] = of_question
        return carry

    lax.fori_loop(0, 4, value_inputs, 0)
    spread.phase_two_onward()
    loads[3].wait()
    ql[0] = dot32(qg[...], own_out[...], nt).astype(BF16)
    lv[0] = jnp.dot(own_out[...], w_val[...], preferred_element_type=F32).astype(BF16)

    def absorb(j, k, rows):
        s[j] = s[j] + dot32(ql[k], rows, nt)
        values[j] = values[j] + jnp.dot(rows, lv[k], preferred_element_type=F32)

    def absorb_own(j, carry):
        absorb(j, 0, ctx[chunk(j)])
        return carry

    lax.fori_loop(0, 4, absorb_own, 0)
    loads[5].wait()
    half, rest = pl.ds(0, 2048), pl.ds(2048, 2048)

    def fold_left(k, carry):
        ql_part[k] = dot32(qg[:, half], left[k], nt)
        lv_part[k] = jnp.dot(left[k], w_val[half], preferred_element_type=F32)
        return carry

    lax.fori_loop(0, 3, fold_left, 0)
    ring.pass_right(2)
    ring.pass_left(3)
    ring.pass_right(1)
    spread.finish()

    def fold_right(k, carry):
        rows = right[k].reshape(512, 2048)
        ql[k + 1] = (ql_part[k] + dot32(qg[:, rest], rows, nt)).astype(BF16)
        lv[k + 1] = (
            lv_part[k] + jnp.dot(rows, w_val[rest], preferred_element_type=F32)
        ).astype(BF16)
        return carry

    lax.fori_loop(0, 3, fold_right, 0)

    ring.pass_left(0)

    ring.far[2].wait_recv()
    mine = chunk(at.z)

    def group_rows(k, n):
        if k == 0:
            return own_out[:, pl.ds(n * 1024, 1024)]
        if n < 2:
            return left[k - 1, :, pl.ds(n * 1024, 1024)]
        return right[k - 1, :, :, :, :, pl.ds((n - 2) * 1024, 1024)].reshape(512, 1024)

    squares = jnp.zeros((256, 1), F32)
    for n in range(4):
        cols = pl.ds(n * 1024, 1024)
        attended = None
        for k in range(4):
            rows = ctx[mine] if k == 0 else others[k - 1, mine]
            product = jnp.dot(rows, group_rows(k, n), preferred_element_type=F32)
            product = product.astype(BF16).astype(F32)
            attended = product if k == 0 else attended + product
        own_rows = x_seq[pl.ds(at.z * 8, 8), :, cols].reshape(256, 1024).astype(F32)
        own_rows = (own_rows + attended).astype(BF16)
        encoded[:, cols] = own_rows
        own_rows = own_rows.astype(F32)
        squares = squares + jnp.sum(own_rows * own_rows, axis=1, keepdims=True)
    keep = pltpu.make_async_copy(encoded, encoded_out, local_sem.at[8])
    keep.start()
    norm = lax.rsqrt(squares * (1.0 / 4096) + EPSILON)
    inv[at.z] = jnp.transpose(jnp.broadcast_to(norm, (256, 128)))[0:1]
    near = [mover.go(inv.at[at.z], inv.at[at.z], at.up(turn(at.z, k))) for k in range(1, 4)]

    def absorb_other(k, u):
        j = turn(at.z, k + u)
        absorb(j, k, others[k - 1, chunk(j)])

    absorb_other(3, 2)
    absorb_other(1, 3)
    absorb_other(3, 1)
    absorb_other(2, 2)
    ring.to_left[2].wait_recv()
    absorb_other(1, 2)
    ring.to_right[3].wait_recv()
    absorb_other(3, 3)
    ring.to_left[1].wait_recv()
    absorb_other(1, 1)
    absorb_other(1, 0)
    ring.far[3].wait_recv()
    absorb_other(2, 3)
    ring.to_right[0].wait_recv()
    absorb_other(3, 0)
    ring.far[1].wait_recv()
    absorb_other(2, 1)
    ring.far[0].wait_recv()
    absorb_other(2, 0)
    for copy in near:
        copy.wait_recv()

    passage = lax.broadcasted_iota(jnp.int32, (1, 256), 1) // 32
    top = None
    for j in range(4):
        row = jnp.zeros((1, 256), F32)
        line = scores[j]
        for p in range(8):
            row = row + jnp.where(passage == p, line[:, p : p + 1], 0.0)
        total = s[j] * (inv[j] * scale) + row
        s[j] = total
        here = jnp.max(total, axis=1, keepdims=True)
        top = here if top is None else jnp.maximum(top, here)
    sums = jnp.zeros((256, 1), F32)
    for j in range(4):
        ex = jnp.exp(s[j] - top)
        s[j] = ex
        sums = sums + jnp.sum(ex, axis=1, keepdims=True)
    for j in range(4):
        w[j] = (s[j] * inv[j] / sums).astype(BF16)
    heads_out = jnp.zeros((256, 512), F32)
    for j in range(4):
        heads_out = heads_out + jnp.dot(
            w[j], values[j].astype(BF16), preferred_element_type=F32
        )
    head = lax.broadcasted_iota(jnp.int32, (32, 512), 1) // HEAD
    context = jnp.zeros((32, 512), F32)
    for h in range(8):
        context = context + jnp.where(head == h, heads_out[32 * h : 32 * h + 32], 0.0)
    context = context.astype(BF16)
    loads[6].wait()
    for j in range(4):
        parts[j] = jnp.dot(
            context, w_out[:, pl.ds(1024 * j, 1024)], preferred_element_type=F32
        ).astype(BF16)
    last = [
        mover.go(parts.at[turn(at.z, k)], part_buf.at[k - 1], at.up(turn(at.z, k)))
        for k in range(1, 4)
    ]
    for copy in last:
        copy.wait_recv()
    total = parts[at.z].astype(F32)
    for k in range(3):
        total = total + part_buf[k].astype(F32)
    decoded[...] = total.astype(BF16)
    keep.wait()
    mover.finish_sends()


def reader(*args):
    return pl.pallas_call(
        reader_kernel,
        out_shape=(
            jax.ShapeDtypeStruct((256, 4096), BF16),
            jax.ShapeDtypeStruct((32, 1024), BF16),
        ),
        in_specs=[VM, VM, VM, ANY, VM, ANY, VM, ANY, ANY, ANY, ANY, ANY],
        out_specs=(ANY, VM),
        scratch_shapes=[
            pltpu.VMEM((256, 4096), BF16), pltpu.VMEM((256, 4096), BF16),
            pltpu.VMEM((1024, 512), BF16), pltpu.VMEM((3, 1024, 512), BF16),
            pltpu.VMEM((32, 32, 4096), BF16), pltpu.VMEM((3, 512, 2048), BF16),
            pltpu.VMEM((3, 4, 4, 2, 16, 2048), BF16), pltpu.VMEM((512, 4096), BF16),
            pltpu.VMEM((4096, 512), BF16), pltpu.VMEM((512, 4096), BF16),
            pltpu.VMEM((4, 256, 512), BF16), pltpu.VMEM((3, 256, 512), F32),
            pltpu.VMEM((4, 512, 512), BF16), pltpu.VMEM((3, 512, 512), F32),
            pltpu.VMEM((4, 256, 256), F32), pltpu.VMEM((4, 256, 256), BF16),
            pltpu.VMEM((4, 256, 512), F32), pltpu.VMEM((4, 1, 256), F32),
            pltpu.VMEM((4, 32, 1024), BF16), pltpu.VMEM((3, 32, 1024), BF16),
            pltpu.SemaphoreType.DMA((64,)), pltpu.SemaphoreType.DMA((64,)),
            pltpu.SemaphoreType.DMA((9,)),
        ],
        compiler_params=params(3, 60),
    )(*args)


def shards(
    question_ids, answer_ids, owner, slot, passage_score, memory, embedding, live_gain, live_qkv,
    rel_bias, live_out, enc_gain, cross_kv, dec_gain, cross_query, cross_out,
):
    n_psg = lax.axis_size("psg")
    width = live_gain.shape[0]
    plen = memory.shape[1]
    qlen = question_ids.shape[1]
    own_count = owner.shape[1]
    total = own_count * n_psg
    seq = plen + qlen
    cols = live_out.shape[0]

    spread_of = jnp.asarray(spread_table(seq, rel_bias.shape[1]))
    x_mem, token_full, scores, left, right, proj_mem, proj_q, qg, w_val, bias = fetch(
        question_ids, answer_ids, owner.reshape(1, own_count), slot, rel_bias, spread_of, memory,
        embedding, passage_score, live_out,
        jnp.transpose(live_qkv, (1, 0, 2)), cross_kv, cross_query,
        live_gain.reshape(1, width), enc_gain.reshape(1, width), dec_gain.reshape(1, width),
    )
    encoded, decoded = reader(
        proj_mem, proj_q, bias, x_mem.reshape(total, plen, width), token_full, qg, scores,
        left.reshape(3, cols, width // 2), right, live_out, w_val, cross_out,
    )
    return encoded.reshape(1, own_count, seq, width), decoded[None]


def solution(mesh):
    return jax.shard_map(
        shards,
        mesh=mesh,
        in_specs=(
            P("cache", None), P("cache", None), P("cache", "psg", None), P("cache", "psg"),
            P("cache", "psg"), P("cache", None, "psg"), P("cache", "psg"), P(),
            P(None, None, "psg"), P("psg", None), P("psg", None), P(), P(None, None, "psg"), P(),
            P(None, "psg"), P("psg", None),
        ),
        out_specs=(P("cache", "psg", None, None), P("cache", None, "psg")),
        check_vma=False,
    )
```

```python
import functools

import jax
import jax.numpy as jnp
import numpy as np
from jax import lax
from jax.experimental import pallas as pl
from jax.experimental.pallas import tpu as pltpu
from jax.sharding import PartitionSpec as P

HEAD = 64
EPSILON = 1e-06
F32 = jnp.float32
BF16 = jnp.bfloat16


def bucket_table(length, bucket_count):
    positions = np.arange(length)
    relative = positions[None, :] - positions[:, None]
    halfway = bucket_count // 2
    exact_span = halfway // 2
    upper_side = (relative > 0).astype(np.int64) * halfway
    distance = np.abs(relative)
    log_bucket = exact_span + (
        np.log(np.maximum(distance, 1) / exact_span)
        / np.log(128.0 / exact_span)
        * (halfway - exact_span)
    ).astype(np.int64)
    log_bucket = np.minimum(log_bucket, halfway - 1)
    return upper_side + np.where(distance < exact_span, distance, log_bucket)


def spread_table(length, bucket_count):
    buckets = np.tile(bucket_table(length, bucket_count).T, (1, 4)).reshape(-1)
    return (buckets[None, :] == np.arange(bucket_count)[:, None]).astype(np.float32)


def dot32(a, b, dims):
    return lax.dot_general(a, b, (dims, ((), ())), preferred_element_type=F32)


MESH = pl.DeviceIdType.MESH
VM = pl.BlockSpec(memory_space=pltpu.VMEM)
SM = pl.BlockSpec(memory_space=pltpu.SMEM)
ANY = pl.BlockSpec(memory_space=pl.ANY)


def params(collective_id, mib):
    return pltpu.CompilerParams(
        collective_id=collective_id, has_side_effects=True, vmem_limit_bytes=mib << 20
    )


class Place:
    def __init__(self):
        self.c = lax.axis_index("cache")
        self.z = lax.axis_index("psg")
        self.core = lax.rem(self.c, 2)
        self.x = lax.rem(lax.div(self.c, 2), 4)
        self.y = lax.div(self.c, 8)

    def cache(self, c):
        return {"cache": c, "psg": self.z}

    def chip(self, y, x):
        return self.cache((y * 4 + x) * 2 + self.core)

    def sibling(self):
        return self.cache(self.c + 1 - 2 * self.core)

    def up(self, z):
        return {"cache": self.c, "psg": z}


def turn(p, k):
    return lax.rem(p + k + 4, 4)


def greet_all(at):
    barrier = pltpu.get_barrier_semaphore()

    def greet(d, carry):
        pl.semaphore_signal(
            barrier, inc=1, device_id=at.cache(lax.rem(at.c + d, 32)), device_id_type=MESH
        )
        return carry

    lax.fori_loop(1, 32, greet, 0)
    for k in range(1, 4):
        pl.semaphore_signal(barrier, inc=1, device_id=at.up(turn(at.z, k)), device_id_type=MESH)
    pl.semaphore_wait(barrier, 34)


class Mover:
    def __init__(self, send, recv):
        self.send, self.recv, self.count, self.started = send, recv, 0, []

    def go(self, src, dst, device):
        i = self.count
        self.count += 1
        copy = pltpu.make_async_remote_copy(
            src_ref=src, dst_ref=dst, send_sem=self.send.at[i], recv_sem=self.recv.at[i],
            device_id=device, device_id_type=MESH,
        )
        copy.start()
        self.started.append(copy)
        return copy

    def finish_sends(self):
        for copy in self.started:
            copy.wait_send()


class Ring:
    def __init__(self, mover, pos, device, own, dst, units, start=True):
        self.mover, self.pos, self.device, self.own, self.dst = mover, pos, device, own, dst
        self.right, self.left = device(turn(pos, 1)), device(turn(pos, -1))
        self.to_right, self.to_left, self.far = {}, {}, {}
        half = len(units) // 2
        self.first, self.last = units[:half], units[half:]
        if start:
            for u, v in zip(units, self.last + self.first):
                self.begin_right(u)
                self.begin_left(v)

    def begin_right(self, u):
        self.to_right[u] = self.mover.go(self.own(u), self.dst(self.pos, u, 1), self.right)

    def begin_left(self, u):
        self.to_left[u] = self.mover.go(self.own(u), self.dst(self.pos, u, -1), self.left)

    def pass_right(self, u):
        self.to_right[u].wait_recv()
        before = turn(self.pos, -1)
        self.far[u] = self.mover.go(self.dst(before, u, 1), self.dst(before, u, 2), self.right)

    def pass_left(self, u):
        self.to_left[u].wait_recv()
        after = turn(self.pos, 1)
        self.far[u] = self.mover.go(self.dst(after, u, -1), self.dst(after, u, 2), self.left)

    def onward(self):
        for u, v in zip(self.first, self.last):
            self.pass_right(u)
            self.pass_left(v)

    def near(self):
        for u in self.last:
            self.to_right[u].wait_recv()
        for v in self.first:
            self.to_left[v].wait_recv()

    def end(self):
        for copy in self.far.values():
            copy.wait_recv()


class Spread:
    def __init__(self, at, mover, full, width):
        self.at, self.mover, self.full = at, mover, full
        self.quarter, self.width = width // 4, width

    def begin(self, live_out, first):
        at = self.at
        rows = pl.ds(pl.multiple_of(at.c * 16, 16), 16)
        self.start = [
            self.mover.go(
                live_out.at[rows, pl.ds(first, self.width)],
                self.full.at[k - 1, at.y, at.x, at.core],
                at.up(turn(at.z, -k)),
            )
            for k in range(1, 4)
        ]

    def cols(self, u, n=1):
        return pl.ds(u * self.quarter, n * self.quarter)

    def phase_one(self):
        at, full = self.at, self.full
        for copy in self.start:
            copy.wait_recv()
        a = lambda pos, u, k=0: full.at[:, at.y, pos, at.core, :, self.cols(u)]
        b = lambda pos, u, k=0: full.at[:, pos, at.x, at.core, :, self.cols(u)]
        self.one = [
            Ring(self.mover, at.x, lambda p: at.chip(at.y, p), lambda u: a(at.x, u), a, [0, 1]),
            Ring(self.mover, at.y, lambda p: at.chip(p, at.x), lambda u: b(at.y, u), b, [2, 3]),
        ]

    def phase_one_onward(self):
        for ring in self.one:
            ring.onward()

    def phase_one_end(self):
        for ring in self.one:
            ring.near()
            ring.end()

    def line(self, full, axis):
        at = self.at
        if axis == "x":
            return full.at[:, at.y, :, at.core, :, self.cols(0, 2)]
        return full.at[:, :, at.x, at.core, :, self.cols(2, 2)]

    def phase_two(self):
        at, full = self.at, self.full
        a = lambda pos, u, k=0: full.at[:, pos, :, at.core, :, self.cols(u)]
        b = lambda pos, u, k=0: full.at[:, :, pos, at.core, :, self.cols(u)]
        self.two = [
            Ring(self.mover, at.y, lambda p: at.chip(p, at.x), lambda u: a(at.y, u), a, [0, 1]),
            Ring(self.mover, at.x, lambda p: at.chip(at.y, p), lambda u: b(at.x, u), b, [2, 3]),
        ]
        self.over = []
        self.cross(0)

    def cross(self, k):
        at, full = self.at, self.full
        a = full.at[:, turn(at.y, k), :, at.core, :, self.cols(0, 2)]
        b = full.at[:, :, turn(at.x, k), at.core, :, self.cols(2, 2)]
        for view in (a, b):
            self.over.append(self.mover.go(view, view, at.sibling()))

    def phase_two_onward(self):
        for ring in self.two:
            ring.onward()
        for ring in self.two:
            ring.near()
        self.cross(1)
        self.cross(-1)

    def finish(self):
        for ring in self.two:
            ring.end()
        self.cross(2)
        for copy in self.over:
            copy.wait_recv()


def norm_rows(rows, gain):
    wide = rows.astype(F32)
    inverse = lax.rsqrt(jnp.mean(wide * wide, axis=-1, keepdims=True) + EPSILON)
    return (wide * gain).astype(BF16), inverse


def fetch_kernel(
    question_ids, answer_ids, owner, slot, rel_bias, spread_of, memory, embedding, own_score,
    live_out, w_qkv, cross_kv, cross_query,
    live_gain, enc_gain, dec_gain,
    x_out, tokens, scores, full, full_next, proj_mem, proj_q, qg_out, w_val_out, bias,
    line_buf, score, by_key, every, table, turned, plan, tok, table_w, out_buf, in_buf0, in_buf1, in_buf2, in_buf3, own, pair_buf, a_buf, b_buf, a2_buf, b2_buf, tok_sum,
    qg, x_full, weights, acc, squares, scaled, w_query, kv_buf, w_key, w_val,
    send, recv, a2a_send, a2a_recv, line_send, line_recv, local_sem, kv_sem, out_sem,
):
    at = Place()
    line_buf[...] = jnp.zeros((8, 128), jnp.int32)
    line_buf[0:1, 0:8] = owner[...]
    line_buf[0:1, 32:40] = slot[...]
    line_buf[1:2, 64:80] = question_ids[...]
    line_buf[1:2, 80:112] = answer_ids[...]
    placed = pltpu.roll(line_buf[0:1], 8 * at.z, 1)
    every[at.c, at.z] = placed + jnp.where(at.z == 0, line_buf[1:2], 0)
    score[...] = jnp.zeros((1, 128), F32)
    score[:, 0:8] = own_score[...]
    table[32:128] = jnp.zeros((96, 128), jnp.int32)
    load_table = pltpu.make_async_copy(embedding, table_w, local_sem.at[5])
    load_table.start()
    load_weights = [
        pltpu.make_async_copy(w_qkv.at[i], weights.at[i], local_sem.at[i]) for i in range(3)
    ] + [pltpu.make_async_copy(cross_query, w_query, local_sem.at[3])]
    for copy in load_weights:
        copy.start()

    def kv_copy(i):
        slot = lax.rem(i, 4)
        return pltpu.make_async_copy(
            cross_kv.at[pl.ds(i * 256, 256)], kv_buf.at[slot], kv_sem.at[slot]
        )

    for i in range(3):
        kv_copy(i).start()

    def split_kv(first, last):
        def one(i, carry):
            @pl.when(i < 13)
            def _():
                kv_copy(i + 3).start()

            kv_copy(i).wait()
            rows = pl.ds(pl.multiple_of(i * 256, 256), 256)
            slot = lax.rem(i, 4)
            w_key[rows] = kv_buf[slot, :, 0, :]
            gain = jnp.transpose(jnp.broadcast_to(enc_gain[:, rows], (128, 256)))[:, 0:1]
            w_val[rows] = (kv_buf[slot, :, 1, :].astype(F32) * gain).astype(BF16)
            return carry

        lax.fori_loop(first, last, one, 0)

    greet_all(at)
    mover = Mover(send, recv)
    in_buf = (in_buf0, in_buf1, in_buf2, in_buf3)

    spread = Spread(at, mover, full, 2048)
    spread.begin(live_out, 0)
    spread_next = Spread(at, mover, full_next, 2048)
    spread_next.begin(live_out, 2048)

    near = [
        mover.go(every.at[at.c, at.z], every.at[at.c, at.z], at.up(turn(at.z, k)))
        for k in range(1, 4)
    ]

    def line_copy(d):
        return pltpu.make_async_remote_copy(
            src_ref=every.at[at.c], dst_ref=every.at[at.c], send_sem=line_send.at[d],
            recv_sem=line_recv.at[d], device_id=at.cache(lax.rem(at.c + d, 32)),
            device_id_type=MESH,
        )

    def send_line(d, carry):
        line_copy(d).start()
        return carry

    def wait_line(d, carry):
        line_copy(d).wait()
        return carry

    for copy in near:
        copy.wait_recv()
    lax.fori_loop(1, 32, send_line, 0)
    split_kv(0, 4)
    spread.phase_one()
    spread_next.phase_one()
    split_kv(4, 6)

    by_bucket = jnp.dot(
        rel_bias[...], spread_of[...], precision=lax.Precision.HIGHEST, preferred_element_type=F32
    )
    for b in range(32):
        by_key[b] = by_bucket[:, 128 * b : 128 * b + 128]
    for h in range(8):
        bias[h] = by_key[:, h, :]
    lax.fori_loop(1, 32, wait_line, 0)
    for q in range(32):
        table[q : q + 1] = (every[q, 0] + every[q, 1]) + (every[q, 2] + every[q, 3])

    names = table[0:32]
    turned[...] = jnp.transpose(table[...].astype(F32))
    lane = lax.broadcasted_iota(jnp.int32, (32, 128), 1)
    rank = jnp.zeros((32, 128), jnp.int32)
    for shift in range(1, 32):
        same = jnp.logical_and(pltpu.roll(names, shift, 1) == names, lane >= shift)
        rank = rank + jnp.where(same, 1, 0)
    entries = pltpu.roll(names, 96, 1)
    found = []
    for r in range(2):
        hit = jnp.logical_and(jnp.logical_and(names == at.c, rank == r), lane < 32)
        entry = jnp.where(hit, entries, 0)
        for shift in (64, 32, 16, 8, 4, 2, 1):
            entry = entry + pltpu.roll(entry, shift, 1)
        found.append(entry)
    asks = jnp.where(lane == 32, found[0], found[1])
    table[0:32] = jnp.where(lane < 32, names * 2 + rank, asks)
    to_plan = pltpu.make_async_copy(table.at[pl.ds(0, 32)], plan, local_sem.at[6])
    to_plan.start()
    to_plan.wait()

    def passage_copy(h, d):
        q = lax.rem(at.c + d, 32)
        return pltpu.make_async_remote_copy(
            src_ref=out_buf.at[h, pl.ds(2 * q, 2)], dst_ref=in_buf[h].at[pl.ds(2 * at.c, 2)],
            send_sem=a2a_send.at[h, d], recv_sem=a2a_recv.at[h, d],
            device_id=at.cache(q), device_id_type=MESH,
        )

    def send_part(h):
        lanes = pl.ds(h * 256, 256)

        def one(d, carry):
            q = lax.rem(at.c + d, 32)
            if h > 0:
                passage_copy(h - 1, d).wait_send()
            out_buf[h, 2 * q] = memory[plan[q, 32], :, lanes]
            out_buf[h, 2 * q + 1] = memory[plan[q, 33], :, lanes]
            passage_copy(h, d).start()
            return carry

        lax.fori_loop(1, 32, one, 0)
        in_buf[h][2 * at.c] = memory[plan[at.c, 32], :, lanes]
        in_buf[h][2 * at.c + 1] = memory[plan[at.c, 33], :, lanes]

    def wait_part(h):
        def one(d, carry):
            passage_copy(h, d).wait_recv()
            return carry

        lax.fori_loop(1, 32, one, 0)

        def pack(j, carry):
            own[h, pl.ds(pl.multiple_of(16 * j, 16), 16)] = in_buf[h][plan[at.c, j]]
            return carry

        lax.fori_loop(0, 32, pack, 0)

    def lanes_of(pos, h):
        return pl.ds(pl.multiple_of(pos * 1024 + h * 512, 512), 512)

    def part(pos, unit, k=0):
        h, g = unit
        return x_full.at[
            pl.ds(g * 256, 256), pl.ds(pl.multiple_of(pos * 1024 + h * 256, 256), 256)
        ]

    def ring_part(h):
        return Ring(
            mover, at.z, at.up, lambda u: own.at[u[0], pl.ds(u[1] * 256, 256)], part,
            [(h, 0), (h, 1)],
        )

    stored = []

    def multiply(k, h):
        pos = turn(at.z, k)
        lanes = lanes_of(pos, h)
        if k == 0:
            x_full[:, lanes] = jnp.concatenate([own[2 * h], own[2 * h + 1]], axis=1)
        keep = pltpu.make_async_copy(
            x_full.at[:, lanes], x_out.at[:, lanes], out_sem.at[len(stored)]
        )
        keep.start()
        first = not stored
        stored.append(keep)
        gain = live_gain[:, lanes]
        for r in range(2):
            rows = pl.ds(r * 256, 256)
            wide = x_full[rows, lanes].astype(F32)
            scaled[rows] = (wide * gain).astype(BF16)
            square = jnp.sum(wide * wide, axis=1, keepdims=True)
            squares[rows] = square if first else squares[rows] + square

        def one(i, carry):
            product = jnp.dot(scaled[...], weights[i, lanes], preferred_element_type=F32)
            acc[i] = product if first else acc[i] + product
            return carry

        lax.fori_loop(0, 3, one, 0)

    def sent_part(h):
        def one(d, carry):
            passage_copy(h, d).wait_send()
            return carry

        lax.fori_loop(1, 32, one, 0)

    send_part(0)

    load_table.wait()
    held = lax.broadcasted_iota(jnp.int32, (48, 1004), 1).astype(F32) + (at.c * 1004).astype(F32)
    for b in range(8):
        picks = [
            jnp.where(held == turned[64:112, q : q + 1], 1.0, 0.0).astype(BF16)
            for q in range(4 * b, 4 * b + 4)
        ]
        named = jnp.dot(
            jnp.concatenate(picks, axis=0), table_w[...], preferred_element_type=F32
        ).astype(BF16)
        for n in range(4):
            q = 4 * b + n
            tok[q // 8, (q // 2) % 4, q % 2] = named[48 * n : 48 * (n + 1)]
    other = 1 - at.core
    pair = mover.go(tok.at[:, :, other], pair_buf, at.sibling())
    spread.phase_one_onward()
    spread_next.phase_one_onward()
    send_part(1)

    pair.wait_recv()

    def add_pair(y, carry):
        for x in range(4):
            pair_buf[y, x] = pair_buf[y, x] + tok[y, x, at.core]
        return carry

    lax.fori_loop(0, 4, add_pair, 0)
    wait_part(0)
    rings = [ring_part(0)]
    send_part(2)
    wait_part(1)
    rings.append(ring_part(1))
    send_part(3)
    lo, hi = pl.ds(0, 512), pl.ds(512, 512)
    tok_a = [
        mover.go(
            pair_buf.at[:, turn(at.x, k), :, lo], a_buf.at[k - 1], at.chip(at.y, turn(at.x, k))
        )
        for k in range(1, 4)
    ]
    tok_b = [
        mover.go(
            pair_buf.at[turn(at.y, k), :, :, hi], b_buf.at[k - 1], at.chip(turn(at.y, k), at.x)
        )
        for k in range(1, 4)
    ]
    near_scores = [
        mover.go(score, scores.at[at.z], at.up(turn(at.z, k))) for k in range(1, 4)
    ]
    scores[at.z] = score[...]
    wait_part(2)
    rings.append(ring_part(2))
    rings[0].onward()
    wait_part(3)
    rings.append(ring_part(3))
    rings[1].onward()
    spread.phase_one_end()
    spread_next.phase_one_end()
    for copy in load_weights:
        copy.wait()
    multiply(0, 0)
    multiply(0, 1)
    for copy in tok_a + tok_b:
        copy.wait_recv()

    def add_line(i, carry):
        a_buf[0, i] = (a_buf[0, i] + a_buf[1, i]) + (a_buf[2, i] + pair_buf[i, at.x, :, lo])
        b_buf[0, i] = (b_buf[0, i] + b_buf[1, i]) + (b_buf[2, i] + pair_buf[at.y, i, :, hi])
        return carry

    lax.fori_loop(0, 4, add_line, 0)
    tok_a2 = [
        mover.go(a_buf.at[0, turn(at.y, k)], a2_buf.at[k - 1], at.chip(turn(at.y, k), at.x))
        for k in range(1, 4)
    ]
    tok_b2 = [
        mover.go(b_buf.at[0, turn(at.x, k)], b2_buf.at[k - 1], at.chip(at.y, turn(at.x, k)))
        for k in range(1, 4)
    ]
    spread.phase_two()
    split_kv(6, 9)
    rings[0].near()
    rings[1].near()
    rings[2].onward()
    multiply(1, 0)
    multiply(-1, 0)
    for copy in tok_a2 + tok_b2:
        copy.wait_recv()
    tok_sum[:, lo] = (a2_buf[0] + a2_buf[1]) + (a2_buf[2] + a_buf[0, at.y])
    tok_sum[:, hi] = (b2_buf[0] + b2_buf[1]) + (b2_buf[2] + b_buf[0, at.x])
    mine = pl.ds(pl.multiple_of(at.z * 1024, 1024), 1024)
    near_tokens = [
        mover.go(tok_sum, tokens.at[:, mine], at.up(turn(at.z, k))) for k in range(1, 4)
    ]
    tokens[:, mine] = tok_sum[...]
    rings[3].onward()
    rings[0].end()
    rings[1].end()
    multiply(2, 0)
    split_kv(9, 13)
    spread.phase_two_onward()
    split_kv(13, 16)
    keep_values = pltpu.make_async_copy(w_val, w_val_out, local_sem.at[4])
    keep_values.start()
    for copy in near_scores + near_tokens:
        copy.wait_recv()

    rows, inverse = norm_rows(tokens[0:16], live_gain[...])

    def project(i, carry):
        total = jnp.dot(rows, weights[i], preferred_element_type=F32)
        proj_q[i] = (total * inverse).astype(BF16)
        return carry

    lax.fori_loop(0, 3, project, 0)
    rows_a, inverse_a = norm_rows(tokens[16:48], dec_gain[...])
    queries = jnp.dot(rows_a, w_query[...], preferred_element_type=F32) * inverse_a
    head = lax.broadcasted_iota(jnp.int32, (32, 512), 1) // HEAD
    for h in range(8):
        scaled[pl.ds(32 * h, 32)] = jnp.where(head == h, queries, 0.0).astype(BF16)

    def fold(n, carry):
        cols = pl.ds(pl.multiple_of(n * 1024, 1024), 1024)
        product = dot32(scaled[pl.ds(0, 256)], w_key[cols], ((1,), (1,)))
        qg[:, cols] = (product * enc_gain[:, cols]).astype(BF16)
        return carry

    lax.fori_loop(0, 4, fold, 0)
    keep_folded = pltpu.make_async_copy(qg, qg_out, local_sem.at[7])
    keep_folded.start()
    rings[2].near()
    rings[3].near()
    multiply(1, 1)
    multiply(-1, 1)
    rings[2].end()
    rings[3].end()
    multiply(2, 1)
    inverse_m = lax.rsqrt(squares[...] * (1.0 / 4096) + EPSILON)

    def close(i, carry):
        proj_mem[i] = (acc[i] * inverse_m).astype(BF16)
        return carry

    lax.fori_loop(0, 3, close, 0)
    spread.finish()
    for copy in stored:
        copy.wait()
    keep_values.wait()
    keep_folded.wait()
    mover.finish_sends()

    sent_part(3)


def fetch(*args):
    return pl.pallas_call(
        fetch_kernel,
        out_shape=(
            jax.ShapeDtypeStruct((512, 4096), BF16),
            jax.ShapeDtypeStruct((48, 4096), BF16),
            jax.ShapeDtypeStruct((4, 1, 128), F32),
            jax.ShapeDtypeStruct((3, 4, 4, 2, 16, 2048), BF16),
            jax.ShapeDtypeStruct((3, 4, 4, 2, 16, 2048), BF16),
            jax.ShapeDtypeStruct((3, 512, 512), BF16),
            jax.ShapeDtypeStruct((3, 16, 512), BF16),
            jax.ShapeDtypeStruct((256, 4096), BF16),
            jax.ShapeDtypeStruct((4096, 512), BF16),
            jax.ShapeDtypeStruct((8, 32, 128), F32),
        ),
        in_specs=[VM] * 7 + [ANY, VM, ANY, ANY, ANY, ANY, VM, VM, VM],
        out_specs=(ANY, VM, VM, ANY, ANY, VM, VM, ANY, ANY, VM),
        scratch_shapes=[
            pltpu.VMEM((8, 128), jnp.int32), pltpu.VMEM((1, 128), F32),
            pltpu.VMEM((32, 8, 128), F32),
            pltpu.VMEM((32, 4, 1, 128), jnp.int32), pltpu.VMEM((128, 128), jnp.int32),
            pltpu.VMEM((128, 128), F32), pltpu.SMEM((32, 128), jnp.int32),
            pltpu.VMEM((4, 4, 2, 48, 1024), BF16), pltpu.VMEM((1004, 1024), BF16),
            pltpu.VMEM((4, 64, 16, 256), BF16), pltpu.VMEM((64, 16, 256), BF16),
            pltpu.VMEM((64, 16, 256), BF16), pltpu.VMEM((64, 16, 256), BF16),
            pltpu.VMEM((64, 16, 256), BF16),
            pltpu.VMEM((4, 512, 256), BF16), pltpu.VMEM((4, 4, 48, 1024), BF16),
            pltpu.VMEM((3, 4, 48, 512), BF16), pltpu.VMEM((3, 4, 48, 512), BF16),
            pltpu.VMEM((3, 48, 512), BF16), pltpu.VMEM((3, 48, 512), BF16),
            pltpu.VMEM((48, 1024), BF16),
            pltpu.VMEM((256, 4096), BF16),
            pltpu.VMEM((512, 4096), BF16), pltpu.VMEM((3, 4096, 512), BF16),
            pltpu.VMEM((3, 512, 512), F32), pltpu.VMEM((512, 1), F32),
            pltpu.VMEM((512, 512), BF16), pltpu.VMEM((4096, 512), BF16),
            pltpu.VMEM((4, 256, 2, 512), BF16), pltpu.VMEM((4096, 512), BF16),
            pltpu.VMEM((4096, 512), BF16),
            pltpu.SemaphoreType.DMA((112,)), pltpu.SemaphoreType.DMA((112,)),
            pltpu.SemaphoreType.DMA((4, 32)), pltpu.SemaphoreType.DMA((4, 32)),
            pltpu.SemaphoreType.DMA((32,)), pltpu.SemaphoreType.DMA((32,)),
            pltpu.SemaphoreType.DMA((8,)), pltpu.SemaphoreType.DMA((4,)),
            pltpu.SemaphoreType.DMA((8,)),
        ],
        compiler_params=params(2, 60),
    )(*args)


def reader_kernel(
    proj_mem, proj_q, bias, x_mem, tokens, qg_in, scores, left_in, right_in, live_out, w_val_in,
    cross_out_in,
    encoded_out, decoded,
    qg, encoded, ctx, others, x_seq, left, right, own_out, w_val, w_out, ql, ql_part, lv, lv_part, s, w, values,
    inv, parts, part_buf, send, recv, local_sem,
):
    at = Place()
    mover = Mover(send, recv)
    spread = Spread(at, mover, right, 2048)
    loads = [
        pltpu.make_async_copy(a, b, local_sem.at[i])
        for i, (a, b) in enumerate([
            (spread.line(right_in, "x"), spread.line(right, "x")),
            (spread.line(right_in, "y"), spread.line(right, "y")),
            (x_mem, x_seq.at[:, pl.ds(0, 16)]), (live_out, own_out), (w_val_in, w_val),
            (left_in, left), (cross_out_in, w_out), (qg_in, qg),
        ])
    ]
    for copy in loads:
        copy.start()
    greet_all(at)
    scale = HEAD ** (-0.5)
    nt = ((1,), (1,))
    def chunk(j):
        return pl.ds(pl.multiple_of(j * 256, 256), 256)

    def part(pos, u, k):
        return others.at[{1: 2, -1: 0, 2: 1}[k], chunk(turn(pos, u))]

    ring = Ring(
        mover, at.z, at.up, lambda u: ctx.at[chunk(turn(at.z, u))], part, [2, 1, 3, 0], False
    )

    low = lax.broadcasted_iota(jnp.int32, (128, 128), 1) < HEAD
    owner_lane = lax.broadcasted_iota(jnp.int32, (32, 256), 1) // 32 % 4

    def attend(j):
        def group(g, carry):
            first = j * 8 + g * 4

            def pair(i, p):
                lanes = pl.ds(128 * p, 128)
                pieces = []
                for n in range(4):
                    pieces.append(
                        proj_mem[i, pl.ds(pl.multiple_of((first + n) * 16, 16), 16), lanes]
                    )
                    pieces.append(proj_q[i, :, lanes])
                return jnp.concatenate(pieces, axis=0)

            for p in range(4):
                q, k, v = pair(0, p), pair(1, p), pair(2, p)
                none = jnp.zeros_like(q)
                both = jnp.concatenate([jnp.where(low, q, none), jnp.where(low, none, q)], axis=0)
                full = dot32(k, both, nt)
                sc = full[0:32]
                for n in range(1, 4):
                    sc = jnp.where(owner_lane == n, full[32 * n : 32 * n + 32], sc)
                sc = sc * scale + jnp.concatenate([bias[2 * p], bias[2 * p + 1]], axis=1)
                ex = jnp.exp(sc - jnp.max(sc, axis=0, keepdims=True))
                ex = ex * (1.0 / jnp.sum(ex, axis=0, keepdims=True))
                full = jnp.concatenate(
                    [jnp.where(owner_lane == n, ex, 0.0) for n in range(4)], axis=0
                ).astype(BF16)
                out = dot32(full, v, ((0,), (0,)))
                ctx[pl.ds(pl.multiple_of(first * 32, 128), 128), pl.ds(128 * p, 128)] = jnp.where(
                    low, out[0:128], out[128:256]
                ).astype(BF16)
            return carry

        lax.fori_loop(0, 2, group, 0)

    for u in (2, 3, 1, 0):
        attend(turn(at.z, u))
        ring.begin_right(u)
        ring.begin_left(u)
        if u == 2:
            loads[0].wait()
            loads[1].wait()
            spread.phase_two()

    loads[2].wait()
    loads[7].wait()

    def fill(p, carry):
        x_seq[p, pl.ds(16, 16)] = tokens[pl.ds(0, 16)]
        return carry

    lax.fori_loop(0, 32, fill, 0)

    def rows_of(j):
        return x_seq[pl.ds(j * 8, 8)].reshape(256, 4096)

    def score_inputs(j, carry):
        s[j] = dot32(qg[...], rows_of(j), nt)
        return carry

    lax.fori_loop(0, 4, score_inputs, 0)
    loads[4].wait()
    of_question = jnp.dot(tokens[pl.ds(0, 16)], w_val[...], preferred_element_type=F32)

    def value_inputs(j, carry):
        rows = jnp.dot(
            x_seq[pl.ds(j * 8, 8), pl.ds(0, 16)].reshape(128, 4096), w_val[...],
            preferred_element_type=F32,
        )
        for p in range(8):
            values[j, pl.ds(32 * p, 16)] = rows[16 * p : 16 * p + 16]
            values[j, pl.ds(32 * p + 16, 16)] = of_question
        return carry

    lax.fori_loop(0, 4, value_inputs, 0)
    spread.phase_two_onward()
    loads[3].wait()
    ql[0] = dot32(qg[...], own_out[...], nt).astype(BF16)
    lv[0] = jnp.dot(own_out[...], w_val[...], preferred_element_type=F32).astype(BF16)

    def absorb(j, k, rows):
        s[j] = s[j] + dot32(ql[k], rows, nt)
        values[j] = values[j] + jnp.dot(rows, lv[k], preferred_element_type=F32)

    def absorb_own(j, carry):
        absorb(j, 0, ctx[chunk(j)])
        return carry

    lax.fori_loop(0, 4, absorb_own, 0)
    loads[5].wait()
    half, rest = pl.ds(0, 2048), pl.ds(2048, 2048)

    def fold_left(k, carry):
        ql_part[k] = dot32(qg[:, half], left[k], nt)
        lv_part[k] = jnp.dot(left[k], w_val[half], preferred_element_type=F32)
        return carry

    lax.fori_loop(0, 3, fold_left, 0)
    ring.pass_right(2)
    ring.pass_left(3)
    ring.pass_right(1)
    spread.finish()

    def fold_right(k, carry):
        rows = right[k].reshape(512, 2048)
        ql[k + 1] = (ql_part[k] + dot32(qg[:, rest], rows, nt)).astype(BF16)
        lv[k + 1] = (
            lv_part[k] + jnp.dot(rows, w_val[rest], preferred_element_type=F32)
        ).astype(BF16)
        return carry

    lax.fori_loop(0, 3, fold_right, 0)

    ring.pass_left(0)

    ring.far[2].wait_recv()
    mine = chunk(at.z)

    def group_rows(k, n):
        if k == 0:
            return own_out[:, pl.ds(n * 1024, 1024)]
        if n < 2:
            return left[k - 1, :, pl.ds(n * 1024, 1024)]
        return right[k - 1, :, :, :, :, pl.ds((n - 2) * 1024, 1024)].reshape(512, 1024)

    squares = jnp.zeros((256, 1), F32)
    for n in range(4):
        cols = pl.ds(n * 1024, 1024)
        attended = None
        for k in range(4):
            rows = ctx[mine] if k == 0 else others[k - 1, mine]
            product = jnp.dot(rows, group_rows(k, n), preferred_element_type=F32)
            product = product.astype(BF16).astype(F32)
            attended = product if k == 0 else attended + product
        own_rows = x_seq[pl.ds(at.z * 8, 8), :, cols].reshape(256, 1024).astype(F32)
        own_rows = (own_rows + attended).astype(BF16)
        encoded[:, cols] = own_rows
        own_rows = own_rows.astype(F32)
        squares = squares + jnp.sum(own_rows * own_rows, axis=1, keepdims=True)
    keep = pltpu.make_async_copy(encoded, encoded_out, local_sem.at[8])
    keep.start()
    norm = lax.rsqrt(squares * (1.0 / 4096) + EPSILON)
    inv[at.z] = jnp.transpose(jnp.broadcast_to(norm, (256, 128)))[0:1]
    near = [mover.go(inv.at[at.z], inv.at[at.z], at.up(turn(at.z, k))) for k in range(1, 4)]

    def absorb_other(k, u):
        j = turn(at.z, k + u)
        absorb(j, k, others[k - 1, chunk(j)])

    absorb_other(3, 2)
    absorb_other(1, 3)
    absorb_other(3, 1)
    absorb_other(2, 2)
    ring.to_left[2].wait_recv()
    absorb_other(1, 2)
    ring.to_right[3].wait_recv()
    absorb_other(3, 3)
    ring.to_left[1].wait_recv()
    absorb_other(1, 1)
    absorb_other(1, 0)
    ring.far[3].wait_recv()
    absorb_other(2, 3)
    ring.to_right[0].wait_recv()
    absorb_other(3, 0)
    ring.far[1].wait_recv()
    absorb_other(2, 1)
    ring.far[0].wait_recv()
    absorb_other(2, 0)
    for copy in near:
        copy.wait_recv()

    passage = lax.broadcasted_iota(jnp.int32, (1, 256), 1) // 32
    top = None
    for j in range(4):
        row = jnp.zeros((1, 256), F32)
        line = scores[j]
        for p in range(8):
            row = row + jnp.where(passage == p, line[:, p : p + 1], 0.0)
        total = s[j] * (inv[j] * scale) + row
        s[j] = total
        here = jnp.max(total, axis=1, keepdims=True)
        top = here if top is None else jnp.maximum(top, here)
    sums = jnp.zeros((256, 1), F32)
    for j in range(4):
        ex = jnp.exp(s[j] - top)
        s[j] = ex
        sums = sums + jnp.sum(ex, axis=1, keepdims=True)
    for j in range(4):
        w[j] = (s[j] * inv[j] / sums).astype(BF16)
    heads_out = jnp.zeros((256, 512), F32)
    for j in range(4):
        heads_out = heads_out + jnp.dot(
            w[j], values[j].astype(BF16), preferred_element_type=F32
        )
    head = lax.broadcasted_iota(jnp.int32, (32, 512), 1) // HEAD
    context = jnp.zeros((32, 512), F32)
    for h in range(8):
        context = context + jnp.where(head == h, heads_out[32 * h : 32 * h + 32], 0.0)
    context = context.astype(BF16)
    loads[6].wait()
    for j in range(4):
        parts[j] = jnp.dot(
            context, w_out[:, pl.ds(1024 * j, 1024)], preferred_element_type=F32
        ).astype(BF16)
    last = [
        mover.go(parts.at[turn(at.z, k)], part_buf.at[k - 1], at.up(turn(at.z, k)))
        for k in range(1, 4)
    ]
    for copy in last:
        copy.wait_recv()
    total = parts[at.z].astype(F32)
    for k in range(3):
        total = total + part_buf[k].astype(F32)
    decoded[...] = total.astype(BF16)
    keep.wait()
    mover.finish_sends()


def reader(*args):
    return pl.pallas_call(
        reader_kernel,
        out_shape=(
            jax.ShapeDtypeStruct((256, 4096), BF16),
            jax.ShapeDtypeStruct((32, 1024), BF16),
        ),
        in_specs=[VM, VM, VM, ANY, VM, ANY, VM, ANY, ANY, ANY, ANY, ANY],
        out_specs=(ANY, VM),
        scratch_shapes=[
            pltpu.VMEM((256, 4096), BF16), pltpu.VMEM((256, 4096), BF16),
            pltpu.VMEM((1024, 512), BF16), pltpu.VMEM((3, 1024, 512), BF16),
            pltpu.VMEM((32, 32, 4096), BF16), pltpu.VMEM((3, 512, 2048), BF16),
            pltpu.VMEM((3, 4, 4, 2, 16, 2048), BF16), pltpu.VMEM((512, 4096), BF16),
            pltpu.VMEM((4096, 512), BF16), pltpu.VMEM((512, 4096), BF16),
            pltpu.VMEM((4, 256, 512), BF16), pltpu.VMEM((3, 256, 512), F32),
            pltpu.VMEM((4, 512, 512), BF16), pltpu.VMEM((3, 512, 512), F32),
            pltpu.VMEM((4, 256, 256), F32), pltpu.VMEM((4, 256, 256), BF16),
            pltpu.VMEM((4, 256, 512), F32), pltpu.VMEM((4, 1, 256), F32),
            pltpu.VMEM((4, 32, 1024), BF16), pltpu.VMEM((3, 32, 1024), BF16),
            pltpu.SemaphoreType.DMA((64,)), pltpu.SemaphoreType.DMA((64,)),
            pltpu.SemaphoreType.DMA((9,)),
        ],
        compiler_params=params(3, 60),
    )(*args)


def shards(
    question_ids, answer_ids, owner, slot, passage_score, memory, embedding, live_gain, live_qkv,
    rel_bias, live_out, enc_gain, cross_kv, dec_gain, cross_query, cross_out,
):
    n_psg = lax.axis_size("psg")
    width = live_gain.shape[0]
    plen = memory.shape[1]
    qlen = question_ids.shape[1]
    own_count = owner.shape[1]
    total = own_count * n_psg
    seq = plen + qlen
    cols = live_out.shape[0]

    spread_of = jnp.asarray(spread_table(seq, rel_bias.shape[1]))
    x_mem, token_full, scores, left, right, proj_mem, proj_q, qg, w_val, bias = fetch(
        question_ids, answer_ids, owner.reshape(1, own_count), slot, rel_bias, spread_of, memory,
        embedding, passage_score, live_out,
        jnp.transpose(live_qkv, (1, 0, 2)), cross_kv, cross_query,
        live_gain.reshape(1, width), enc_gain.reshape(1, width), dec_gain.reshape(1, width),
    )
    encoded, decoded = reader(
        proj_mem, proj_q, bias, x_mem.reshape(total, plen, width), token_full, qg, scores,
        left.reshape(3, cols, width // 2), right, live_out, w_val, cross_out,
    )
    return encoded.reshape(1, own_count, seq, width), decoded[None]


def solution(mesh):
    return jax.shard_map(
        shards,
        mesh=mesh,
        in_specs=(
            P("cache", None), P("cache", None), P("cache", "psg", None), P("cache", "psg"),
            P("cache", "psg"), P("cache", None, "psg"), P("cache", "psg"), P(),
            P(None, None, "psg"), P("psg", None), P("psg", None), P(), P(None, None, "psg"), P(),
            P(None, "psg"), P("psg", None),
        ),
        out_specs=(P("cache", "psg", None, None), P("cache", None, "psg")),
        check_vma=False,
    )
```
